256 devices in a mesh: seq: 64 (over z, y, core), tp: 4 (over x).
Axes of the slice: x: 4, y: 4, z: 8, core: 2. Of those that a mesh axis runs over, the one named last changes fastest.
Arguments:
- frames: bfloat16 [192, 128, 1152], P('seq', None, 'tp'), may hold values from -6 to 6
- frame_counts: int32 [64], replicated, may hold values from 1 to 3, 128 in all
- weights: bfloat16 [2, 4, 1152, 1152], P(None, None, None, 'tp'), may hold values from -0.1875 to 0.1875
- grad_out: bfloat16 [128, 128, 1152], P(None, 'seq', 'tp'), may hold values from -6 to 6
Outputs:
- frame_grads: bfloat16 [192, 128, 1152], P('seq', None, 'tp')
- weight_grads: float32 [1152, 2, 4, 1152], P('seq', None, None, 'tp')
The draws below stay inside these ranges and needn't reach their ends.
Inputs may be any that keep to these rules, and one draw needn't show every extreme that they name: Index s of seq holds frame_counts[s] frames in its first slots: the global frames after those of lower indices, in order. Its other slots reach no output. The counts sum to 128, and some index holds 3.
All inputs are finite; a program needn't handle non-finite values.
Results may differ from the reference program's by a relative error of at most 0.03.
Values may be sent and summed in bfloat16 or wider, within the bound.
No kernel may reach another device: no remote copies, remote signals or barrier semaphores. Data moves between devices by JAX's collectives and lax.ppermute only.
A program may use at most 128 MiB of HBM per device.

```python
import math
import jax
import jax.numpy as jnp
import numpy as np
from jax import lax

HD = 72
D = 1152
P_SIZE = 128
TF = 16
SLOTS = 3
F_ALL = 128
VIDEOS = 8
CAP = 192
N_SEQ = 64


def block_scale(own_key, dims, split, least, largest):
    def one(axis_at, parts):
        draws = jax.random.uniform(jax.random.fold_in(jax.random.fold_in(own_key, 6), axis_at), (parts,), jnp.float32, least / len(split), largest / len(split))
        return jnp.repeat(jnp.exp(draws), dims[axis_at] // parts).reshape((-1,) + (1,) * (len(dims) - axis_at - 1))

    loudness = one(*split[0])
    for cut in split[1:]:
        loudness = loudness * one(*cut)
    return loudness


def profile(amount, total, bound, skew):
    loads = [(1 << 20) // math.isqrt(rank ** skew) + 1 for rank in range(2, amount + 1)]
    spare, given = total - bound - (amount - 1), [1] * (amount - 1)
    while spare > 0:
        movable = [i for i in range(amount - 1) if given[i] < bound]
        mass, left = sum([loads[i] for i in movable]), spare
        for i in movable:
            addition = min(bound - given[i], max(1, left * loads[i] // mass), spare)
            given[i] = given[i] + addition
            spare = spare - addition
    return np.array([bound] + given)


def ragged_sizes(stream_key, number_of, total, limit, skew):
    if number_of == 2:
        one = jax.random.randint(stream_key, (), max(1, total - limit), min(limit, total - 1) + 1)
        return jnp.stack([one, total - one])
    lengths = jnp.asarray(profile(number_of, total, limit, skew), jnp.int32)
    couples = (number_of - 1) // 2
    giver, taker = lengths[1:1 + 2 * couples:2], lengths[2:2 + 2 * couples:2]
    room = jnp.minimum(giver - 1, limit - taker)
    shifted = jax.random.randint(jax.random.fold_in(stream_key, 1), (couples,), 0, 1 << 20) % (room + 1)
    lengths = lengths.at[1:1 + 2 * couples:2].set(giver - shifted).at[2:2 + 2 * couples:2].set(taker + shifted)
    return lengths[jax.random.permutation(jax.random.fold_in(stream_key, 2), number_of)]


def normal_values(own_key, dims, width, limit, split=(), held_as=jnp.bfloat16):
    drawn = width * jax.random.normal(own_key, dims, jnp.float32)
    if split:
        drawn = drawn * block_scale(own_key, dims, split, -0.22, 0.18)
    return jnp.clip(drawn, -limit, limit).astype(held_as)


def setup_inputs(seed: int = 0) -> dict:
    streams_of = jax.random.split(jax.random.key(seed), 5)
    return {
        "frames": normal_values(streams_of[0], (CAP, P_SIZE, D), 1.0, 6.0, ((0, 64), (2, 4))),
        "frame_counts": ragged_sizes(streams_of[1], N_SEQ, F_ALL, SLOTS, 2).astype(jnp.int32),
        "weights": normal_values(streams_of[2], (2, 4, D, D), D ** -0.5, 0.1875, ((3, 4),)),
        "grad_out": normal_values(streams_of[3], (F_ALL, P_SIZE, D), 1.0, 6.0, ((1, 64), (2, 4))),
    }


epsilon = 1e-06

def to_half(values):
    return lax.optimization_barrier(values.astype(jnp.bfloat16))

def layer_norm(values):
    center = values - lax.optimization_barrier(jnp.mean(values, axis=-1, keepdims=True))
    inverse = lax.rsqrt(lax.optimization_barrier(jnp.mean(center * center, axis=-1, keepdims=True)) + epsilon)
    return center * inverse

def layer_norm_back(values, upstream):
    center = values - lax.optimization_barrier(jnp.mean(values, axis=-1, keepdims=True))
    inverse = lax.rsqrt(lax.optimization_barrier(jnp.mean(center * center, axis=-1, keepdims=True)) + epsilon)
    normed = center * inverse
    return inverse * (upstream - lax.optimization_barrier(jnp.mean(upstream, axis=-1, keepdims=True)) - normed * lax.optimization_barrier(jnp.mean(upstream * normed, axis=-1, keepdims=True)))

def head_norm(values):
    headed = values.reshape(values.shape[:-1] + (values.shape[-1] // HD, HD))
    inverse = lax.rsqrt(lax.optimization_barrier(jnp.mean(headed * headed, axis=-1, keepdims=True)) + epsilon)
    return headed * inverse

def head_norm_back(values, upstream):
    headed = values.reshape(values.shape[:-1] + (values.shape[-1] // HD, HD))
    inverse = lax.rsqrt(lax.optimization_barrier(jnp.mean(headed * headed, axis=-1, keepdims=True)) + epsilon)
    result = inverse * upstream - headed * inverse ** 3 * lax.optimization_barrier(jnp.mean(upstream * headed, axis=-1, keepdims=True))
    return result.reshape(values.shape)

def attend_core(query_rows, key_rows, value_rows):
    query_unit = to_half(head_norm(query_rows))
    key_unit = to_half(head_norm(key_rows))
    value_heads = to_half(value_rows).reshape(query_unit.shape)
    scores = jnp.einsum('blhe,bmhe->bhlm', query_unit.astype(jnp.float32), key_unit.astype(jnp.float32)) * HD ** (-0.5)
    raised = jnp.exp(scores)
    probabilities = raised / lax.optimization_barrier(jnp.sum(raised, axis=-1, keepdims=True))
    return (query_unit, key_unit, value_heads, probabilities)

def attend_mix(query_rows, key_rows, value_rows):
    query_unit, key_unit, value_heads, probabilities = attend_core(query_rows, key_rows, value_rows)
    mixture = jnp.einsum('bhlm,bmhe->blhe', to_half(probabilities).astype(jnp.float32), value_heads.astype(jnp.float32))
    return (to_half(mixture.reshape(query_rows.shape)),)

def attend_back(query_rows, key_rows, value_rows, grad_mixture):
    query_unit, key_unit, value_heads, probabilities = attend_core(query_rows, key_rows, value_rows)
    grad_heads = grad_mixture.reshape(value_heads.shape).astype(jnp.float32)
    grad_probs = jnp.einsum('blhe,bmhe->bhlm', grad_heads, value_heads.astype(jnp.float32))
    grad_value = jnp.einsum('bhlm,blhe->bmhe', to_half(probabilities).astype(jnp.float32), grad_heads)
    grad_scores = to_half(probabilities * (grad_probs - lax.optimization_barrier(jnp.sum(grad_probs * probabilities, axis=-1, keepdims=True)))).astype(jnp.float32)
    query_slope = jnp.einsum('bhlm,bmhe->blhe', grad_scores, key_unit.astype(jnp.float32)) * HD ** (-0.5)
    key_slope = jnp.einsum('bhlm,blhe->bmhe', grad_scores, query_unit.astype(jnp.float32)) * HD ** (-0.5)
    grad_query = to_half(head_norm_back(query_rows, query_slope))
    grad_key = to_half(head_norm_back(key_rows, key_slope))
    return (grad_query, grad_key, to_half(grad_value.reshape(query_rows.shape)))

def over_blocks(function, arrays, size):
    leading = arrays[0].shape[0]
    shaped = tuple((member.reshape((leading // size, size) + member.shape[1:]) for member in arrays))
    results = lax.map(lambda group_rows: function(*group_rows), shaped)
    return tuple((member.reshape((leading,) + member.shape[2:]) for member in results))

def block_inner(inputs, matrices, size):
    normed = to_half(layer_norm(inputs.astype(jnp.float32)))
    wide = normed.astype(jnp.float32)
    query_rows = jnp.einsum('bld,de->ble', wide, matrices[0].astype(jnp.float32))
    key_rows = jnp.einsum('bld,de->ble', wide, matrices[1].astype(jnp.float32))
    value_rows = jnp.einsum('bld,de->ble', wide, matrices[2].astype(jnp.float32))
    mixture = over_blocks(attend_mix, (query_rows, key_rows, value_rows), size)[0]
    return (normed, query_rows, key_rows, value_rows, mixture)

def block_out(mixture, matrices):
    return jnp.einsum('ble,de->bld', mixture.astype(jnp.float32), matrices[3].astype(jnp.float32))

def block_back(inputs, matrices, cached, upstream, size):
    normed, query_rows, key_rows, value_rows, mixture = cached
    upward = upstream.astype(jnp.float32)
    grad_mixture = to_half(jnp.einsum('bld,de->ble', upward, matrices[3].astype(jnp.float32)))
    grad_query, grad_key, grad_value = over_blocks(attend_back, (query_rows, key_rows, value_rows, grad_mixture), size)
    grad_normed = jnp.einsum('ble,de->bld', grad_query.astype(jnp.float32), matrices[0].astype(jnp.float32))
    grad_normed = grad_normed + jnp.einsum('ble,de->bld', grad_key.astype(jnp.float32), matrices[1].astype(jnp.float32))
    grad_normed = grad_normed + jnp.einsum('ble,de->bld', grad_value.astype(jnp.float32), matrices[2].astype(jnp.float32))
    grad_input = layer_norm_back(inputs.astype(jnp.float32), grad_normed)
    wide = normed.astype(jnp.float32)
    gradients = jnp.stack([jnp.einsum('bld,ble->de', wide, grad_query.astype(jnp.float32)), jnp.einsum('bld,ble->de', wide, grad_key.astype(jnp.float32)), jnp.einsum('bld,ble->de', wide, grad_value.astype(jnp.float32)), jnp.einsum('bld,ble->de', upward, mixture.astype(jnp.float32))])
    return (grad_input, gradients)

def to_sequences(values):
    shaped = values.reshape(VIDEOS, TF, P_SIZE, values.shape[-1])
    return jnp.transpose(shaped, (0, 2, 1, 3)).reshape(VIDEOS * P_SIZE, TF, values.shape[-1])

def from_sequences(values):
    shaped = values.reshape(VIDEOS, P_SIZE, TF, values.shape[-1])
    return jnp.transpose(shaped, (0, 2, 1, 3)).reshape(F_ALL, P_SIZE, values.shape[-1])

def reference(frames, frame_counts, weights, grad_out):
    frame_ids = jnp.arange(F_ALL, dtype=jnp.int32)
    count_ends = jnp.cumsum(frame_counts).astype(jnp.int32)
    before = count_ends[None, :] <= frame_ids[:, None]
    holder = lax.optimization_barrier(jnp.sum(before.astype(jnp.int32), axis=1)).astype(jnp.int32)
    holder_start = lax.optimization_barrier(jnp.sum(jnp.where(before, frame_counts[None, :], 0), axis=1)).astype(jnp.int32)
    slot_index = (holder * SLOTS + frame_ids - holder_start).astype(jnp.int32)
    inputs = frames[slot_index]
    spatial_cache = block_inner(inputs, weights[0], 8)
    hidden = to_half(inputs.astype(jnp.float32) + block_out(spatial_cache[4], weights[0]))
    temporal_in = to_sequences(hidden)
    temporal_cache = block_inner(temporal_in, weights[1], P_SIZE)
    grad_temporal, grads_temporal = block_back(temporal_in, weights[1], temporal_cache, to_sequences(grad_out), P_SIZE)
    grad_hidden = to_half(grad_out.astype(jnp.float32) + from_sequences(grad_temporal))
    grad_spatial, grads_spatial = block_back(inputs, weights[0], spatial_cache, grad_hidden, 8)
    grad_inputs = (grad_hidden.astype(jnp.float32) + grad_spatial).astype(jnp.bfloat16)
    frame_grads = jnp.zeros(frames.shape, jnp.bfloat16).at[slot_index].set(grad_inputs)
    grad_scale = 1.0 / math.sqrt(F_ALL * P_SIZE)
    weight_grads = jnp.transpose(jnp.stack([grads_spatial, grads_temporal]), (2, 0, 1, 3)) * grad_scale
    return (frame_grads, weight_grads.astype(jnp.float32))
```

```python
import functools
import math

import jax
import jax.numpy as jnp
from jax import lax
from jax.experimental import pallas as pl
from jax.experimental.pallas import tpu as pltpu
from jax.sharding import Mesh
from jax.sharding import PartitionSpec as P

HD = 72
TF = 16
HEADS = 4
OWN = HEADS * HD
TP = 4
D = OWN * TP
PAGE = 128
SLOTS = 3
NZ, NY, NC = 8, 4, 2
CHIPS = NZ * NY
ROWS = 36
PAD = 40
HALF = 640
EPS = 1e-06
SCALE = HD**-0.5
F32 = jnp.float32
BF = jnp.bfloat16


def nn(a, b):
    return lax.dot_general(a, b, (((1,), (0,)), ((), ())), preferred_element_type=F32)


def nt(a, b):
    return lax.dot_general(a, b, (((1,), (1,)), ((), ())), preferred_element_type=F32)


def tn(a, b):
    return lax.dot_general(a, b, (((0,), (0,)), ((), ())), preferred_element_type=F32)


def iota(shape, dim):
    return lax.broadcasted_iota(jnp.int32, shape, dim)


def eye(n):
    return (iota((n, n), 0) == iota((n, n), 1)).astype(BF)


def call(body, ins, outs, scratch=(), smem=1, flops=1_000_000, specs=None, limit=40):
    in_specs = [
        pl.BlockSpec(memory_space=pltpu.SMEM) if i < smem else pl.BlockSpec(memory_space=pltpu.VMEM)
        for i in range(len(ins))
    ]
    for at, spec in (specs or {}).items():
        in_specs[at] = spec
    grid = {"grid": (1,)} if specs else {}
    size = sum(math.prod(o.shape) * o.dtype.itemsize for o in outs)
    size += sum(math.prod(i.shape) * i.dtype.itemsize for i in ins)
    if specs:
        out_specs = [pl.BlockSpec(o.shape, functools.partial(lambda n, i: (0,) * n, len(o.shape))) for o in outs]
        for i in range(len(ins)):
            if i >= smem and i not in specs:
                n = len(ins[i].shape)
                in_specs[i] = pl.BlockSpec(ins[i].shape, functools.partial(lambda n, i: (0,) * n, n))
    else:
        out_specs = [pl.BlockSpec(memory_space=pltpu.VMEM) for _ in outs]
    return pl.pallas_call(
        body,
        out_shape=list(outs),
        in_specs=in_specs,
        out_specs=out_specs,
        scratch_shapes=list(scratch),
        compiler_params=pltpu.CompilerParams(vmem_limit_bytes=limit * 2**20),
        cost_estimate=pl.CostEstimate(flops=flops, bytes_accessed=size, transcendentals=0),
        **grid,
    )(*ins)


def half(*shape):
    return jax.ShapeDtypeStruct(shape, BF)


def full(*shape):
    return jax.ShapeDtypeStruct(shape, F32)


def normalise(x):
    center = x - jnp.sum(x, axis=0, keepdims=True) * (1.0 / D)
    inverse = lax.rsqrt(jnp.sum(center * center, axis=0, keepdims=True) * (1.0 / D) + EPS)
    return center * inverse, inverse


def normalise_back(normed, inverse, up):
    mean = jnp.sum(up, axis=0, keepdims=True) * (1.0 / D)
    along = jnp.sum(up * normed, axis=0, keepdims=True) * (1.0 / D)
    return inverse * (up - mean - normed * along)


def unit(rows):
    inverse = lax.rsqrt(jnp.sum(rows * rows, axis=0, keepdims=True) * (1.0 / HD) + EPS)
    return inverse, (rows * inverse).astype(BF)


def unit_back(rows, inverse, up):
    along = jnp.sum(up * rows, axis=0, keepdims=True) * (1.0 / HD)
    return inverse * up - rows * (inverse * inverse * inverse * along)


def head_parts(qkv, h):
    q = qkv[h * HD : (h + 1) * HD]
    k = qkv[OWN + h * HD : OWN + (h + 1) * HD]
    v = qkv[2 * OWN + h * HD : 2 * OWN + (h + 1) * HD]
    q_inv, q_unit = unit(q)
    k_inv, k_unit = unit(k)
    return q, k, q_inv, q_unit, k_inv, k_unit, v.astype(BF)


def weights_of(k_unit, q_unit, mask):
    raised = jnp.exp(tn(k_unit, q_unit) * SCALE)
    if mask is not None:
        raised = jnp.where(mask, raised, 0.0)
    return raised * (1.0 / jnp.sum(raised, axis=0, keepdims=True))


def mixture_of(qkv, tokens, mask):
    heads = []
    for h in range(HEADS):
        _, _, _, q_unit, _, k_unit, v = head_parts(qkv, h)
        blocks = []
        for b in range(tokens // PAGE):
            at = slice(b * PAGE, (b + 1) * PAGE)
            probs = weights_of(k_unit[:, at], q_unit[:, at], mask)
            blocks.append(nn(v[:, at], probs.astype(BF)))
        heads.append(jnp.concatenate(blocks, axis=1))
    return jnp.concatenate(heads, axis=0).astype(BF)


def attend_back(qkv, grad_mix, tokens, mask, with_mixture):
    queries, keys, values, mixes = [], [], [], []
    for h in range(HEADS):
        q, k, q_inv, q_unit, k_inv, k_unit, v = head_parts(qkv, h)
        gm = grad_mix[h * HD : (h + 1) * HD].astype(BF)
        q_slope, k_slope, v_grad, mix = [], [], [], []
        for b in range(tokens // PAGE):
            at = slice(b * PAGE, (b + 1) * PAGE)
            probs = weights_of(k_unit[:, at], q_unit[:, at], mask)
            probs_half = probs.astype(BF)
            if with_mixture:
                mix.append(nn(v[:, at], probs_half))
            grad_probs = tn(v[:, at], gm[:, at])
            v_grad.append(nt(gm[:, at], probs_half))
            weighted = probs * grad_probs
            grad_scores = (weighted - probs * jnp.sum(weighted, axis=0, keepdims=True)).astype(BF)
            q_slope.append(nn(k_unit[:, at], grad_scores) * SCALE)
            k_slope.append(nt(q_unit[:, at], grad_scores) * SCALE)
        queries.append(unit_back(q, q_inv, jnp.concatenate(q_slope, axis=1)))
        keys.append(unit_back(k, k_inv, jnp.concatenate(k_slope, axis=1)))
        values.append(jnp.concatenate(v_grad, axis=1))
        if with_mixture:
            mixes.append(jnp.concatenate(mix, axis=1))
    join = lambda parts: jnp.concatenate(parts, axis=0).astype(BF)
    return join(queries), join(keys), join(values), join(mixes) if with_mixture else None


def assemble(own, chunks, held):
    for k, chunk in enumerate(chunks):
        held[(own + TP - k) % TP] = chunk[...]
    return held[...].reshape(D, held.shape[2])


def deal(own, value, held, outs):
    held[...] = value.astype(BF).reshape(held.shape)
    for k, out in enumerate(outs):
        out[...] = held[(own + k) % TP]


def turn_kernel(x_ref, out_ref):
    same = eye(OWN)
    for n in range(x_ref.shape[0]):
        out_ref[:, n * PAGE : (n + 1) * PAGE] = nt(same, x_ref[n]).astype(BF)


def prepare_kernel(w_ref, out_ref):
    out_ref[0, 0] = nt(eye(OWN), w_ref[0, 0]).astype(BF)


def spatial_kernel(me, c0, c1, c2, c3, wt_ref, w_ref, p0, p1, p2, p3, x_out, qkv_out, mix_out, held, dealt):
    x = assemble(me[0], (c0, c1, c2, c3), held)
    x_out[...] = x
    normed, _ = normalise(x.astype(F32))
    qkv = nn(wt_ref[0, :3].reshape(3 * OWN, D), normed.astype(BF))
    qkv_out[...] = qkv
    mix = mixture_of(qkv, x.shape[1], None)
    mix_out[...] = mix
    deal(me[0], nn(w_ref[0, 0], mix), dealt, (p0, p1, p2, p3))


def temporal_kernel(
    me, h0, h1, h2, h3, g0, g1, g2, g3, wt_ref, w_ref,
    p0, p1, p2, p3, normed_out, up_out, grads_out, held, held_g, dealt,
):
    x = assemble(me[0], (h0, h1, h2, h3), held)
    up = assemble(me[0], (g0, g1, g2, g3), held_g)
    up_out[...] = up
    normed, inverse = normalise(x.astype(F32))
    normed_half = normed.astype(BF)
    normed_out[...] = normed_half
    qkv = nn(wt_ref[0, :3].reshape(3 * OWN, D), normed_half)
    grad_mix = nn(wt_ref[0, 3], up)
    mask = (iota((PAGE, PAGE), 0) // TF) == (iota((PAGE, PAGE), 1) // TF)
    gq, gk, gv, mix = attend_back(qkv, grad_mix, x.shape[1], mask, True)
    for m, part in enumerate((gq, gk, gv, mix)):
        grads_out[m * OWN : (m + 1) * OWN] = part
    grad_normed = nn(w_ref[0, 0], gq) + nn(w_ref[0, 1], gk) + nn(w_ref[0, 2], gv)
    deal(me[0], normalise_back(normed, inverse, grad_normed), dealt, (p0, p1, p2, p3))


def spatial_back_kernel(
    me, g0, g1, g2, g3, x_ref, qkv_ref, mix_ref, wt_ref, w_ref,
    p0, p1, p2, p3, normed_out, up_out, grads_out, held_g, dealt,
):
    up = assemble(me[0], (g0, g1, g2, g3), held_g)
    up_out[...] = up
    normed, inverse = normalise(x_ref[...].astype(F32))
    normed_out[...] = normed.astype(BF)
    grad_mix = nn(wt_ref[0, 0], up)
    gq, gk, gv, _ = attend_back(qkv_ref[...], grad_mix, up.shape[1], None, False)
    for m, part in enumerate((gq, gk, gv, mix_ref[...])):
        grads_out[m * OWN : (m + 1) * OWN] = part
    grad_normed = nn(w_ref[0, 0], gq) + nn(w_ref[0, 1], gk) + nn(w_ref[0, 2], gv)
    deal(me[0], normalise_back(normed, inverse, grad_normed), dealt, (p0, p1, p2, p3))


def regroup(ref, held):
    for y in range(NY):
        for z in range(NZ):
            at = (y * NZ + z) * PAD
            held[at + PAD - 8 : at + PAD] = jnp.zeros((8, held.shape[1]), F32)
            held[at : at + ROWS] = ref[z * NY * ROWS + y * ROWS : z * NY * ROWS + (y + 1) * ROWS]
    return held[...].astype(BF)


def weight_kernel(me, normed_ref, up_ref, grads_ref, keep, send, wide, held):
    tokens = normed_ref.shape[1]
    zeros = lambda n: jnp.zeros((n, tokens), BF)
    wide[...] = normed_ref[...].astype(F32)
    lines = regroup(wide, held)
    wide[...] = up_ref[...].astype(F32)
    up_lines = regroup(wide, held)
    first = nt(lines, jnp.concatenate([grads_ref[: 2 * OWN], zeros(HALF - 2 * OWN)], axis=0)).astype(BF)
    values, mix = grads_ref[2 * OWN : 3 * OWN], grads_ref[3 * OWN :]
    low = nt(lines, jnp.concatenate([values, zeros(96)], axis=0))
    low = low + nt(up_lines, jnp.concatenate([zeros(OWN), mix[:96]], axis=0))
    high = nt(up_lines, jnp.concatenate([mix[96:], zeros(64)], axis=0))
    core = me[3]

    @pl.when(core == 0)
    def _():
        keep[...] = first
        send[:, :384] = low.astype(BF)
        send[:, 384:] = high.astype(BF)

    @pl.when(core == 1)
    def _():
        send[...] = first
        keep[:, :384] = low.astype(BF)
        keep[:, 384:] = high.astype(BF)


def pair_kernel(me, keep, got, o0, o1, o2, o3):
    span = NZ * PAD
    for k, out in enumerate((o0, o1, o2, o3)):
        rows = pl.ds(pl.multiple_of(((me[1] + k) % NY) * span, 16), span)
        out[...] = (keep[rows].astype(F32) + got[rows].astype(F32)).astype(BF)


def column_kernel(me, a, b, c, d, *rest):
    outs, held = rest[:NZ], rest[NZ]
    total = a[...].astype(F32) + b[...].astype(F32) + c[...].astype(F32) + d[...].astype(F32)
    held[...] = total.reshape(NZ, PAD, HALF)
    for k, out in enumerate(outs):
        out[...] = held[(me[2] + k) % NZ].astype(BF)


def last_kernel(scale, me, *rest):
    parts, (keep, send) = rest[:NZ], rest[NZ:]
    total = parts[0][...].astype(F32)
    for part in parts[1:]:
        total = total + part[...].astype(F32)
    total = total * scale
    upper, lower = total[: ROWS // 2], total[ROWS // 2 : ROWS]
    first = me[3] == 0
    keep[...] = jnp.where(first, upper, lower)
    send[...] = jnp.where(first, lower, upper)


def spread_kernel(me, a, b, c, d, own, keep, send):
    total = a[...].astype(F32) + b[...].astype(F32) + c[...].astype(F32) + d[...].astype(F32)
    hidden = (own[...].astype(F32) + total).astype(BF)
    rows, tokens = CHIPS * 8, SLOTS * PAGE
    row, col = iota((rows, tokens), 0), iota((rows, tokens), 1)
    part, chip = row % 8, row // 8
    base = (part // 2) * PAGE + 4 * chip + part % 2
    for out, core in ((keep, me[3]), (send, 1 - me[3])):
        pick = jnp.logical_and(part < 6, col == base + 2 * core)
        out[...] = nt(pick.astype(BF), hidden).astype(BF)


def pick_kernel(me, arrived, index_ref, out_ref):
    rows, tokens = CHIPS * 16, 2 * PAGE
    row, col = iota((rows, tokens), 0), iota((rows, tokens), 1)
    part, chip, rel = row % 8, row // 16, (row // 8) % 2
    core = jnp.where(rel == 0, me[3], 1 - me[3])
    slot = (2 * chip + core) * SLOTS + part // 2
    pick = jnp.logical_and(part < 6, part % 2 == col // PAGE)
    pick = jnp.logical_and(pick, slot == index_ref[0:1])
    out_ref[...] = tn(arrived[...], pick.astype(BF)).astype(BF)


def scatter_kernel(me, a, b, c, d, own, index_ref, keep, send):
    total = a[...].astype(F32) + b[...].astype(F32) + c[...].astype(F32) + d[...].astype(F32)
    grad = (own[...].astype(F32) + total).astype(BF)
    rows, tokens = CHIPS * 8, 2 * PAGE
    row, col = iota((rows, tokens), 0), iota((rows, tokens), 1)
    part, chip = row % 8, row // 8
    live = jnp.logical_and(part < 6, part % 2 == col // PAGE)
    for out, core in ((keep, me[3]), (send, 1 - me[3])):
        slot = (2 * chip + core) * SLOTS + part // 2
        pick = jnp.logical_and(live, slot == index_ref[0:1])
        out[...] = nt(pick.astype(BF), grad).astype(BF)


def collect_kernel(me, arrived, out_ref):
    rows, tokens = CHIPS * 16, SLOTS * PAGE
    row, col = iota((rows, tokens), 0), iota((rows, tokens), 1)
    part, chip, rel = row % 8, row // 16, (row // 8) % 2
    core = jnp.where(rel == 0, me[3], 1 - me[3])
    position = 4 * chip + 2 * core + part % 2
    pick = jnp.logical_and(part < 6, col == (part // 2) * PAGE + position)
    out_ref[...] = tn(arrived[...], pick.astype(BF)).astype(BF)


def finish_kernel(a, b, c, d, own, out_ref):
    total = a[...].astype(F32) + b[...].astype(F32) + c[...].astype(F32) + d[...].astype(F32)
    grad = (own[...].astype(F32) + total).astype(BF)
    for n in range(SLOTS):
        out_ref[n] = nt(eye(PAGE), grad[:, n * PAGE : (n + 1) * PAGE]).astype(BF)


def shift(value, axis, size, by):
    return lax.ppermute(value, axis, [(i, (i + by) % size) for i in range(size)])


def gathered(value):
    return (value,) + tuple(shift(value, "x", TP, k) for k in range(1, TP))


def exchanged(parts):
    return (parts[0],) + tuple(shift(parts[k], "x", TP, k) for k in range(1, TP))


def over_chips(keep, send):
    got = shift(send, "c", NC, 1)
    rows = jnp.concatenate([keep.reshape(CHIPS, 8, OWN), got.reshape(CHIPS, 8, OWN)], axis=1)
    arrived = lax.all_to_all(rows, ("z", "y"), 0, 0)
    return arrived.reshape(CHIPS * 16, OWN)


def reduce_weights(me, keep, send, scale):
    got = shift(send, "c", NC, 1)
    span = NZ * PAD
    cols = call(pair_kernel, (me, keep, got), [half(span, HALF)] * NY)
    cols = [cols[0]] + [shift(cols[k], "y", NY, k) for k in range(1, NY)]
    parts = call(
        column_kernel, (me, *cols), [half(PAD, HALF)] * NZ, [pltpu.VMEM((NZ, PAD, HALF), F32)]
    )
    parts = [parts[0]] + [shift(parts[k], "z", NZ, k) for k in range(1, NZ)]
    out = [full(ROWS // 2, HALF)] * 2
    mine, other = call(functools.partial(last_kernel, scale), (me, *parts), out)
    other = shift(other, "c", NC, 1)
    mine, other = mine[:, : 2 * OWN], other[:, : 2 * OWN]
    first = me[3] == 0
    low, high = jnp.where(first, mine, other), jnp.where(first, other, mine)
    return jnp.concatenate([low, high], axis=1).reshape(ROWS // 2, 4, OWN)


def per_device(frames, frame_counts, weights, grad_out):
    me = jnp.stack([lax.axis_index(a) for a in ("x", "y", "z", "c")]).astype(jnp.int32)
    frame_total = grad_out.shape[0]
    scale = 1.0 / math.sqrt(frame_total * PAGE)
    ends = jnp.cumsum(frame_counts)
    ids = jnp.arange(frame_total, dtype=jnp.int32)
    before = ends[None, :] <= ids[:, None]
    holder = jnp.sum(before.astype(jnp.int32), axis=1)
    start = jnp.sum(jnp.where(before, frame_counts[None, :], 0), axis=1)
    index = holder * SLOTS + ids - start
    index = jnp.broadcast_to(jnp.tile(index, 2)[None, :], (8, 2 * frame_total))

    tokens, t_tokens = SLOTS * PAGE, 2 * PAGE
    own = call(turn_kernel, (frames,), [half(OWN, tokens)], smem=0)[0]
    chunks = gathered(own)
    turned = pl.pallas_call(
        prepare_kernel,
        out_shape=half(2, 4, OWN, D),
        grid=(2, 4),
        in_specs=[pl.BlockSpec((1, 1, D, OWN), lambda l, m: (l, m, 0, 0))],
        out_specs=pl.BlockSpec((1, 1, OWN, D), lambda l, m: (l, m, 0, 0)),
        cost_estimate=pl.CostEstimate(flops=8 * 2 * D * OWN * OWN, bytes_accessed=16 * D * OWN, transcendentals=0),
    )(weights)
    up_own = call(turn_kernel, (jnp.transpose(grad_out, (1, 0, 2)),), [half(OWN, t_tokens)], smem=0)[0]

    big = 2 * tokens * D * 4 * OWN
    blocks = [half(OWN, tokens)] * TP
    *parts, x, qkv, mix = call(
        spatial_kernel,
        (me, *chunks, turned, weights),
        blocks + [half(D, tokens), full(3 * OWN, tokens), half(OWN, tokens)],
        [pltpu.VMEM((TP, OWN, tokens), BF)] * 2,
        specs={
            5: pl.BlockSpec((1, 4, OWN, D), lambda i: (0, 0, 0, 0)),
            6: pl.BlockSpec((1, 1, D, OWN), lambda i: (0, 3, 0, 0)),
        },
        flops=big,
    )
    parts = exchanged(parts)
    keep, send = call(spread_kernel, (me, *parts, own), [half(CHIPS * 8, OWN)] * 2)
    keep, up_own = lax.optimization_barrier((keep, up_own))
    ups = gathered(up_own)
    arrived = over_chips(keep, send)
    rows = call(pick_kernel, (me, arrived, index), [half(OWN, t_tokens)])[0]
    hidden = gathered(rows)
    blocks = [half(OWN, t_tokens)] * TP
    saved = lambda n: [half(D, n)] * 3
    *parts, normed, up, grads = call(
        temporal_kernel,
        (me, *hidden, *ups, turned, weights),
        blocks + saved(t_tokens),
        [pltpu.VMEM((TP, OWN, t_tokens), BF)] * 3,
        specs={
            9: pl.BlockSpec((1, 4, OWN, D), lambda i: (1, 0, 0, 0)),
            10: pl.BlockSpec((1, 4, D, OWN), lambda i: (1, 0, 0, 0)),
        },
        flops=big,
    )
    lines = [half(CHIPS * PAD, HALF)] * 2
    room = lambda n: [pltpu.VMEM((D, n), F32), pltpu.VMEM((CHIPS * PAD, n), F32)]
    parts = exchanged(parts)
    t_keep, t_send = call(weight_kernel, (me, normed, up, grads), lines, room(t_tokens), flops=big)
    temporal_grads = reduce_weights(me, t_keep, t_send, scale)
    keep, send = call(scatter_kernel, (me, *parts, up_own, index), [half(CHIPS * 8, OWN)] * 2)
    arrived = over_chips(keep, send)
    grad_hidden = call(collect_kernel, (me, arrived), [half(OWN, tokens)])[0]
    ups = gathered(grad_hidden)
    blocks = [half(OWN, tokens)] * TP
    *parts, normed, up, grads = call(
        spatial_back_kernel,
        (me, *ups, x, qkv, mix, turned, weights),
        blocks + saved(tokens),
        [pltpu.VMEM((TP, OWN, tokens), BF)] * 2,
        specs={
            8: pl.BlockSpec((1, 1, OWN, D), lambda i: (0, 3, 0, 0)),
            9: pl.BlockSpec((1, 4, D, OWN), lambda i: (0, 0, 0, 0)),
        },
        flops=big,
    )
    s_keep, s_send = call(weight_kernel, (me, normed, up, grads), lines, room(tokens), flops=big)
    parts = exchanged(parts)
    spatial_grads = reduce_weights(me, s_keep, s_send, scale)
    frame_grads = call(finish_kernel, (*parts, grad_hidden), [half(SLOTS, PAGE, OWN)], smem=0)[0]
    return frame_grads, jnp.stack([spatial_grads, temporal_grads], axis=1)


def solution(mesh):
    fine = Mesh(mesh.devices.reshape(NZ, NY, NC, TP), ("z", "y", "c", "x"))
    seq = ("z", "y", "c")
    return jax.shard_map(
        per_device,
        mesh=fine,
        in_specs=(P(seq, None, "x"), P(), P(None, None, None, "x"), P(None, seq, "x")),
        out_specs=(P(seq, None, "x"), P(seq, None, None, "x")),
        check_vma=False,
    )
```

```python
import functools
import math

import jax
import jax.numpy as jnp
from jax import lax
from jax.experimental import pallas as pl
from jax.experimental.pallas import tpu as pltpu
from jax.sharding import Mesh
from jax.sharding import PartitionSpec as P

HD = 72
TF = 16
HEADS = 4
OWN = HEADS * HD
TP = 4
D = OWN * TP
PAGE = 128
SLOTS = 3
NZ, NY, NC = 8, 4, 2
CHIPS = NZ * NY
ROWS = 36
PAD = 40
HALF = 640
EPS = 1e-06
SCALE = HD**-0.5
F32 = jnp.float32
BF = jnp.bfloat16


def nn(a, b):
    return lax.dot_general(a, b, (((1,), (0,)), ((), ())), preferred_element_type=F32)


def nt(a, b):
    return lax.dot_general(a, b, (((1,), (1,)), ((), ())), preferred_element_type=F32)


def tn(a, b):
    return lax.dot_general(a, b, (((0,), (0,)), ((), ())), preferred_element_type=F32)


def iota(shape, dim):
    return lax.broadcasted_iota(jnp.int32, shape, dim)


def call(body, ins, outs, scratch=(), smem=1, flops=1_000_000, whole=(), limit=40):
    in_specs = [
        pl.BlockSpec(memory_space=pltpu.SMEM) if i < smem else pl.BlockSpec(memory_space=pltpu.VMEM)
        for i in range(len(ins))
    ]
    for at in whole:
        in_specs[at] = pl.BlockSpec(memory_space=pl.ANY)
    size = sum(math.prod(o.shape) * o.dtype.itemsize for o in outs)
    size += sum(math.prod(i.shape) * i.dtype.itemsize for i in ins)
    out_specs = [pl.BlockSpec(memory_space=pltpu.VMEM) for _ in outs]
    return pl.pallas_call(
        body,
        out_shape=list(outs),
        in_specs=in_specs,
        out_specs=out_specs,
        scratch_shapes=list(scratch),
        compiler_params=pltpu.CompilerParams(vmem_limit_bytes=limit * 2**20),
        cost_estimate=pl.CostEstimate(flops=flops, bytes_accessed=size, transcendentals=0),
    )(*ins)


def half(*shape):
    return jax.ShapeDtypeStruct(shape, BF)


def full(*shape):
    return jax.ShapeDtypeStruct(shape, F32)


def normalise(x):
    center = x - jnp.sum(x, axis=0, keepdims=True) * (1.0 / D)
    inverse = lax.rsqrt(jnp.sum(center * center, axis=0, keepdims=True) * (1.0 / D) + EPS)
    return center * inverse, inverse


def normalise_back(normed, inverse, up):
    mean = jnp.sum(up, axis=0, keepdims=True) * (1.0 / D)
    along = jnp.sum(up * normed, axis=0, keepdims=True) * (1.0 / D)
    return inverse * (up - mean - normed * along)


def unit(rows):
    inverse = lax.rsqrt(jnp.sum(rows * rows, axis=0, keepdims=True) * (1.0 / HD) + EPS)
    return inverse, (rows * inverse).astype(BF)


def unit_back(rows, inverse, up):
    along = jnp.sum(up * rows, axis=0, keepdims=True) * (1.0 / HD)
    return inverse * up - rows * (inverse * inverse * inverse * along)


def head_parts(qkv, h):
    q = qkv[h * HD : (h + 1) * HD]
    k = qkv[OWN + h * HD : OWN + (h + 1) * HD]
    v = qkv[2 * OWN + h * HD : 2 * OWN + (h + 1) * HD]
    q_inv, q_unit = unit(q)
    k_inv, k_unit = unit(k)
    return q, k, q_inv, q_unit, k_inv, k_unit, v.astype(BF)


def weights_of(k_unit, q_unit, mask):
    raised = jnp.exp(tn(k_unit, q_unit) * SCALE)
    if mask is not None:
        raised = jnp.where(mask, raised, 0.0)
    return raised * (1.0 / jnp.sum(raised, axis=0, keepdims=True))


def mixture_of(qkv, tokens, mask):
    heads = []
    for h in range(HEADS):
        _, _, _, q_unit, _, k_unit, v = head_parts(qkv, h)
        blocks = []
        for b in range(tokens // PAGE):
            at = slice(b * PAGE, (b + 1) * PAGE)
            probs = weights_of(k_unit[:, at], q_unit[:, at], mask)
            blocks.append(nn(v[:, at], probs.astype(BF)))
        heads.append(jnp.concatenate(blocks, axis=1))
    return jnp.concatenate(heads, axis=0).astype(BF)


def attend_back(qkv, grad_mix, tokens, mask, with_mixture):
    queries, keys, values, mixes = [], [], [], []
    for h in range(HEADS):
        q, k, q_inv, q_unit, k_inv, k_unit, v = head_parts(qkv, h)
        gm = grad_mix[h * HD : (h + 1) * HD].astype(BF)
        q_slope, k_slope, v_grad, mix = [], [], [], []
        for b in range(tokens // PAGE):
            at = slice(b * PAGE, (b + 1) * PAGE)
            probs = weights_of(k_unit[:, at], q_unit[:, at], mask)
            probs_half = probs.astype(BF)
            if with_mixture:
                mix.append(nn(v[:, at], probs_half))
            grad_probs = tn(v[:, at], gm[:, at])
            v_grad.append(nt(gm[:, at], probs_half))
            weighted = probs * grad_probs
            grad_scores = (weighted - probs * jnp.sum(weighted, axis=0, keepdims=True)).astype(BF)
            q_slope.append(nn(k_unit[:, at], grad_scores) * SCALE)
            k_slope.append(nt(q_unit[:, at], grad_scores) * SCALE)
        queries.append(unit_back(q, q_inv, jnp.concatenate(q_slope, axis=1)))
        keys.append(unit_back(k, k_inv, jnp.concatenate(k_slope, axis=1)))
        values.append(jnp.concatenate(v_grad, axis=1))
        if with_mixture:
            mixes.append(jnp.concatenate(mix, axis=1))
    join = lambda parts: jnp.concatenate(parts, axis=0).astype(BF)
    return join(queries), join(keys), join(values), join(mixes) if with_mixture else None


def assemble(own, chunks, held):
    for k, chunk in enumerate(chunks):
        at = (own + TP - k) % TP
        if len(chunk.shape) == 3:
            for n in range(chunk.shape[0]):
                held[at, :, n * PAGE : (n + 1) * PAGE] = chunk[n]
        else:
            held[at] = chunk[...]
    return held[...].reshape(D, held.shape[2])


def fetch(layer, w_ref, wide, sems):
    first = pltpu.make_async_copy(w_ref.at[layer, pl.ds(0, 3)], wide.at[pl.ds(0, 3)], sems.at[0])
    second = pltpu.make_async_copy(w_ref.at[layer, 3], wide.at[3], sems.at[1])
    second.start()
    first.start()
    return first, second


def deal(own, value, held, outs):
    held[...] = value.astype(BF).reshape(held.shape)
    for k, out in enumerate(outs):
        out[...] = held[(own + k) % TP]


def pages(ref):
    return jnp.concatenate([ref[n] for n in range(ref.shape[0])], axis=1)


def spatial_kernel(me, c0, c1, c2, c3, w_ref, p0, p1, p2, p3, x_out, qkv_out, mix_out, held, dealt, wide, sems):
    first, second = fetch(0, w_ref, wide, sems)
    x = assemble(me[0], (c0, c1, c2, c3), held)
    x_out[...] = x
    normed, _ = normalise(x.astype(F32))
    normed = normed.astype(BF)
    first.wait()
    qkv = nn(wide[:3].reshape(3 * OWN, D), normed)
    qkv_out[...] = qkv
    mix = mixture_of(qkv, x.shape[1], None)
    mix_out[...] = mix
    second.wait()
    deal(me[0], tn(wide[3], mix), dealt, (p0, p1, p2, p3))


def temporal_kernel(
    me, h0, h1, h2, h3, g0, g1, g2, g3, w_ref,
    p0, p1, p2, p3, normed_out, up_out, grads_out, held, held_g, dealt, wide, sems,
):
    first, second = fetch(1, w_ref, wide, sems)
    x = assemble(me[0], (h0, h1, h2, h3), held)
    up = assemble(me[0], (g0, g1, g2, g3), held_g)
    up_out[...] = up
    normed, inverse = normalise(x.astype(F32))
    normed_half = normed.astype(BF)
    normed_out[...] = normed_half
    second.wait()
    grad_mix = nn(wide[3], up)
    first.wait()
    qkv = nn(wide[:3].reshape(3 * OWN, D), normed_half)
    mask = (iota((PAGE, PAGE), 0) // TF) == (iota((PAGE, PAGE), 1) // TF)
    gq, gk, gv, mix = attend_back(qkv, grad_mix, x.shape[1], mask, True)
    for m, part in enumerate((gq, gk, gv, mix)):
        grads_out[m * OWN : (m + 1) * OWN] = part
    grad_normed = tn(wide[:3].reshape(3 * OWN, D), jnp.concatenate([gq, gk, gv], axis=0))
    deal(me[0], normalise_back(normed, inverse, grad_normed), dealt, (p0, p1, p2, p3))


def spatial_back_kernel(
    me, g0, g1, g2, g3, x_ref, qkv_ref, mix_ref, w_ref,
    p0, p1, p2, p3, normed_out, up_out, grads_out, held_g, dealt, wide, sems,
):
    first, second = fetch(0, w_ref, wide, sems)
    up = assemble(me[0], (g0, g1, g2, g3), held_g)
    up_out[...] = up
    normed, inverse = normalise(x_ref[...].astype(F32))
    normed_out[...] = normed.astype(BF)
    second.wait()
    grad_mix = nn(wide[3], up)
    first.wait()
    gq, gk, gv, _ = attend_back(qkv_ref[...], grad_mix, up.shape[1], None, False)
    for m, part in enumerate((gq, gk, gv, mix_ref[...])):
        grads_out[m * OWN : (m + 1) * OWN] = part
    grad_normed = tn(wide[:3].reshape(3 * OWN, D), jnp.concatenate([gq, gk, gv], axis=0))
    deal(me[0], normalise_back(normed, inverse, grad_normed), dealt, (p0, p1, p2, p3))


def regroup(ref, held):
    for y in range(NY):
        for z in range(NZ):
            at = (y * NZ + z) * PAD
            held[at + PAD - 8 : at + PAD] = jnp.zeros((8, held.shape[1]), F32)
            held[at : at + ROWS] = ref[z * NY * ROWS + y * ROWS : z * NY * ROWS + (y + 1) * ROWS]
    return held[...].astype(BF)


def weight_kernel(me, normed_ref, up_ref, grads_ref, keep, send, wide, held):
    tokens = normed_ref.shape[1]
    zeros = lambda n: jnp.zeros((n, tokens), BF)
    wide[...] = normed_ref[...].astype(F32)
    lines = regroup(wide, held)
    wide[...] = up_ref[...].astype(F32)
    up_lines = regroup(wide, held)
    first = nt(lines, jnp.concatenate([grads_ref[: 2 * OWN], zeros(HALF - 2 * OWN)], axis=0)).astype(BF)
    values, mix = grads_ref[2 * OWN : 3 * OWN], grads_ref[3 * OWN :]
    low = nt(lines, jnp.concatenate([values, zeros(96)], axis=0))
    low = low + nt(up_lines, jnp.concatenate([zeros(OWN), mix[:96]], axis=0))
    high = nt(up_lines, jnp.concatenate([mix[96:], zeros(64)], axis=0))
    core = me[3]

    @pl.when(core == 0)
    def _():
        keep[...] = first
        send[:, :384] = low.astype(BF)
        send[:, 384:] = high.astype(BF)

    @pl.when(core == 1)
    def _():
        send[...] = first
        keep[:, :384] = low.astype(BF)
        keep[:, 384:] = high.astype(BF)


def pair_kernel(me, keep, got, o0, o1, o2, o3):
    span = NZ * PAD
    for k, out in enumerate((o0, o1, o2, o3)):
        rows = pl.ds(pl.multiple_of(((me[1] + k) % NY) * span, 16), span)
        out[...] = (keep[rows].astype(F32) + got[rows].astype(F32)).astype(BF)


def column_kernel(*refs):
    ins, out = refs[:-1], refs[-1]
    for layer in range(2):
        a, b, c, d = (ref[...].astype(F32) for ref in ins[NY * layer : NY * layer + NY])
        out[:, layer * HALF : (layer + 1) * HALF] = (a + b + c + d).astype(BF)


def last_kernel(scale, me, parts, keep, send):
    total = parts[0].astype(F32)
    for z in range(1, NZ):
        total = total + parts[z].astype(F32)
    total = total * scale
    upper, lower = total[: ROWS // 2], total[ROWS // 2 : ROWS]
    first = me[3] == 0
    keep[...] = jnp.where(first, upper, lower)
    send[...] = jnp.where(first, lower, upper)


def spread_kernel(me, a, b, c, d, own, keep, send):
    total = a[...].astype(F32) + b[...].astype(F32) + c[...].astype(F32) + d[...].astype(F32)
    hidden = (pages(own).astype(F32) + total).astype(BF)
    rows, tokens = CHIPS * 8, SLOTS * PAGE
    row, col = iota((rows, tokens), 0), iota((rows, tokens), 1)
    part, chip = row % 8, row // 8
    base = (part // 2) * PAGE + 4 * chip + part % 2
    for out, core in ((keep, me[3]), (send, 1 - me[3])):
        pick = jnp.logical_and(part < 6, col == base + 2 * core)
        out[...] = nt(pick.astype(BF), hidden).astype(BF)


def pick_kernel(me, arrived, index_ref, out_ref):
    rows, tokens = CHIPS * 16, 2 * PAGE
    row, col = iota((rows, tokens), 0), iota((rows, tokens), 1)
    part, chip, rel = row % 8, row // 16, (row // 8) % 2
    core = jnp.where(rel == 0, me[3], 1 - me[3])
    slot = (2 * chip + core) * SLOTS + part // 2
    pick = jnp.logical_and(part < 6, part % 2 == col // PAGE)
    pick = jnp.logical_and(pick, slot == index_ref[0:1])
    out_ref[...] = tn(arrived[...], pick.astype(BF)).astype(BF)


def scatter_kernel(me, a, b, c, d, own, index_ref, keep, send):
    total = a[...].astype(F32) + b[...].astype(F32) + c[...].astype(F32) + d[...].astype(F32)
    grad = (pages(own).astype(F32) + total).astype(BF)
    rows, tokens = CHIPS * 8, 2 * PAGE
    row, col = iota((rows, tokens), 0), iota((rows, tokens), 1)
    part, chip = row % 8, row // 8
    live = jnp.logical_and(part < 6, part % 2 == col // PAGE)
    for out, core in ((keep, me[3]), (send, 1 - me[3])):
        slot = (2 * chip + core) * SLOTS + part // 2
        pick = jnp.logical_and(live, slot == index_ref[0:1])
        out[...] = nt(pick.astype(BF), grad).astype(BF)


def collect_kernel(me, arrived, out_ref):
    rows, tokens = CHIPS * 16, SLOTS * PAGE
    row, col = iota((rows, tokens), 0), iota((rows, tokens), 1)
    part, chip, rel = row % 8, row // 16, (row // 8) % 2
    core = jnp.where(rel == 0, me[3], 1 - me[3])
    position = 4 * chip + 2 * core + part % 2
    pick = jnp.logical_and(part < 6, col == (part // 2) * PAGE + position)
    out_ref[...] = tn(arrived[...], pick.astype(BF)).astype(BF)


def finish_kernel(a, b, c, d, own, out_ref):
    total = a[...].astype(F32) + b[...].astype(F32) + c[...].astype(F32) + d[...].astype(F32)
    grad = (own[...].astype(F32) + total).astype(BF)
    for n in range(SLOTS):
        out_ref[n] = grad[:, n * PAGE : (n + 1) * PAGE]


def shift(value, axis, size, by):
    return lax.ppermute(value, axis, [(i, (i + by) % size) for i in range(size)])


def gathered(value):
    return (value,) + tuple(shift(value, "x", TP, k) for k in range(1, TP))


def exchanged(parts):
    return (parts[0],) + tuple(shift(parts[k], "x", TP, k) for k in range(1, TP))


def over_chips(keep, send):
    got = shift(send, "c", NC, 1)
    rows = jnp.concatenate([keep.reshape(CHIPS, 8, OWN), got.reshape(CHIPS, 8, OWN)], axis=1)
    arrived = lax.all_to_all(rows, ("z", "y"), 0, 0)
    return arrived.reshape(CHIPS * 16, OWN)


def over_pair(me, keep, send):
    got = shift(send, "c", NC, 1)
    return call(pair_kernel, (me, keep, got), [half(NZ * PAD, HALF)] * NY)


def over_column(cols):
    return [cols[0]] + [shift(cols[k], "y", NY, k) for k in range(1, NY)]


def over_rows(me, spatial, temporal, scale):
    sums = call(column_kernel, (*spatial, *temporal), [half(NZ * PAD, 2 * HALF)], smem=0)[0]
    parts = lax.all_to_all(sums.reshape(NZ, PAD, 2 * HALF), "z", 0, 0)
    out = [full(ROWS // 2, 2 * HALF)] * 2
    mine, other = call(functools.partial(last_kernel, scale), (me, parts), out)
    other = shift(other, "c", NC, 1)
    mine, other = (v.reshape(ROWS // 2, 2, HALF)[:, :, : 2 * OWN] for v in (mine, other))
    first = me[3] == 0
    low, high = jnp.where(first, mine, other), jnp.where(first, other, mine)
    return jnp.concatenate([low, high], axis=2).reshape(ROWS // 2, 2, 4, OWN)


def per_device(frames, frame_counts, weights, grad_out):
    me = jnp.stack([lax.axis_index(a) for a in ("x", "y", "z", "c")]).astype(jnp.int32)
    frame_total = grad_out.shape[0]
    scale = 1.0 / math.sqrt(frame_total * PAGE)
    ends = jnp.cumsum(frame_counts)
    ids = jnp.arange(frame_total, dtype=jnp.int32)
    before = ends[None, :] <= ids[:, None]
    holder = jnp.sum(before.astype(jnp.int32), axis=1)
    start = jnp.sum(jnp.where(before, frame_counts[None, :], 0), axis=1)
    index = holder * SLOTS + ids - start
    index = jnp.broadcast_to(jnp.tile(index, 2)[None, :], (8, 2 * frame_total))

    tokens, t_tokens = SLOTS * PAGE, 2 * PAGE
    own = jnp.transpose(frames, (0, 2, 1))
    up_own = jnp.transpose(grad_out, (1, 2, 0))
    turned = jnp.swapaxes(weights, 2, 3)
    copies = [pltpu.VMEM((4, OWN, D), BF), pltpu.SemaphoreType.DMA((2,))]

    big = 2 * tokens * D * 4 * OWN
    blocks = [half(OWN, tokens)] * TP
    *parts, x, qkv, mix = call(
        spatial_kernel,
        (me, *gathered(own), turned),
        blocks + [half(D, tokens), full(3 * OWN, tokens), half(OWN, tokens)],
        [pltpu.VMEM((TP, OWN, tokens), BF)] * 2 + copies,
        whole=(5,),
        limit=50,
        flops=big,
    )
    parts = exchanged(parts)
    keep, send = call(spread_kernel, (me, *parts, own), [half(CHIPS * 8, OWN)] * 2)
    keep, up_own = lax.optimization_barrier((keep, up_own))
    ups = gathered(up_own)
    arrived = over_chips(keep, send)
    rows = call(pick_kernel, (me, arrived, index), [half(OWN, t_tokens)])[0]
    hidden = gathered(rows)
    blocks = [half(OWN, t_tokens)] * TP
    saved = lambda n: [half(D, n)] * 3
    *parts, normed, up, grads = call(
        temporal_kernel,
        (me, *hidden, *ups, turned),
        blocks + saved(t_tokens),
        [pltpu.VMEM((TP, OWN, t_tokens), BF)] * 3 + copies,
        whole=(9,),
        limit=50,
        flops=big,
    )
    lines = [half(CHIPS * PAD, HALF)] * 2
    room = lambda n: [pltpu.VMEM((D, n), F32), pltpu.VMEM((CHIPS * PAD, n), F32)]
    parts = exchanged(parts)
    t_keep, t_send = call(weight_kernel, (me, normed, up, grads), lines, room(t_tokens), flops=big)
    parts, t_keep, t_send = lax.optimization_barrier((parts, t_keep, t_send))
    keep, send = call(scatter_kernel, (me, *parts, up_own, index), [half(CHIPS * 8, OWN)] * 2)
    t_cols = over_pair(me, t_keep, t_send)
    arrived = over_chips(keep, send)
    arrived, t_cols = lax.optimization_barrier((arrived, t_cols))
    grad_hidden = call(collect_kernel, (me, arrived), [half(OWN, tokens)])[0]
    ups = gathered(grad_hidden)
    t_cols = over_column(t_cols)
    blocks = [half(OWN, tokens)] * TP
    *parts, normed, up, grads = call(
        spatial_back_kernel,
        (me, *ups, x, qkv, mix, turned),
        blocks + saved(tokens),
        [pltpu.VMEM((TP, OWN, tokens), BF)] * 2 + copies,
        whole=(8,),
        limit=50,
        flops=big,
    )
    s_keep, s_send = call(weight_kernel, (me, normed, up, grads), lines, room(tokens), flops=big)
    s_cols = over_column(over_pair(me, s_keep, s_send))
    parts = exchanged(parts)
    weight_grads = over_rows(me, s_cols, t_cols, scale)
    frame_grads = call(finish_kernel, (*parts, grad_hidden), [half(SLOTS, OWN, PAGE)], smem=0)[0]
    return jnp.transpose(frame_grads, (0, 2, 1)), weight_grads


def solution(mesh):
    fine = Mesh(mesh.devices.reshape(NZ, NY, NC, TP), ("z", "y", "c", "x"))
    seq = ("z", "y", "c")
    return jax.shard_map(
        per_device,
        mesh=fine,
        in_specs=(P(seq, None, "x"), P(), P(None, None, None, "x"), P(None, seq, "x")),
        out_specs=(P(seq, None, "x"), P(seq, None, None, "x")),
        check_vma=False,
    )
```

```python
import functools
import math

import jax
import jax.numpy as jnp
from jax import lax
from jax.experimental import pallas as pl
from jax.experimental.pallas import tpu as pltpu
from jax.sharding import Mesh
from jax.sharding import PartitionSpec as P

HD = 72
TF = 16
HEADS = 4
OWN = HEADS * HD
TP = 4
D = OWN * TP
PAGE = 128
SLOTS = 3
NZ, NY, NC = 8, 4, 2
CHIPS = NZ * NY
ROWS = 36
PAD = 40
HALF = 640
MOST = 512
EPS = 1e-06
SCALE = HD**-0.5
F32 = jnp.float32
BF = jnp.bfloat16


def nn(a, b):
    return lax.dot_general(a, b, (((1,), (0,)), ((), ())), preferred_element_type=F32)


def nt(a, b):
    return lax.dot_general(a, b, (((1,), (1,)), ((), ())), preferred_element_type=F32)


def tn(a, b):
    return lax.dot_general(a, b, (((0,), (0,)), ((), ())), preferred_element_type=F32)


def iota(shape, dim):
    return lax.broadcasted_iota(jnp.int32, shape, dim)


def call(body, ins, outs, scratch=(), smem=1, flops=1_000_000, whole=(), limit=40):
    in_specs = [
        pl.BlockSpec(memory_space=pltpu.SMEM) if i < smem else pl.BlockSpec(memory_space=pltpu.VMEM)
        for i in range(len(ins))
    ]
    for at in whole:
        in_specs[at] = pl.BlockSpec(memory_space=pl.ANY)
    size = sum(math.prod(o.shape) * o.dtype.itemsize for o in outs)
    size += sum(math.prod(i.shape) * i.dtype.itemsize for i in ins)
    out_specs = [pl.BlockSpec(memory_space=pltpu.VMEM) for _ in outs]
    return pl.pallas_call(
        body,
        out_shape=list(outs),
        in_specs=in_specs,
        out_specs=out_specs,
        scratch_shapes=list(scratch),
        compiler_params=pltpu.CompilerParams(vmem_limit_bytes=limit * 2**20),
        cost_estimate=pl.CostEstimate(flops=flops, bytes_accessed=size, transcendentals=0),
    )(*ins)


def half(*shape):
    return jax.ShapeDtypeStruct(shape, BF)


def full(*shape):
    return jax.ShapeDtypeStruct(shape, F32)


def normalise(x):
    center = x - jnp.sum(x, axis=0, keepdims=True) * (1.0 / D)
    inverse = lax.rsqrt(jnp.sum(center * center, axis=0, keepdims=True) * (1.0 / D) + EPS)
    return center * inverse, inverse


def normalise_back(normed, inverse, up):
    mean = jnp.sum(up, axis=0, keepdims=True) * (1.0 / D)
    along = jnp.sum(up * normed, axis=0, keepdims=True) * (1.0 / D)
    return inverse * (up - mean - normed * along)


def unit(rows):
    inverse = lax.rsqrt(jnp.sum(rows * rows, axis=0, keepdims=True) * (1.0 / HD) + EPS)
    return inverse, (rows * inverse).astype(BF)


def unit_back(rows, inverse, up):
    along = jnp.sum(up * rows, axis=0, keepdims=True) * (1.0 / HD)
    return inverse * up - rows * (inverse * inverse * inverse * along)


def head_parts(qkv, h):
    q = qkv[h * HD : (h + 1) * HD]
    k = qkv[OWN + h * HD : OWN + (h + 1) * HD]
    v = qkv[2 * OWN + h * HD : 2 * OWN + (h + 1) * HD]
    q_inv, q_unit = unit(q)
    k_inv, k_unit = unit(k)
    return q, k, q_inv, q_unit, k_inv, k_unit, v.astype(BF)


def weights_of(k_unit, q_unit, mask):
    raised = jnp.exp(tn(k_unit, q_unit) * SCALE)
    if mask is not None:
        raised = jnp.where(mask, raised, 0.0)
    return raised * (1.0 / jnp.sum(raised, axis=0, keepdims=True))


def mixture_of(qkv, tokens, mask):
    heads = []
    for h in range(HEADS):
        _, _, _, q_unit, _, k_unit, v = head_parts(qkv, h)
        blocks = []
        for b in range(tokens // PAGE):
            at = slice(b * PAGE, (b + 1) * PAGE)
            probs = weights_of(k_unit[:, at], q_unit[:, at], mask)
            blocks.append(nn(v[:, at], probs.astype(BF)))
        heads.append(jnp.concatenate(blocks, axis=1))
    return jnp.concatenate(heads, axis=0).astype(BF)


def attend_back(qkv, grad_mix, tokens, mask, with_mixture):
    queries, keys, values, mixes = [], [], [], []
    for h in range(HEADS):
        q, k, q_inv, q_unit, k_inv, k_unit, v = head_parts(qkv, h)
        gm = grad_mix[h * HD : (h + 1) * HD].astype(BF)
        q_slope, k_slope, v_grad, mix = [], [], [], []
        for b in range(tokens // PAGE):
            at = slice(b * PAGE, (b + 1) * PAGE)
            probs = weights_of(k_unit[:, at], q_unit[:, at], mask)
            probs_half = probs.astype(BF)
            if with_mixture:
                mix.append(nn(v[:, at], probs_half))
            grad_probs = tn(v[:, at], gm[:, at])
            v_grad.append(nt(gm[:, at], probs_half))
            weighted = probs * grad_probs
            grad_scores = (weighted - probs * jnp.sum(weighted, axis=0, keepdims=True)).astype(BF)
            q_slope.append(nn(k_unit[:, at], grad_scores) * SCALE)
            k_slope.append(nt(q_unit[:, at], grad_scores) * SCALE)
        queries.append(unit_back(q, q_inv, jnp.concatenate(q_slope, axis=1)))
        keys.append(unit_back(k, k_inv, jnp.concatenate(k_slope, axis=1)))
        values.append(jnp.concatenate(v_grad, axis=1))
        if with_mixture:
            mixes.append(jnp.concatenate(mix, axis=1))
    join = lambda parts: jnp.concatenate(parts, axis=0).astype(BF)
    return join(queries), join(keys), join(values), join(mixes) if with_mixture else None


def assemble(own, chunks, held):
    for k, chunk in enumerate(chunks):
        at = (own + TP - k) % TP
        if len(chunk.shape) == 3:
            for n in range(chunk.shape[0]):
                held[at, :, n * PAGE : (n + 1) * PAGE] = chunk[n]
        else:
            held[at] = chunk[...]
    return held[...].reshape(D, held.shape[2])


def fetch(layer, w_ref, wide, sems):
    first = pltpu.make_async_copy(w_ref.at[layer, pl.ds(0, 3)], wide.at[pl.ds(0, 3)], sems.at[0])
    second = pltpu.make_async_copy(w_ref.at[layer, 3], wide.at[3], sems.at[1])
    second.start()
    first.start()
    return first, second


def deal(own, value, held, outs):
    held[...] = value.astype(BF).reshape(held.shape)
    for k, out in enumerate(outs):
        out[...] = held[(own + k) % TP]


def pages(ref):
    return jnp.concatenate([ref[n] for n in range(ref.shape[0])], axis=1)


def spatial_kernel(me, c0, c1, c2, c3, w_ref, p0, p1, p2, p3, x_out, qkv_out, mix_out, held, dealt, wide, sems):
    first, second = fetch(0, w_ref, wide, sems)
    x = assemble(me[0], (c0, c1, c2, c3), held)
    x_out[...] = x
    normed, _ = normalise(x.astype(F32))
    normed = normed.astype(BF)
    first.wait()
    qkv = nn(wide[:3].reshape(3 * OWN, D), normed)
    qkv_out[...] = qkv
    mix = mixture_of(qkv, x.shape[1], None)
    mix_out[...] = mix
    second.wait()
    deal(me[0], tn(wide[3], mix), dealt, (p0, p1, p2, p3))


def temporal_kernel(
    me, h0, h1, h2, h3, g0, g1, g2, g3, w_ref,
    p0, p1, p2, p3, normed_out, up_out, grads_out, held, held_g, dealt, wide, sems,
):
    first, second = fetch(1, w_ref, wide, sems)
    x = assemble(me[0], (h0, h1, h2, h3), held)
    up = assemble(me[0], (g0, g1, g2, g3), held_g)
    up_out[...] = up
    normed, inverse = normalise(x.astype(F32))
    normed_half = normed.astype(BF)
    normed_out[...] = normed_half
    second.wait()
    grad_mix = nn(wide[3], up)
    first.wait()
    qkv = nn(wide[:3].reshape(3 * OWN, D), normed_half)
    mask = (iota((PAGE, PAGE), 0) // TF) == (iota((PAGE, PAGE), 1) // TF)
    gq, gk, gv, mix = attend_back(qkv, grad_mix, x.shape[1], mask, True)
    for m, part in enumerate((gq, gk, gv, mix)):
        grads_out[m * OWN : (m + 1) * OWN] = part
    grad_normed = tn(wide[:3].reshape(3 * OWN, D), jnp.concatenate([gq, gk, gv], axis=0))
    deal(me[0], normalise_back(normed, inverse, grad_normed), dealt, (p0, p1, p2, p3))


def spatial_back_kernel(
    me, g0, g1, g2, g3, x_ref, qkv_ref, mix_ref, w_ref,
    p0, p1, p2, p3, normed_out, up_out, grads_out, held_g, dealt, wide, sems,
):
    first, second = fetch(0, w_ref, wide, sems)
    up = assemble(me[0], (g0, g1, g2, g3), held_g)
    up_out[...] = up
    normed, inverse = normalise(x_ref[...].astype(F32))
    normed_out[...] = normed.astype(BF)
    second.wait()
    grad_mix = nn(wide[3], up)
    first.wait()
    gq, gk, gv, _ = attend_back(qkv_ref[...], grad_mix, up.shape[1], None, False)
    for m, part in enumerate((gq, gk, gv, mix_ref[...])):
        grads_out[m * OWN : (m + 1) * OWN] = part
    grad_normed = tn(wide[:3].reshape(3 * OWN, D), jnp.concatenate([gq, gk, gv], axis=0))
    deal(me[0], normalise_back(normed, inverse, grad_normed), dealt, (p0, p1, p2, p3))


def regroup(ref, held):
    for y in range(NY):
        for z in range(NZ):
            at = (y * NZ + z) * PAD
            held[at + PAD - 8 : at + PAD] = jnp.zeros((8, held.shape[1]), F32)
            held[at : at + ROWS] = ref[z * NY * ROWS + y * ROWS : z * NY * ROWS + (y + 1) * ROWS]
    return held[...].astype(BF)


def weight_kernel(me, normed_ref, up_ref, grads_ref, keep, send, wide, held):
    tokens = normed_ref.shape[1]
    zeros = lambda n: jnp.zeros((n, tokens), BF)
    wide[...] = normed_ref[...].astype(F32)
    lines = regroup(wide, held)
    wide[...] = up_ref[...].astype(F32)
    up_lines = regroup(wide, held)
    first = nt(lines, jnp.concatenate([grads_ref[: 2 * OWN], zeros(HALF - 2 * OWN)], axis=0)).astype(BF)
    values, mix = grads_ref[2 * OWN : 3 * OWN], grads_ref[3 * OWN :]
    low = nt(lines, jnp.concatenate([values, zeros(96)], axis=0))
    low = low + nt(up_lines, jnp.concatenate([zeros(OWN), mix[:96]], axis=0))
    high = nt(up_lines, jnp.concatenate([mix[96:], zeros(64)], axis=0))
    core = me[3]

    @pl.when(core == 0)
    def _():
        keep[...] = first
        send[:, :384] = low.astype(BF)
        send[:, 384:] = high.astype(BF)

    @pl.when(core == 1)
    def _():
        send[...] = first
        keep[:, :384] = low.astype(BF)
        keep[:, 384:] = high.astype(BF)


def pair_kernel(me, keep, got, *outs):
    span = NZ * PAD
    for k, out in enumerate(outs):
        rows = pl.ds(pl.multiple_of(((me[1] + k) % NY) * span, 16), span)
        out[...] = (keep[rows].astype(F32) + got[rows].astype(F32)).astype(BF)


def split_kernel(me, keep, got, t0, t1, t2, t3, o0, o1, o2, o3, packed):
    span = NZ * PAD
    for k, out in enumerate((o0, o1, o2, o3)):
        rows = pl.ds(pl.multiple_of(((me[1] + k) % NY) * span, 16), span)
        out[...] = (keep[rows, :MOST].astype(F32) + got[rows, :MOST].astype(F32)).astype(BF)
    rest = keep[:, MOST:].astype(F32) + got[:, MOST:].astype(F32)
    column = t0[...].astype(F32) + t1[...].astype(F32) + t2[...].astype(F32) + t3[...].astype(F32)
    for z in range(NZ):
        lines = [rest[(y * NZ + z) * PAD : (y * NZ + z + 1) * PAD] for y in range(NY)]
        piece = column[z * PAD : (z + 1) * PAD]
        lines += [piece[:, n * PAGE : (n + 1) * PAGE] for n in range(HALF // PAGE)]
        packed[z] = jnp.concatenate(lines, axis=0).astype(BF)


def column_kernel(a, b, c, d, out):
    total = a[...].astype(F32) + b[...].astype(F32) + c[...].astype(F32) + d[...].astype(F32)
    out[...] = total.astype(BF)


def unpack_kernel(me, arrived, o0, o1, o2, o3, temporal, held):
    total = arrived[0].astype(F32)
    for z in range(1, NZ):
        total = total + arrived[z].astype(F32)
    held[...] = total[: NY * PAD].reshape(NY, PAD, PAGE)
    for k, out in enumerate((o0, o1, o2, o3)):
        out[...] = held[(me[1] + k) % NY]
    for n in range(HALF // PAGE):
        at = (NY + n) * PAD
        temporal[:, n * PAGE : (n + 1) * PAGE] = total[at : at + PAD]


def last_kernel(scale, me, parts, r0, r1, r2, r3, temporal, keep, send):
    total = parts[0].astype(F32)
    for z in range(1, NZ):
        total = total + parts[z].astype(F32)
    first = me[3] == 0
    rest = r0[...] + r1[...] + r2[...] + r3[...]
    for at, value in ((0, total), (MOST, rest), (HALF, temporal[...])):
        value = value * scale
        upper, lower = value[: ROWS // 2], value[ROWS // 2 : ROWS]
        keep[:, at : at + value.shape[1]] = jnp.where(first, upper, lower)
        send[:, at : at + value.shape[1]] = jnp.where(first, lower, upper)


def spread_kernel(me, a, b, c, d, own, keep, send):
    total = a[...].astype(F32) + b[...].astype(F32) + c[...].astype(F32) + d[...].astype(F32)
    hidden = (pages(own).astype(F32) + total).astype(BF)
    rows, tokens = CHIPS * 8, SLOTS * PAGE
    row, col = iota((rows, tokens), 0), iota((rows, tokens), 1)
    part, chip = row % 8, row // 8
    base = (part // 2) * PAGE + 4 * chip + part % 2
    for out, core in ((keep, me[3]), (send, 1 - me[3])):
        pick = jnp.logical_and(part < 6, col == base + 2 * core)
        out[...] = nt(pick.astype(BF), hidden).astype(BF)


def pick_kernel(me, arrived, index_ref, out_ref):
    rows, tokens = CHIPS * 16, 2 * PAGE
    row, col = iota((rows, tokens), 0), iota((rows, tokens), 1)
    part, chip, rel = row % 8, row // 16, (row // 8) % 2
    core = jnp.where(rel == 0, me[3], 1 - me[3])
    slot = (2 * chip + core) * SLOTS + part // 2
    pick = jnp.logical_and(part < 6, part % 2 == col // PAGE)
    pick = jnp.logical_and(pick, slot == index_ref[0:1])
    out_ref[...] = tn(arrived[...], pick.astype(BF)).astype(BF)


def scatter_kernel(me, a, b, c, d, own, index_ref, keep, send):
    total = a[...].astype(F32) + b[...].astype(F32) + c[...].astype(F32) + d[...].astype(F32)
    grad = (pages(own).astype(F32) + total).astype(BF)
    rows, tokens = CHIPS * 8, 2 * PAGE
    row, col = iota((rows, tokens), 0), iota((rows, tokens), 1)
    part, chip = row % 8, row // 8
    live = jnp.logical_and(part < 6, part % 2 == col // PAGE)
    for out, core in ((keep, me[3]), (send, 1 - me[3])):
        slot = (2 * chip + core) * SLOTS + part // 2
        pick = jnp.logical_and(live, slot == index_ref[0:1])
        out[...] = nt(pick.astype(BF), grad).astype(BF)


def collect_kernel(me, arrived, out_ref):
    rows, tokens = CHIPS * 16, SLOTS * PAGE
    row, col = iota((rows, tokens), 0), iota((rows, tokens), 1)
    part, chip, rel = row % 8, row // 16, (row // 8) % 2
    core = jnp.where(rel == 0, me[3], 1 - me[3])
    position = 4 * chip + 2 * core + part % 2
    pick = jnp.logical_and(part < 6, col == (part // 2) * PAGE + position)
    out_ref[...] = tn(arrived[...], pick.astype(BF)).astype(BF)


def finish_kernel(a, b, c, d, own, out_ref):
    total = a[...].astype(F32) + b[...].astype(F32) + c[...].astype(F32) + d[...].astype(F32)
    grad = (own[...].astype(F32) + total).astype(BF)
    for n in range(SLOTS):
        out_ref[n] = grad[:, n * PAGE : (n + 1) * PAGE]


def shift(value, axis, size, by):
    return lax.ppermute(value, axis, [(i, (i + by) % size) for i in range(size)])


def gathered(value):
    return (value,) + tuple(shift(value, "x", TP, k) for k in range(1, TP))


def exchanged(parts):
    return (parts[0],) + tuple(shift(parts[k], "x", TP, k) for k in range(1, TP))


def over_chips(keep, send):
    got = shift(send, "c", NC, 1)
    rows = jnp.concatenate([keep.reshape(CHIPS, 8, OWN), got.reshape(CHIPS, 8, OWN)], axis=1)
    arrived = lax.all_to_all(rows, ("z", "y"), 0, 0)
    return arrived.reshape(CHIPS * 16, OWN)


def over_column(cols):
    return [cols[0]] + [shift(cols[k], "y", NY, k) for k in range(1, NY)]


def temporal_pairs(me, keep, send):
    got = shift(send, "c", NC, 1)
    return call(pair_kernel, (me, keep, got), [half(NZ * PAD, HALF)] * NY)


def reduce_weights(me, keep, send, temporal, scale):
    got = shift(send, "c", NC, 1)
    packs = [half(NZ * PAD, MOST)] * NY + [half(NZ, (2 * NY + 1) * PAD, PAGE)]
    *cols, packed = call(split_kernel, (me, keep, got, *temporal), packs)
    cols = over_column(cols)
    arrived = lax.all_to_all(packed, "z", 0, 0)
    column = call(column_kernel, cols, [half(NZ * PAD, MOST)], smem=0)[0]
    *rest, temporal = call(
        unpack_kernel,
        (me, arrived),
        [full(PAD, PAGE)] * NY + [full(PAD, HALF)],
        [pltpu.VMEM((NY, PAD, PAGE), F32)],
    )
    parts = lax.all_to_all(column.reshape(NZ, PAD, MOST), "z", 0, 0)
    rest = over_column(rest)
    out = [full(ROWS // 2, 2 * HALF)] * 2
    mine, other = call(functools.partial(last_kernel, scale), (me, parts, *rest, temporal), out)
    other = shift(other, "c", NC, 1)
    mine, other = (v.reshape(ROWS // 2, 2, HALF)[:, :, : 2 * OWN] for v in (mine, other))
    first = me[3] == 0
    low, high = jnp.where(first, mine, other), jnp.where(first, other, mine)
    return jnp.concatenate([low, high], axis=2).reshape(ROWS // 2, 2, 4, OWN)


def per_device(frames, frame_counts, weights, grad_out):
    me = jnp.stack([lax.axis_index(a) for a in ("x", "y", "z", "c")]).astype(jnp.int32)
    frame_total = grad_out.shape[0]
    scale = 1.0 / math.sqrt(frame_total * PAGE)
    ends = jnp.cumsum(frame_counts)
    ids = jnp.arange(frame_total, dtype=jnp.int32)
    before = ends[None, :] <= ids[:, None]
    holder = jnp.sum(before.astype(jnp.int32), axis=1)
    start = jnp.sum(jnp.where(before, frame_counts[None, :], 0), axis=1)
    index = holder * SLOTS + ids - start
    index = jnp.broadcast_to(jnp.tile(index, 2)[None, :], (8, 2 * frame_total))

    tokens, t_tokens = SLOTS * PAGE, 2 * PAGE
    own = jnp.transpose(frames, (0, 2, 1))
    up_own = jnp.transpose(grad_out, (1, 2, 0))
    turned = jnp.swapaxes(weights, 2, 3)
    copies = [pltpu.VMEM((4, OWN, D), BF), pltpu.SemaphoreType.DMA((2,))]

    big = 2 * tokens * D * 4 * OWN
    blocks = [half(OWN, tokens)] * TP
    *parts, x, qkv, mix = call(
        spatial_kernel,
        (me, *gathered(own), turned),
        blocks + [half(D, tokens), full(3 * OWN, tokens), half(OWN, tokens)],
        [pltpu.VMEM((TP, OWN, tokens), BF)] * 2 + copies,
        whole=(5,),
        limit=50,
        flops=big,
    )
    parts = exchanged(parts)
    keep, send = call(spread_kernel, (me, *parts, own), [half(CHIPS * 8, OWN)] * 2)
    keep, up_own = lax.optimization_barrier((keep, up_own))
    ups = gathered(up_own)
    arrived = over_chips(keep, send)
    rows = call(pick_kernel, (me, arrived, index), [half(OWN, t_tokens)])[0]
    hidden = gathered(rows)
    blocks = [half(OWN, t_tokens)] * TP
    saved = lambda n: [half(D, n)] * 3
    *parts, normed, up, grads = call(
        temporal_kernel,
        (me, *hidden, *ups, turned),
        blocks + saved(t_tokens),
        [pltpu.VMEM((TP, OWN, t_tokens), BF)] * 3 + copies,
        whole=(9,),
        limit=50,
        flops=big,
    )
    lines = [half(CHIPS * PAD, HALF)] * 2
    room = lambda n: [pltpu.VMEM((D, n), F32), pltpu.VMEM((CHIPS * PAD, n), F32)]
    parts = exchanged(parts)
    t_keep, t_send = call(weight_kernel, (me, normed, up, grads), lines, room(t_tokens), flops=big)
    parts, t_keep, t_send = lax.optimization_barrier((parts, t_keep, t_send))
    keep, send = call(scatter_kernel, (me, *parts, up_own, index), [half(CHIPS * 8, OWN)] * 2)
    t_cols = temporal_pairs(me, t_keep, t_send)
    arrived = over_chips(keep, send)
    arrived, t_cols = lax.optimization_barrier((arrived, t_cols))
    grad_hidden = call(collect_kernel, (me, arrived), [half(OWN, tokens)])[0]
    ups = gathered(grad_hidden)
    t_cols = over_column(t_cols)
    ups, t_cols = lax.optimization_barrier((ups, t_cols))
    blocks = [half(OWN, tokens)] * TP
    *parts, normed, up, grads = call(
        spatial_back_kernel,
        (me, *ups, x, qkv, mix, turned),
        blocks + saved(tokens),
        [pltpu.VMEM((TP, OWN, tokens), BF)] * 2 + copies,
        whole=(8,),
        limit=50,
        flops=big,
    )
    s_keep, s_send = call(weight_kernel, (me, normed, up, grads), lines, room(tokens), flops=big)
    parts = exchanged(parts)
    weight_grads = reduce_weights(me, s_keep, s_send, t_cols, scale)
    frame_grads = call(finish_kernel, (*parts, grad_hidden), [half(SLOTS, OWN, PAGE)], smem=0)[0]
    return jnp.transpose(frame_grads, (0, 2, 1)), weight_grads


def solution(mesh):
    fine = Mesh(mesh.devices.reshape(NZ, NY, NC, TP), ("z", "y", "c", "x"))
    seq = ("z", "y", "c")
    return jax.shard_map(
        per_device,
        mesh=fine,
        in_specs=(P(seq, None, "x"), P(), P(None, None, None, "x"), P(None, seq, "x")),
        out_specs=(P(seq, None, "x"), P(seq, None, None, "x")),
        check_vma=False,
    )
```

```python
import functools
import math

import jax
import jax.numpy as jnp
from jax import lax
from jax.experimental import pallas as pl
from jax.experimental.pallas import tpu as pltpu
from jax.sharding import Mesh
from jax.sharding import PartitionSpec as P

HD = 72
TF = 16
HEADS = 4
OWN = HEADS * HD
TP = 4
D = OWN * TP
PAGE = 128
SLOTS = 3
NZ, NY, NC = 8, 4, 2
CHIPS = NZ * NY
ROWS = 36
PAD = 40
HALF = 640
EPS = 1e-06
SCALE = HD**-0.5
F32 = jnp.float32
BF = jnp.bfloat16


def nn(a, b):
    return lax.dot_general(a, b, (((1,), (0,)), ((), ())), preferred_element_type=F32)


def nt(a, b):
    return lax.dot_general(a, b, (((1,), (1,)), ((), ())), preferred_element_type=F32)


def tn(a, b):
    return lax.dot_general(a, b, (((0,), (0,)), ((), ())), preferred_element_type=F32)


def iota(shape, dim):
    return lax.broadcasted_iota(jnp.int32, shape, dim)


def call(body, ins, outs, scratch=(), smem=1, flops=1_000_000, limit=16):
    in_specs = [
        pl.BlockSpec(memory_space=pltpu.SMEM) if i < smem else pl.BlockSpec(memory_space=pltpu.VMEM)
        for i in range(len(ins))
    ]
    size = sum(math.prod(o.shape) * o.dtype.itemsize for o in outs)
    size += sum(math.prod(i.shape) * i.dtype.itemsize for i in ins)
    out_specs = [pl.BlockSpec(memory_space=pltpu.VMEM) for _ in outs]
    return pl.pallas_call(
        body,
        out_shape=list(outs),
        in_specs=in_specs,
        out_specs=out_specs,
        scratch_shapes=list(scratch),
        compiler_params=pltpu.CompilerParams(vmem_limit_bytes=limit * 2**20),
        cost_estimate=pl.CostEstimate(flops=flops, bytes_accessed=size, transcendentals=0),
    )(*ins)


def half(*shape):
    return jax.ShapeDtypeStruct(shape, BF)


def full(*shape):
    return jax.ShapeDtypeStruct(shape, F32)


def normalise(x):
    center = x - jnp.sum(x, axis=0, keepdims=True) * (1.0 / D)
    inverse = lax.rsqrt(jnp.sum(center * center, axis=0, keepdims=True) * (1.0 / D) + EPS)
    return center * inverse, inverse


def normalise_back(normed, inverse, up):
    mean = jnp.sum(up, axis=0, keepdims=True) * (1.0 / D)
    along = jnp.sum(up * normed, axis=0, keepdims=True) * (1.0 / D)
    return inverse * (up - mean - normed * along)


def unit(rows):
    inverse = lax.rsqrt(jnp.sum(rows * rows, axis=0, keepdims=True) * (1.0 / HD) + EPS)
    return inverse, (rows * inverse).astype(BF)


def unit_back(rows, inverse, up):
    along = jnp.sum(up * rows, axis=0, keepdims=True) * (1.0 / HD)
    return inverse * up - rows * (inverse * inverse * inverse * along)


def head_parts(qkv, h):
    q = qkv[h * HD : (h + 1) * HD]
    k = qkv[OWN + h * HD : OWN + (h + 1) * HD]
    v = qkv[2 * OWN + h * HD : 2 * OWN + (h + 1) * HD]
    q_inv, q_unit = unit(q)
    k_inv, k_unit = unit(k)
    return q, k, q_inv, q_unit, k_inv, k_unit, v.astype(BF)


def weights_of(k_unit, q_unit, mask):
    raised = jnp.exp(tn(k_unit, q_unit) * SCALE)
    if mask is not None:
        raised = jnp.where(mask, raised, 0.0)
    return raised * (1.0 / jnp.sum(raised, axis=0, keepdims=True))


def mixture_of(qkv, tokens, mask):
    heads = []
    for h in range(HEADS):
        _, _, _, q_unit, _, k_unit, v = head_parts(qkv, h)
        blocks = []
        for b in range(tokens // PAGE):
            at = slice(b * PAGE, (b + 1) * PAGE)
            probs = weights_of(k_unit[:, at], q_unit[:, at], mask)
            blocks.append(nn(v[:, at], probs.astype(BF)))
        heads.append(jnp.concatenate(blocks, axis=1))
    return jnp.concatenate(heads, axis=0).astype(BF)


def attend_back(qkv, grad_mix, tokens, mask, given=None):
    queries, keys, values, mixes = [], [], [], []
    for h in range(HEADS):
        q, k, q_inv, q_unit, k_inv, k_unit, v = head_parts(qkv, h)
        gm = grad_mix[h * HD : (h + 1) * HD].astype(BF)
        with_mixture = given is None
        q_slope, k_slope, v_grad, mix = [], [], [], []
        for b in range(tokens // PAGE):
            at = slice(b * PAGE, (b + 1) * PAGE)
            if with_mixture:
                probs = weights_of(k_unit[:, at], q_unit[:, at], mask)
            else:
                unit_at = (h * (tokens // PAGE) + b) * PAGE
                probs = given[unit_at : unit_at + PAGE]
            probs_half = probs.astype(BF)
            if with_mixture:
                mix.append(nn(v[:, at], probs_half))
            grad_probs = tn(v[:, at], gm[:, at])
            v_grad.append(nt(gm[:, at], probs_half))
            weighted = probs * grad_probs
            grad_scores = (weighted - probs * jnp.sum(weighted, axis=0, keepdims=True)).astype(BF)
            q_slope.append(nn(k_unit[:, at], grad_scores) * SCALE)
            k_slope.append(nt(q_unit[:, at], grad_scores) * SCALE)
        queries.append(unit_back(q, q_inv, jnp.concatenate(q_slope, axis=1)))
        keys.append(unit_back(k, k_inv, jnp.concatenate(k_slope, axis=1)))
        values.append(jnp.concatenate(v_grad, axis=1))
        if with_mixture:
            mixes.append(jnp.concatenate(mix, axis=1))
    join = lambda parts: jnp.concatenate(parts, axis=0).astype(BF)
    return join(queries), join(keys), join(values), join(mixes) if given is None else None


def rows_of(w_ref, layer):
    return w_ref[layer, :3].reshape(3 * OWN, D)


def assemble(own, chunks, held):
    for k, chunk in enumerate(chunks):
        at = (own + TP - k) & (TP - 1)
        if len(chunk.shape) == 3:
            for n in range(chunk.shape[0]):
                held[at, :, n * PAGE : (n + 1) * PAGE] = chunk[n]
        else:
            held[at] = chunk[...]
    return held[...].reshape(D, held.shape[2])


def deal(own, value, held, outs):
    held[...] = value.astype(BF).reshape(held.shape)
    for k, out in enumerate(outs):
        out[...] = held[(own + k) & (TP - 1)]


def pages(ref):
    return jnp.concatenate([ref[n] for n in range(ref.shape[0])], axis=1)


def stage_kernel(counts, a_ref, b_ref, w_ref, a_out, b_out, index_out):
    a_out[...] = a_ref[...]
    b_out[...] = b_ref[...]
    frame = iota(index_out.shape, 1) & (PAGE - 1)
    index = jnp.zeros(index_out.shape, jnp.int32)
    start = jnp.int32(0)
    for s in range(counts.shape[0]):
        index = jnp.where(frame >= start, frame + (s * SLOTS - start), index)
        start = start + counts[s]
    index_out[...] = index


def join_kernel(a_ref, b_ref, out_ref):
    out_ref[:, :8] = a_ref[...].reshape(CHIPS, 8, OWN)
    out_ref[:, 8:] = b_ref[...].reshape(CHIPS, 8, OWN)


def spatial_kernel(me, c0, c1, c2, c3, w_ref, p0, p1, p2, p3, x_out, mix_out, held, dealt):
    x = assemble(me[0], (c0, c1, c2, c3), held)
    x_out[...] = x
    normed, _ = normalise(x.astype(F32))
    qkv = nn(rows_of(w_ref, 0), normed.astype(BF))
    mix = mixture_of(qkv, x.shape[1], None)
    mix_out[...] = mix
    deal(me[0], tn(w_ref[0, 3], mix), dealt, (p0, p1, p2, p3))


def upstream_kernel(me, g0, g1, g2, g3, w_ref, up_out, mix_out, held):
    up = assemble(me[0], (g0, g1, g2, g3), held)
    up_out[...] = up
    mix_out[...] = nn(w_ref[1, 3], up).astype(BF).astype(F32)


def temporal_kernel(
    me, h0, h1, h2, h3, grad_mix, w_ref, p0, p1, p2, p3, normed_out, grads_out, held, dealt
):
    x = assemble(me[0], (h0, h1, h2, h3), held)
    normed, inverse = normalise(x.astype(F32))
    normed_half = normed.astype(BF)
    normed_out[...] = normed_half
    qkv = nn(rows_of(w_ref, 1), normed_half)
    mask = (iota((PAGE, PAGE), 0) >> 4) == (iota((PAGE, PAGE), 1) >> 4)
    gq, gk, gv, mix = attend_back(qkv, grad_mix, x.shape[1], mask)
    for m, part in enumerate((gq, gk, gv, mix)):
        grads_out[m * OWN : (m + 1) * OWN] = part
    grad_normed = tn(rows_of(w_ref, 1), jnp.concatenate([gq, gk, gv], axis=0))
    deal(me[0], normalise_back(normed, inverse, grad_normed), dealt, (p0, p1, p2, p3))


def ready_kernel(x_ref, w_ref, qkv_out, lines_out, probs_out, wide, held):
    normed, _ = normalise(x_ref[...].astype(F32))
    normed = normed.astype(BF)
    wide[...] = normed.astype(F32)
    lines_out[...] = regroup(wide, held)
    qkv = nn(rows_of(w_ref, 0), normed)
    qkv_out[...] = qkv
    tokens = x_ref.shape[1]
    for h in range(HEADS):
        _, _, _, q_unit, _, k_unit, _ = head_parts(qkv, h)
        for b in range(tokens // PAGE):
            at = slice(b * PAGE, (b + 1) * PAGE)
            unit_at = (h * (tokens // PAGE) + b) * PAGE
            probs_out[unit_at : unit_at + PAGE] = weights_of(k_unit[:, at], q_unit[:, at], None)


def spatial_back_kernel(
    me, g0, g1, g2, g3, qkv_ref, probs_ref, mix_ref, lines_ref, w_ref,
    keep, send, grads_out, held_g, wide, held,
):
    up = assemble(me[0], (g0, g1, g2, g3), held_g)
    wide[...] = up.astype(F32)
    grad_mix = nn(w_ref[0, 3], up)
    gq, gk, gv, _ = attend_back(qkv_ref, grad_mix, up.shape[1], None, probs_ref)
    grads = jnp.concatenate([gq, gk, gv], axis=0)
    grads_out[...] = grads
    weight_products(me[3], lines_ref[...], regroup(wide, held), grads, mix_ref[...], keep, send)


def spatial_input_kernel(me, x_ref, grads, w_ref, p0, p1, p2, p3, dealt):
    normed, inverse = normalise(x_ref[...].astype(F32))
    grad_normed = tn(rows_of(w_ref, 0), grads[...])
    deal(me[0], normalise_back(normed, inverse, grad_normed), dealt, (p0, p1, p2, p3))


def regroup(ref, held):
    for y in range(NY):
        for z in range(NZ):
            at = (y * NZ + z) * ROWS
            held[at : at + ROWS] = ref[z * NY * ROWS + y * ROWS : z * NY * ROWS + (y + 1) * ROWS]
    return held[...].astype(BF)


def weight_products(core, lines, up_lines, grads, mix, keep, send):
    zeros = lambda n: jnp.zeros((n, mix.shape[1]), BF)
    first = nt(lines, jnp.concatenate([grads[: 2 * OWN], zeros(HALF - 2 * OWN)], axis=0)).astype(BF)
    low = nt(lines, jnp.concatenate([grads[2 * OWN :], zeros(96)], axis=0))
    low = low + nt(up_lines, jnp.concatenate([zeros(OWN), mix[:96]], axis=0))
    high = nt(up_lines, jnp.concatenate([mix[96:], zeros(64)], axis=0))

    @pl.when(core == 0)
    def _():
        keep[...] = first
        send[:, :384] = low.astype(BF)
        send[:, 384:] = high.astype(BF)

    @pl.when(core == 1)
    def _():
        send[...] = first
        keep[:, :384] = low.astype(BF)
        keep[:, 384:] = high.astype(BF)


def weight_kernel(me, normed_ref, up_ref, grads_ref, keep, send, wide, held):
    wide[...] = normed_ref[...].astype(F32)
    lines = regroup(wide, held)
    wide[...] = up_ref[...].astype(F32)
    up_lines = regroup(wide, held)
    weight_products(me[3], lines, up_lines, grads_ref[: 3 * OWN], grads_ref[3 * OWN :], keep, send)


def total_of(ref):
    total = ref[0].astype(F32)
    for n in range(1, ref.shape[0]):
        total = total + ref[n].astype(F32)
    return total


def pair_kernel(me, keep, got, *outs):
    span = NZ * ROWS
    for k, out in enumerate(outs):
        rows = pl.ds(pl.multiple_of(((me[1] + k) & (NY - 1)) * span, 16), span)
        out[...] = (keep[rows].astype(F32) + got[rows].astype(F32)).astype(BF)


def column_kernel(a, b, c, d, *more):
    total = a[...].astype(F32) + b[...].astype(F32) + c[...].astype(F32) + d[...].astype(F32)
    out = more[-1]
    for z in range(NZ):
        lines = total[z * ROWS : (z + 1) * ROWS]
        lines = jnp.concatenate([lines, jnp.zeros((PAD - ROWS, HALF), F32)], axis=0).astype(BF)
        if len(more) == 2:
            lines = jnp.concatenate([lines, more[0][z]], axis=1)
        out[z] = lines


def last_kernel(scale, me, parts, keep, send):
    first = me[3] == 0
    total = total_of(parts) * scale
    upper, lower = total[: ROWS // 2], total[ROWS // 2 : ROWS]
    keep[...] = jnp.where(first, upper, lower)
    send[...] = jnp.where(first, lower, upper)


def order_kernel(me, mine, other, out_ref):
    first = me[3] == 0
    for layer in range(2):
        a = mine[:, layer * HALF : (layer + 1) * HALF]
        b = other[:, layer * HALF : (layer + 1) * HALF]
        for n, part in enumerate((jnp.where(first, a, b), jnp.where(first, b, a))):
            for m in range(2):
                out_ref[layer, 2 * n + m] = part[:, m * OWN : (m + 1) * OWN]


def spread_kernel(me, a, b, c, d, own, keep, send):
    total = a[...].astype(F32) + b[...].astype(F32) + c[...].astype(F32) + d[...].astype(F32)
    hidden = (pages(own).astype(F32) + total).astype(BF)
    rows, tokens = CHIPS * 8, SLOTS * PAGE
    row, col = iota((rows, tokens), 0), iota((rows, tokens), 1)
    part, chip = row & 7, row >> 3
    base = (part >> 1) * PAGE + 4 * chip + (part & 1)
    for out, core in ((keep, me[3]), (send, 1 - me[3])):
        pick = jnp.logical_and(part < 6, col == base + 2 * core)
        out[...] = nt(pick.astype(BF), hidden).astype(BF)


def pick_kernel(me, arrived, index_ref, out_ref):
    rows, tokens = CHIPS * 16, 2 * PAGE
    row, col = iota((rows, tokens), 0), iota((rows, tokens), 1)
    part, chip, rel = row & 7, row >> 4, (row >> 3) & 1
    core = jnp.where(rel == 0, me[3], 1 - me[3])
    slot = (2 * chip + core) * SLOTS + (part >> 1)
    pick = jnp.logical_and(part < 6, (part & 1) == (col >> 7))
    pick = jnp.logical_and(pick, slot == index_ref[0:1])
    out_ref[...] = tn(arrived[...], pick.astype(BF)).astype(BF)


def scatter_kernel(me, a, b, c, d, own, index_ref, keep, send):
    total = a[...].astype(F32) + b[...].astype(F32) + c[...].astype(F32) + d[...].astype(F32)
    grad = (pages(own).astype(F32) + total).astype(BF)
    rows, tokens = CHIPS * 8, 2 * PAGE
    row, col = iota((rows, tokens), 0), iota((rows, tokens), 1)
    part, chip = row & 7, row >> 3
    live = jnp.logical_and(part < 6, (part & 1) == (col >> 7))
    for out, core in ((keep, me[3]), (send, 1 - me[3])):
        slot = (2 * chip + core) * SLOTS + (part >> 1)
        pick = jnp.logical_and(live, slot == index_ref[0:1])
        out[...] = nt(pick.astype(BF), grad).astype(BF)


def collect_kernel(me, arrived, out_ref):
    rows, tokens = CHIPS * 16, SLOTS * PAGE
    row, col = iota((rows, tokens), 0), iota((rows, tokens), 1)
    part, chip, rel = row & 7, row >> 4, (row >> 3) & 1
    core = jnp.where(rel == 0, me[3], 1 - me[3])
    position = 4 * chip + 2 * core + (part & 1)
    pick = jnp.logical_and(part < 6, col == (part >> 1) * PAGE + position)
    out_ref[...] = tn(arrived[...], pick.astype(BF)).astype(BF)


def finish_kernel(a, b, c, d, own, out_ref):
    total = a[...].astype(F32) + b[...].astype(F32) + c[...].astype(F32) + d[...].astype(F32)
    grad = (own[...].astype(F32) + total).astype(BF)
    for n in range(SLOTS):
        out_ref[n] = grad[:, n * PAGE : (n + 1) * PAGE]


def shift(value, axis, size, by):
    return lax.ppermute(value, axis, [(i, (i + by) % size) for i in range(size)])


def gathered(value):
    return (value,) + tuple(shift(value, "x", TP, k) for k in range(1, TP))


def exchanged(parts):
    return (parts[0],) + tuple(shift(parts[k], "x", TP, k) for k in range(1, TP))


def over_chips(keep, send):
    got = shift(send, "c", NC, 1)
    rows = call(join_kernel, (keep, got), [half(CHIPS, 16, OWN)], smem=0)[0]
    arrived = lax.all_to_all(rows, ("z", "y"), 0, 0)
    return arrived.reshape(CHIPS * 16, OWN)


def paired(me, keep, got):
    return call(pair_kernel, (me, keep, got), [half(NZ * ROWS, HALF)] * NY)


def over_column(cols):
    return [cols[0]] + [shift(cols[k], "y", NY, k) for k in range(1, NY)]


def column_sum(cols, more=()):
    return call(column_kernel, (*cols, *more), [half(NZ, PAD, HALF * (1 + len(more)))], smem=0)[0]


def over_rows(total):
    return lax.all_to_all(total, "z", 0, 0)


def finish_weights(me, parts, scale):
    out = [full(ROWS // 2, 2 * HALF)] * 2
    mine, other = call(functools.partial(last_kernel, scale), (me, parts), out)
    other = shift(other, "c", NC, 1)
    ordered = call(order_kernel, (me, mine, other), [full(2, 4, ROWS // 2, OWN)])[0]
    return jnp.transpose(ordered, (2, 0, 1, 3))


def per_device(frames, frame_counts, weights, grad_out):
    me = jnp.stack([lax.axis_index(a) for a in ("x", "y", "z", "c")]).astype(jnp.int32)
    scale = 1.0 / math.sqrt(grad_out.shape[0] * PAGE)
    tokens, t_tokens = SLOTS * PAGE, 2 * PAGE
    own = jnp.transpose(frames, (0, 2, 1))
    up_own = jnp.transpose(grad_out, (1, 2, 0))
    turned = jnp.swapaxes(weights, 2, 3)
    held = lambda n: pltpu.VMEM((TP, OWN, n), BF)
    room = lambda n: [pltpu.VMEM((D, n), F32), pltpu.VMEM((D, n), F32)]
    lines = [half(D, HALF)] * 2
    big = 2 * tokens * D * 4 * OWN

    chunks = gathered(own)
    places = jax.ShapeDtypeStruct((8, t_tokens), jnp.int32)
    own, up_own, index = call(
        stage_kernel, (frame_counts, own, up_own, turned), [half(*own.shape), half(*up_own.shape), places]
    )
    *parts, x, mix = call(
        spatial_kernel,
        (me, own, *chunks[1:], turned),
        [half(OWN, tokens)] * TP + [half(D, tokens), half(OWN, tokens)],
        [held(tokens), held(tokens)],
        flops=big,
    )
    parts = exchanged(parts)
    keep, send = call(spread_kernel, (me, *parts, own), [half(CHIPS * 8, OWN)] * 2)
    keep, up_own = lax.optimization_barrier((keep, up_own))
    ups = gathered(up_own)
    arrived = over_chips(keep, send)
    rows = call(pick_kernel, (me, arrived, index), [half(OWN, t_tokens)])[0]
    hidden = gathered(rows)
    up, grad_mix = call(
        upstream_kernel,
        (me, *ups, turned),
        [half(D, t_tokens), full(OWN, t_tokens)],
        [held(t_tokens)],
        flops=big // 4,
    )
    *parts, normed, grads = call(
        temporal_kernel,
        (me, *hidden, grad_mix, turned),
        [half(OWN, t_tokens)] * TP + [half(D, t_tokens)] * 2,
        [held(t_tokens), held(t_tokens)],
        flops=big,
    )
    parts = exchanged(parts)
    t_keep, t_send = call(weight_kernel, (me, normed, up, grads), lines, room(t_tokens), flops=big)
    parts, t_keep, t_send = lax.optimization_barrier((parts, t_keep, t_send))
    keep, send = call(scatter_kernel, (me, *parts, up_own, index), [half(CHIPS * 8, OWN)] * 2)
    t_cols = over_column(paired(me, t_keep, shift(t_send, "c", NC, 1)))
    arrived = over_chips(keep, send)
    grad_hidden = call(collect_kernel, (me, arrived), [half(OWN, tokens)])[0]
    ups = gathered(grad_hidden)
    qkv, rows, probs = call(
        ready_kernel,
        (x, turned),
        [full(3 * OWN, tokens), half(D, tokens), full(HEADS * tokens, PAGE)],
        room(tokens),
        smem=0,
        flops=big,
    )
    t_column = column_sum(t_cols)
    ups, t_column, rows = lax.optimization_barrier((ups, t_column, rows))
    keep, send, grads = call(
        spatial_back_kernel,
        (me, *ups, qkv, probs, mix, rows, turned),
        lines + [half(3 * OWN, tokens)],
        [held(tokens), *room(tokens)],
        flops=big,
    )
    got = shift(send, "c", NC, 1)
    parts = call(
        spatial_input_kernel,
        (me, x, grads, turned),
        [half(OWN, tokens)] * TP,
        [held(tokens)],
        flops=big,
    )
    got, parts = lax.optimization_barrier((got, parts))
    cols = over_column(paired(me, keep, got))
    parts = exchanged(parts)
    weight_grads = finish_weights(me, over_rows(column_sum(cols, (t_column,))), scale)
    frame_grads = call(finish_kernel, (*parts, grad_hidden), [half(SLOTS, OWN, PAGE)], smem=0)[0]
    return jnp.transpose(frame_grads, (0, 2, 1)), weight_grads


def solution(mesh):
    fine = Mesh(mesh.devices.reshape(NZ, NY, NC, TP), ("z", "y", "c", "x"))
    seq = ("z", "y", "c")
    return jax.shard_map(
        per_device,
        mesh=fine,
        in_specs=(P(seq, None, "x"), P(), P(None, None, None, "x"), P(None, seq, "x")),
        out_specs=(P(seq, None, "x"), P(seq, None, None, "x")),
        check_vma=False,
    )
```

```python
import functools
import math

import jax
import jax.numpy as jnp
from jax import lax
from jax.experimental import pallas as pl
from jax.experimental.pallas import tpu as pltpu
from jax.sharding import Mesh
from jax.sharding import PartitionSpec as P

HD = 72
TF = 16
HEADS = 4
OWN = HEADS * HD
TP = 4
D = OWN * TP
PAGE = 128
SLOTS = 3
NZ, NY, NC = 8, 4, 2
CHIPS = NZ * NY
ROWS = 36
PAD = 40
HALF = 640
EPS = 1e-06
SCALE = HD**-0.5
F32 = jnp.float32
BF = jnp.bfloat16


def nn(a, b):
    return lax.dot_general(a, b, (((1,), (0,)), ((), ())), preferred_element_type=F32)


def nt(a, b):
    return lax.dot_general(a, b, (((1,), (1,)), ((), ())), preferred_element_type=F32)


def tn(a, b):
    return lax.dot_general(a, b, (((0,), (0,)), ((), ())), preferred_element_type=F32)


def iota(shape, dim):
    return lax.broadcasted_iota(jnp.int32, shape, dim)


def call(body, ins, outs, scratch=(), smem=1, flops=1_000_000, limit=16, place=pltpu.VMEM):
    in_specs = [
        pl.BlockSpec(memory_space=pltpu.SMEM) if i < smem else pl.BlockSpec(memory_space=place)
        for i in range(len(ins))
    ]
    size = sum(math.prod(o.shape) * o.dtype.itemsize for o in outs)
    size += sum(math.prod(i.shape) * i.dtype.itemsize for i in ins)
    out_specs = [pl.BlockSpec(memory_space=pltpu.VMEM) for _ in outs]
    return pl.pallas_call(
        body,
        out_shape=list(outs),
        in_specs=in_specs,
        out_specs=out_specs,
        scratch_shapes=list(scratch),
        compiler_params=pltpu.CompilerParams(vmem_limit_bytes=limit * 2**20),
        cost_estimate=pl.CostEstimate(flops=flops, bytes_accessed=size, transcendentals=0),
    )(*ins)


def half(*shape):
    return jax.ShapeDtypeStruct(shape, BF)


def full(*shape):
    return jax.ShapeDtypeStruct(shape, F32)


def normalise(x):
    center = x - jnp.sum(x, axis=0, keepdims=True) * (1.0 / D)
    inverse = lax.rsqrt(jnp.sum(center * center, axis=0, keepdims=True) * (1.0 / D) + EPS)
    return center * inverse, inverse


def normalise_back(normed, inverse, up):
    mean = jnp.sum(up, axis=0, keepdims=True) * (1.0 / D)
    along = jnp.sum(up * normed, axis=0, keepdims=True) * (1.0 / D)
    return inverse * (up - mean - normed * along)


def unit(rows):
    inverse = lax.rsqrt(jnp.sum(rows * rows, axis=0, keepdims=True) * (1.0 / HD) + EPS)
    return inverse, (rows * inverse).astype(BF)


def unit_back(rows, inverse, up):
    along = jnp.sum(up * rows, axis=0, keepdims=True) * (1.0 / HD)
    return inverse * up - rows * (inverse * inverse * inverse * along)


def head_parts(qkv, h):
    q = qkv[h * HD : (h + 1) * HD]
    k = qkv[OWN + h * HD : OWN + (h + 1) * HD]
    v = qkv[2 * OWN + h * HD : 2 * OWN + (h + 1) * HD]
    q_inv, q_unit = unit(q)
    k_inv, k_unit = unit(k)
    return q, k, q_inv, q_unit, k_inv, k_unit, v.astype(BF)


def weights_of(k_unit, q_unit, mask):
    raised = jnp.exp(tn(k_unit, q_unit) * SCALE)
    if mask is not None:
        raised = jnp.where(mask, raised, 0.0)
    return raised * (1.0 / jnp.sum(raised, axis=0, keepdims=True))


def mixture_of(qkv, tokens, mask):
    heads = []
    for h in range(HEADS):
        _, _, _, q_unit, _, k_unit, v = head_parts(qkv, h)
        blocks = []
        for b in range(tokens // PAGE):
            at = slice(b * PAGE, (b + 1) * PAGE)
            probs = weights_of(k_unit[:, at], q_unit[:, at], mask)
            blocks.append(nn(v[:, at], probs.astype(BF)))
        heads.append(jnp.concatenate(blocks, axis=1))
    return jnp.concatenate(heads, axis=0).astype(BF)


def attend_back(qkv, grad_mix, tokens, mask, given=None):
    queries, keys, values, mixes = [], [], [], []
    for h in range(HEADS):
        q, k, q_inv, q_unit, k_inv, k_unit, v = head_parts(qkv, h)
        gm = grad_mix[h * HD : (h + 1) * HD].astype(BF)
        with_mixture = given is None
        q_slope, k_slope, v_grad, mix = [], [], [], []
        for b in range(tokens // PAGE):
            at = slice(b * PAGE, (b + 1) * PAGE)
            if with_mixture:
                probs = weights_of(k_unit[:, at], q_unit[:, at], mask)
            else:
                unit_at = (h * (tokens // PAGE) + b) * PAGE
                probs = given[unit_at : unit_at + PAGE]
            probs_half = probs.astype(BF)
            if with_mixture:
                mix.append(nn(v[:, at], probs_half))
            grad_probs = tn(v[:, at], gm[:, at])
            v_grad.append(nt(gm[:, at], probs_half))
            weighted = probs * grad_probs
            grad_scores = (weighted - probs * jnp.sum(weighted, axis=0, keepdims=True)).astype(BF)
            q_slope.append(nn(k_unit[:, at], grad_scores) * SCALE)
            k_slope.append(nt(q_unit[:, at], grad_scores) * SCALE)
        queries.append(unit_back(q, q_inv, jnp.concatenate(q_slope, axis=1)))
        keys.append(unit_back(k, k_inv, jnp.concatenate(k_slope, axis=1)))
        values.append(jnp.concatenate(v_grad, axis=1))
        if with_mixture:
            mixes.append(jnp.concatenate(mix, axis=1))
    join = lambda parts: jnp.concatenate(parts, axis=0).astype(BF)
    return join(queries), join(keys), join(values), join(mixes) if given is None else None


def rows_of(w_ref, layer):
    return w_ref[layer, :3].reshape(3 * OWN, D)


def assemble(own, chunks, held):
    for k, chunk in enumerate(chunks):
        at = (own + TP - k) & (TP - 1)
        if len(chunk.shape) == 3:
            for n in range(chunk.shape[0]):
                held[at, :, n * PAGE : (n + 1) * PAGE] = chunk[n]
        else:
            held[at] = chunk[...]
    return held[...].reshape(D, held.shape[2])


def deal(own, value, held, outs):
    held[...] = value.astype(BF).reshape(held.shape)
    for k, out in enumerate(outs):
        out[...] = held[(own + k) & (TP - 1)]


def pages(ref):
    return jnp.concatenate([ref[n] for n in range(ref.shape[0])], axis=1)


def stage_kernel(counts, a_ref, b_ref, w_ref, a_out, b_out, index_out):
    a_out[...] = a_ref[...]
    b_out[...] = b_ref[...]
    frame = iota(index_out.shape, 1) & (PAGE - 1)
    index = jnp.zeros(index_out.shape, jnp.int32)
    start = jnp.int32(0)
    for s in range(counts.shape[0]):
        index = jnp.where(frame >= start, frame + (s * SLOTS - start), index)
        start = start + counts[s]
    index_out[...] = index


def join_kernel(a_ref, b_ref, out_ref):
    out_ref[:, :8] = a_ref[...].reshape(CHIPS, 8, OWN)
    out_ref[:, 8:] = b_ref[...].reshape(CHIPS, 8, OWN)


def spatial_kernel(me, c0, c1, c2, c3, w_ref, p0, p1, p2, p3, x_out, mix_out, held, dealt):
    x = assemble(me[0], (c0, c1, c2, c3), held)
    x_out[...] = x
    normed, _ = normalise(x.astype(F32))
    qkv = nn(rows_of(w_ref, 0), normed.astype(BF))
    mix = mixture_of(qkv, x.shape[1], None)
    mix_out[...] = mix
    deal(me[0], tn(w_ref[0, 3], mix), dealt, (p0, p1, p2, p3))


def upstream_kernel(me, g0, g1, g2, g3, w_ref, up_out, mix_out, held):
    up = assemble(me[0], (g0, g1, g2, g3), held)
    up_out[...] = up
    mix_out[...] = nn(w_ref[1, 3], up).astype(BF).astype(F32)


def temporal_kernel(
    me, h0, h1, h2, h3, grad_mix, w_ref, p0, p1, p2, p3, normed_out, grads_out, held, dealt
):
    x = assemble(me[0], (h0, h1, h2, h3), held)
    normed, inverse = normalise(x.astype(F32))
    normed_half = normed.astype(BF)
    normed_out[...] = normed_half
    qkv = nn(rows_of(w_ref, 1), normed_half)
    mask = (iota((PAGE, PAGE), 0) >> 4) == (iota((PAGE, PAGE), 1) >> 4)
    gq, gk, gv, mix = attend_back(qkv, grad_mix, x.shape[1], mask)
    for m, part in enumerate((gq, gk, gv, mix)):
        grads_out[m * OWN : (m + 1) * OWN] = part
    grad_normed = tn(rows_of(w_ref, 1), jnp.concatenate([gq, gk, gv], axis=0))
    deal(me[0], normalise_back(normed, inverse, grad_normed), dealt, (p0, p1, p2, p3))


def ready_kernel(x_ref, w_ref, qkv_out, lines_out, probs_out, wide, held):
    normed, _ = normalise(x_ref[...].astype(F32))
    normed = normed.astype(BF)
    wide[...] = normed.astype(F32)
    lines_out[...] = regroup(wide, held)
    qkv = nn(rows_of(w_ref, 0), normed)
    qkv_out[...] = qkv
    tokens = x_ref.shape[1]
    for h in range(HEADS):
        _, _, _, q_unit, _, k_unit, _ = head_parts(qkv, h)
        for b in range(tokens // PAGE):
            at = slice(b * PAGE, (b + 1) * PAGE)
            unit_at = (h * (tokens // PAGE) + b) * PAGE
            probs_out[unit_at : unit_at + PAGE] = weights_of(k_unit[:, at], q_unit[:, at], None)


def spatial_back_kernel(
    me, g0, g1, g2, g3, qkv_ref, probs_ref, mix_ref, lines_ref, w_ref,
    keep, send, grads_out, held_g, wide, held,
):
    up = assemble(me[0], (g0, g1, g2, g3), held_g)
    wide[...] = up.astype(F32)
    grad_mix = nn(w_ref[0, 3], up)
    gq, gk, gv, _ = attend_back(qkv_ref, grad_mix, up.shape[1], None, probs_ref)
    grads = jnp.concatenate([gq, gk, gv], axis=0)
    grads_out[...] = grads
    weight_products(me[3], lines_ref[...], regroup(wide, held), grads, mix_ref[...], keep, send)


def spatial_input_kernel(me, x_ref, grads, w_ref, p0, p1, p2, p3, dealt):
    normed, inverse = normalise(x_ref[...].astype(F32))
    grad_normed = tn(rows_of(w_ref, 0), grads[...])
    deal(me[0], normalise_back(normed, inverse, grad_normed), dealt, (p0, p1, p2, p3))


def regroup(ref, held):
    for y in range(NY):
        for z in range(NZ):
            at = (y * NZ + z) * ROWS
            held[at : at + ROWS] = ref[z * NY * ROWS + y * ROWS : z * NY * ROWS + (y + 1) * ROWS]
    return held[...].astype(BF)


def weight_products(core, lines, up_lines, grads, mix, keep, send):
    zeros = lambda n: jnp.zeros((n, mix.shape[1]), BF)
    first = nt(lines, jnp.concatenate([grads[: 2 * OWN], zeros(HALF - 2 * OWN)], axis=0)).astype(BF)
    low = nt(lines, jnp.concatenate([grads[2 * OWN :], zeros(96)], axis=0))
    low = low + nt(up_lines, jnp.concatenate([zeros(OWN), mix[:96]], axis=0))
    high = nt(up_lines, jnp.concatenate([mix[96:], zeros(64)], axis=0))

    @pl.when(core == 0)
    def _():
        keep[...] = first
        send[:, :384] = low.astype(BF)
        send[:, 384:] = high.astype(BF)

    @pl.when(core == 1)
    def _():
        send[...] = first
        keep[:, :384] = low.astype(BF)
        keep[:, 384:] = high.astype(BF)


def weight_kernel(me, normed_ref, up_ref, grads_ref, keep, send, wide, held):
    wide[...] = normed_ref[...].astype(F32)
    lines = regroup(wide, held)
    wide[...] = up_ref[...].astype(F32)
    up_lines = regroup(wide, held)
    weight_products(me[3], lines, up_lines, grads_ref[: 3 * OWN], grads_ref[3 * OWN :], keep, send)


def total_of(ref):
    total = ref[0].astype(F32)
    for n in range(1, ref.shape[0]):
        total = total + ref[n].astype(F32)
    return total


def pair_kernel(me, keep, got, *outs):
    span = NZ * ROWS
    for k, out in enumerate(outs):
        rows = pl.ds(pl.multiple_of(((me[1] + k) & (NY - 1)) * span, 16), span)
        out[...] = (keep[rows].astype(F32) + got[rows].astype(F32)).astype(BF)


def sum_kernel(keep, got, out):
    out[...] = (keep[...].astype(F32) + got[...].astype(F32)).astype(BF)


def padded(lines):
    return jnp.concatenate([lines, jnp.zeros((PAD - ROWS, HALF), F32)], axis=0)


def column_kernel(parts, out):
    total = total_of(parts)
    for z in range(NZ):
        out[z] = padded(total[z * ROWS : (z + 1) * ROWS]).astype(BF)


def mark_kernel(a, b, c, d, out):
    out[...] = jnp.zeros((16, PAGE), BF)


def parity_kernel(me, a, b, c, d, keep, send):
    total = a[...].astype(F32) + b[...].astype(F32) + c[...].astype(F32) + d[...].astype(F32)
    even = (me[2] & 1) == 0
    for i in range(NZ // 2):
        at = 2 * i * ROWS
        first = padded(total[at : at + ROWS]).astype(BF)
        second = padded(total[at + ROWS : at + 2 * ROWS]).astype(BF)
        keep[i] = jnp.where(even, first, second)
        send[i] = jnp.where(even, second, first)


def quarter_kernel(me, keep, got, o0, o1, o2, o3):
    for k, out in enumerate((o0, o1, o2, o3)):
        at = ((me[2] >> 1) + k) & 3
        out[...] = (keep[at].astype(F32) + got[at].astype(F32)).astype(BF)


def last_kernel(scale, me, spatial, mark, *refs):
    temporal, (keep, send) = refs[:4], refs[4:]
    first = me[3] == 0
    other = temporal[0][...].astype(F32)
    for part in temporal[1:]:
        other = other + part[...].astype(F32)
    for at, total in ((0, total_of(spatial)), (HALF, other)):
        total = total * scale
        upper, lower = total[: ROWS // 2], total[ROWS // 2 : ROWS]
        keep[:, at : at + HALF] = jnp.where(first, upper, lower)
        send[:, at : at + HALF] = jnp.where(first, lower, upper)


def order_kernel(me, mine, other, out_ref):
    first = me[3] == 0
    for layer in range(2):
        a = mine[:, layer * HALF : (layer + 1) * HALF]
        b = other[:, layer * HALF : (layer + 1) * HALF]
        for n, part in enumerate((jnp.where(first, a, b), jnp.where(first, b, a))):
            for m in range(2):
                out_ref[:, layer, 2 * n + m] = part[:, m * OWN : (m + 1) * OWN]


def spread_kernel(me, a, b, c, d, own, keep, send):
    total = a[...].astype(F32) + b[...].astype(F32) + c[...].astype(F32) + d[...].astype(F32)
    hidden = (pages(own).astype(F32) + total).astype(BF)
    rows, tokens = CHIPS * 8, SLOTS * PAGE
    row, col = iota((rows, tokens), 0), iota((rows, tokens), 1)
    part, chip = row & 7, row >> 3
    base = (part >> 1) * PAGE + 4 * chip + (part & 1)
    for out, core in ((keep, me[3]), (send, 1 - me[3])):
        pick = jnp.logical_and(part < 6, col == base + 2 * core)
        out[...] = nt(pick.astype(BF), hidden).astype(BF)


def pick_kernel(me, arrived, index_ref, out_ref):
    rows, tokens = CHIPS * 16, 2 * PAGE
    row, col = iota((rows, tokens), 0), iota((rows, tokens), 1)
    part, chip, rel = row & 7, row >> 4, (row >> 3) & 1
    core = jnp.where(rel == 0, me[3], 1 - me[3])
    slot = (2 * chip + core) * SLOTS + (part >> 1)
    pick = jnp.logical_and(part < 6, (part & 1) == (col >> 7))
    pick = jnp.logical_and(pick, slot == index_ref[0:1])
    out_ref[...] = tn(arrived[...], pick.astype(BF)).astype(BF)


def scatter_kernel(me, a, b, c, d, own, index_ref, keep, send):
    total = a[...].astype(F32) + b[...].astype(F32) + c[...].astype(F32) + d[...].astype(F32)
    grad = (pages(own).astype(F32) + total).astype(BF)
    rows, tokens = CHIPS * 8, 2 * PAGE
    row, col = iota((rows, tokens), 0), iota((rows, tokens), 1)
    part, chip = row & 7, row >> 3
    live = jnp.logical_and(part < 6, (part & 1) == (col >> 7))
    for out, core in ((keep, me[3]), (send, 1 - me[3])):
        slot = (2 * chip + core) * SLOTS + (part >> 1)
        pick = jnp.logical_and(live, slot == index_ref[0:1])
        out[...] = nt(pick.astype(BF), grad).astype(BF)


def collect_kernel(me, arrived, out_ref):
    rows, tokens = CHIPS * 16, SLOTS * PAGE
    row, col = iota((rows, tokens), 0), iota((rows, tokens), 1)
    part, chip, rel = row & 7, row >> 4, (row >> 3) & 1
    core = jnp.where(rel == 0, me[3], 1 - me[3])
    position = 4 * chip + 2 * core + (part & 1)
    pick = jnp.logical_and(part < 6, col == (part >> 1) * PAGE + position)
    out_ref[...] = tn(arrived[...], pick.astype(BF)).astype(BF)


def finish_kernel(a, b, c, d, own, out_ref):
    total = a[...].astype(F32) + b[...].astype(F32) + c[...].astype(F32) + d[...].astype(F32)
    grad = (own[...].astype(F32) + total).astype(BF)
    for n in range(SLOTS):
        out_ref[n] = grad[:, n * PAGE : (n + 1) * PAGE]


def shift(value, axis, size, by):
    return lax.ppermute(value, axis, [(i, (i + by) % size) for i in range(size)])


def gathered(value):
    return (value,) + tuple(shift(value, "x", TP, k) for k in range(1, TP))


def exchanged(parts):
    return (parts[0],) + tuple(shift(parts[k], "x", TP, k) for k in range(1, TP))


def over_chips(keep, send):
    got = shift(send, "c", NC, 1)
    rows = call(join_kernel, (keep, got), [half(CHIPS, 16, OWN)], smem=0)[0]
    arrived = lax.all_to_all(rows, ("z", "y"), 0, 0)
    return arrived.reshape(CHIPS * 16, OWN)


def paired(me, keep, got):
    return call(pair_kernel, (me, keep, got), [half(NZ * ROWS, HALF)] * NY)


def over_column(cols):
    return [cols[0]] + [shift(cols[k], "y", NY, k) for k in range(1, NY)]


def over_rows(total):
    return lax.all_to_all(total, "z", 0, 0)


def finish_weights(me, spatial, temporal, mark, scale):
    out = [full(ROWS // 2, 2 * HALF)] * 2
    mine, other = call(functools.partial(last_kernel, scale), (me, spatial, mark, *temporal), out)
    other = shift(other, "c", NC, 1)
    return call(order_kernel, (me, mine, other), [full(ROWS // 2, 2, 4, OWN)])[0]


def per_device(frames, frame_counts, weights, grad_out):
    me = jnp.stack([lax.axis_index(a) for a in ("x", "y", "z", "c")]).astype(jnp.int32)
    scale = 1.0 / math.sqrt(grad_out.shape[0] * PAGE)
    tokens, t_tokens = SLOTS * PAGE, 2 * PAGE
    own = jnp.transpose(frames, (0, 2, 1))
    up_own = jnp.transpose(grad_out, (1, 2, 0))
    turned = jnp.swapaxes(weights, 2, 3)
    held = lambda n: pltpu.VMEM((TP, OWN, n), BF)
    room = lambda n: [pltpu.VMEM((D, n), F32), pltpu.VMEM((D, n), F32)]
    lines = [half(D, HALF)] * 2
    big = 2 * tokens * D * 4 * OWN

    chunks = gathered(own)
    places = jax.ShapeDtypeStruct((8, t_tokens), jnp.int32)
    own, up_own, index = call(
        stage_kernel, (frame_counts, own, up_own, turned), [half(*own.shape), half(*up_own.shape), places]
    )
    *parts, x, mix = call(
        spatial_kernel,
        (me, own, *chunks[1:], turned),
        [half(OWN, tokens)] * TP + [half(D, tokens), half(OWN, tokens)],
        [held(tokens), held(tokens)],
        flops=big,
    )
    parts = exchanged(parts)
    keep, send = call(spread_kernel, (me, *parts, own), [half(CHIPS * 8, OWN)] * 2)
    keep, up_own = lax.optimization_barrier((keep, up_own))
    ups = gathered(up_own)
    arrived = over_chips(keep, send)
    rows = call(pick_kernel, (me, arrived, index), [half(OWN, t_tokens)])[0]
    hidden = gathered(rows)
    up, grad_mix = call(
        upstream_kernel,
        (me, *ups, turned),
        [half(D, t_tokens), full(OWN, t_tokens)],
        [held(t_tokens)],
        flops=big // 4,
    )
    *parts, normed, grads = call(
        temporal_kernel,
        (me, *hidden, grad_mix, turned),
        [half(OWN, t_tokens)] * TP + [half(D, t_tokens)] * 2,
        [held(t_tokens), held(t_tokens)],
        flops=big,
    )
    parts = exchanged(parts)
    t_keep, t_send = call(weight_kernel, (me, normed, up, grads), lines, room(t_tokens), flops=big)
    parts, t_keep, t_send = lax.optimization_barrier((parts, t_keep, t_send))
    keep, send = call(scatter_kernel, (me, *parts, up_own, index), [half(CHIPS * 8, OWN)] * 2)
    t_cols = over_column(paired(me, t_keep, shift(t_send, "c", NC, 1)))
    arrived = over_chips(keep, send)
    grad_hidden = call(collect_kernel, (me, arrived), [half(OWN, tokens)])[0]
    ups = gathered(grad_hidden)
    qkv, rows, probs = call(
        ready_kernel,
        (x, turned),
        [full(3 * OWN, tokens), half(D, tokens), full(HEADS * tokens, PAGE)],
        room(tokens),
        smem=0,
        flops=big,
    )
    mark = call(mark_kernel, t_cols, [half(16, PAGE)], smem=0, place=pl.ANY)[0]
    ups, mark, rows = lax.optimization_barrier((ups, mark, rows))
    keep, send, grads = call(
        spatial_back_kernel,
        (me, *ups, qkv, probs, mix, rows, turned),
        lines + [half(3 * OWN, tokens)],
        [held(tokens), *room(tokens)],
        flops=big,
    )
    got = shift(send, "c", NC, 1)
    parts = call(
        spatial_input_kernel,
        (me, x, grads, turned),
        [half(OWN, tokens)] * TP,
        [held(tokens)],
        flops=big,
    )
    got, parts = lax.optimization_barrier((got, parts))
    sums = call(sum_kernel, (keep, got), [half(D, HALF)], smem=0)[0]
    t_cols, sums = lax.optimization_barrier((t_cols, sums))
    t_parts = [half(NZ // 2, PAD, HALF)] * 2
    t_keep, t_send = call(parity_kernel, (me, *t_cols), t_parts)
    t_got = lax.ppermute(t_send, "z", [(z, z ^ 1) for z in range(NZ)])
    t_parts = call(quarter_kernel, (me, t_keep, t_got), [half(PAD, HALF)] * 4)
    t_parts = [t_parts[0]] + [shift(t_parts[k], "z", NZ, 2 * k) for k in range(1, 4)]
    cols = lax.all_to_all(sums.reshape(NY, NZ * ROWS, HALF), "y", 0, 0)
    parts = exchanged(parts)
    cols, t_parts, parts = lax.optimization_barrier((cols, t_parts, parts))
    column = call(column_kernel, (cols,), [half(NZ, PAD, HALF)], smem=0)[0]
    moved = over_rows(column)
    frame_grads = call(finish_kernel, (*parts, grad_hidden), [half(SLOTS, OWN, PAGE)], smem=0)[0]
    moved, frame_grads = lax.optimization_barrier((moved, frame_grads))
    weight_grads = finish_weights(me, moved, t_parts, mark, scale)
    return jnp.transpose(frame_grads, (0, 2, 1)), weight_grads


def solution(mesh):
    fine = Mesh(mesh.devices.reshape(NZ, NY, NC, TP), ("z", "y", "c", "x"))
    seq = ("z", "y", "c")
    return jax.shard_map(
        per_device,
        mesh=fine,
        in_specs=(P(seq, None, "x"), P(), P(None, None, None, "x"), P(None, seq, "x")),
        out_specs=(P(seq, None, "x"), P(seq, None, None, "x")),
        check_vma=False,
    )
```

```python
import functools
import math

import jax
import jax.numpy as jnp
from jax import lax
from jax.experimental import pallas as pl
from jax.experimental.pallas import tpu as pltpu
from jax.sharding import Mesh
from jax.sharding import PartitionSpec as P

HD = 72
TF = 16
HEADS = 4
OWN = HEADS * HD
TP = 4
D = OWN * TP
PAGE = 128
SLOTS = 3
NZ, NY, NC = 8, 4, 2
CHIPS = NZ * NY
ROWS = 36
PAD = 40
HALF = 640
EPS = 1e-06
SCALE = HD**-0.5
F32 = jnp.float32
BF = jnp.bfloat16


def nn(a, b):
    return lax.dot_general(a, b, (((1,), (0,)), ((), ())), preferred_element_type=F32)


def nt(a, b):
    return lax.dot_general(a, b, (((1,), (1,)), ((), ())), preferred_element_type=F32)


def tn(a, b):
    return lax.dot_general(a, b, (((0,), (0,)), ((), ())), preferred_element_type=F32)


def iota(shape, dim):
    return lax.broadcasted_iota(jnp.int32, shape, dim)


class Place:
    def __getitem__(self, at):
        return lax.axis_index("xyzc"[at])


def call(body, ins, outs, scratch=(), smem=1, flops=1_000_000, limit=16, place=pltpu.VMEM):
    if isinstance(ins[0], Place):
        body, ins, smem = functools.partial(body, ins[0]), ins[1:], 0
    in_specs = [
        pl.BlockSpec(memory_space=pltpu.SMEM) if i < smem else pl.BlockSpec(memory_space=place)
        for i in range(len(ins))
    ]
    size = sum(math.prod(o.shape) * o.dtype.itemsize for o in outs)
    size += sum(math.prod(i.shape) * i.dtype.itemsize for i in ins)
    out_specs = [pl.BlockSpec(memory_space=pltpu.VMEM) for _ in outs]
    return pl.pallas_call(
        body,
        out_shape=list(outs),
        in_specs=in_specs,
        out_specs=out_specs,
        scratch_shapes=list(scratch),
        compiler_params=pltpu.CompilerParams(vmem_limit_bytes=limit * 2**20),
        cost_estimate=pl.CostEstimate(flops=flops, bytes_accessed=size, transcendentals=0),
    )(*ins)


def half(*shape):
    return jax.ShapeDtypeStruct(shape, BF)


def full(*shape):
    return jax.ShapeDtypeStruct(shape, F32)


def normalise(x):
    center = x - jnp.sum(x, axis=0, keepdims=True) * (1.0 / D)
    inverse = lax.rsqrt(jnp.sum(center * center, axis=0, keepdims=True) * (1.0 / D) + EPS)
    return center * inverse, inverse


def normalise_back(normed, inverse, up):
    mean = jnp.sum(up, axis=0, keepdims=True) * (1.0 / D)
    along = jnp.sum(up * normed, axis=0, keepdims=True) * (1.0 / D)
    return inverse * (up - mean - normed * along)


def unit(rows):
    inverse = lax.rsqrt(jnp.sum(rows * rows, axis=0, keepdims=True) * (1.0 / HD) + EPS)
    return inverse, (rows * inverse).astype(BF)


def unit_back(rows, inverse, up):
    along = jnp.sum(up * rows, axis=0, keepdims=True) * (1.0 / HD)
    return inverse * up - rows * (inverse * inverse * inverse * along)


def head_parts(qkv, h):
    q = qkv[h * HD : (h + 1) * HD]
    k = qkv[OWN + h * HD : OWN + (h + 1) * HD]
    v = qkv[2 * OWN + h * HD : 2 * OWN + (h + 1) * HD]
    q_inv, q_unit = unit(q)
    k_inv, k_unit = unit(k)
    return q, k, q_inv, q_unit, k_inv, k_unit, v.astype(BF)


def weights_of(k_unit, q_unit, mask):
    raised = jnp.exp(tn(k_unit, q_unit) * SCALE)
    if mask is not None:
        raised = jnp.where(mask, raised, 0.0)
    return raised * (1.0 / jnp.sum(raised, axis=0, keepdims=True))


def mixture_of(qkv, tokens, mask):
    heads = []
    for h in range(HEADS):
        _, _, _, q_unit, _, k_unit, v = head_parts(qkv, h)
        blocks = []
        for b in range(tokens // PAGE):
            at = slice(b * PAGE, (b + 1) * PAGE)
            probs = weights_of(k_unit[:, at], q_unit[:, at], mask)
            blocks.append(nn(v[:, at], probs.astype(BF)))
        heads.append(jnp.concatenate(blocks, axis=1))
    return jnp.concatenate(heads, axis=0).astype(BF)


def attend_back(qkv, grad_mix, tokens, mask, given=None):
    queries, keys, values, mixes = [], [], [], []
    for h in range(HEADS):
        q, k, q_inv, q_unit, k_inv, k_unit, v = head_parts(qkv, h)
        gm = grad_mix[h * HD : (h + 1) * HD].astype(BF)
        with_mixture = given is None
        q_slope, k_slope, v_grad, mix = [], [], [], []
        for b in range(tokens // PAGE):
            at = slice(b * PAGE, (b + 1) * PAGE)
            if with_mixture:
                probs = weights_of(k_unit[:, at], q_unit[:, at], mask)
            else:
                unit_at = (h * (tokens // PAGE) + b) * PAGE
                probs = given[unit_at : unit_at + PAGE]
            probs_half = probs.astype(BF)
            if with_mixture:
                mix.append(nn(v[:, at], probs_half))
            grad_probs = tn(v[:, at], gm[:, at])
            v_grad.append(nt(gm[:, at], probs_half))
            weighted = probs * grad_probs
            grad_scores = (weighted - probs * jnp.sum(weighted, axis=0, keepdims=True)).astype(BF)
            q_slope.append(nn(k_unit[:, at], grad_scores) * SCALE)
            k_slope.append(nt(q_unit[:, at], grad_scores) * SCALE)
        queries.append(unit_back(q, q_inv, jnp.concatenate(q_slope, axis=1)))
        keys.append(unit_back(k, k_inv, jnp.concatenate(k_slope, axis=1)))
        values.append(jnp.concatenate(v_grad, axis=1))
        if with_mixture:
            mixes.append(jnp.concatenate(mix, axis=1))
    join = lambda parts: jnp.concatenate(parts, axis=0).astype(BF)
    return join(queries), join(keys), join(values), join(mixes) if given is None else None


def rows_of(w_ref, layer):
    return w_ref[layer, :3].reshape(3 * OWN, D)


def assemble(own, chunks, held):
    for k, chunk in enumerate(chunks):
        at = (own + TP - k) & (TP - 1)
        if len(chunk.shape) == 3:
            for n in range(chunk.shape[0]):
                held[at, :, n * PAGE : (n + 1) * PAGE] = chunk[n]
        else:
            held[at] = chunk[...]
    return held[...].reshape(D, held.shape[2])


def deal(own, value, held, outs):
    held[...] = value.astype(BF).reshape(held.shape)
    for k, out in enumerate(outs):
        out[...] = held[(own + k) & (TP - 1)]


def pages(ref):
    return jnp.concatenate([ref[n] for n in range(ref.shape[0])], axis=1)


def stage_kernel(counts, a_ref, b_ref, w_ref, a_out, b_out, index_out):
    a_out[...] = a_ref[...]
    b_out[...] = b_ref[...]
    frame = iota(index_out.shape, 1) & (PAGE - 1)
    index = jnp.zeros(index_out.shape, jnp.int32)
    start = jnp.int32(0)
    for s in range(counts.shape[0]):
        index = jnp.where(frame >= start, frame + (s * SLOTS - start), index)
        start = start + counts[s]
    index_out[...] = index


def join_kernel(a_ref, b_ref, out_ref):
    out_ref[:, :8] = a_ref[...].reshape(CHIPS, 8, OWN)
    out_ref[:, 8:] = b_ref[...].reshape(CHIPS, 8, OWN)


def spatial_kernel(me, c0, c1, c2, c3, w_ref, p0, p1, p2, p3, x_out, mix_out, held, dealt):
    x = assemble(me[0], (c0, c1, c2, c3), held)
    x_out[...] = x
    normed, _ = normalise(x.astype(F32))
    qkv = nn(rows_of(w_ref, 0), normed.astype(BF))
    mix = mixture_of(qkv, x.shape[1], None)
    mix_out[...] = mix
    deal(me[0], tn(w_ref[0, 3], mix), dealt, (p0, p1, p2, p3))


def upstream_kernel(me, g0, g1, g2, g3, w_ref, up_out, mix_out, held):
    up = assemble(me[0], (g0, g1, g2, g3), held)
    up_out[...] = up
    mix_out[...] = nn(w_ref[1, 3], up).astype(BF).astype(F32)


def temporal_kernel(
    me, h0, h1, h2, h3, grad_mix, w_ref, p0, p1, p2, p3, normed_out, grads_out, held, dealt
):
    x = assemble(me[0], (h0, h1, h2, h3), held)
    normed, inverse = normalise(x.astype(F32))
    normed_half = normed.astype(BF)
    normed_out[...] = normed_half
    qkv = nn(rows_of(w_ref, 1), normed_half)
    mask = (iota((PAGE, PAGE), 0) >> 4) == (iota((PAGE, PAGE), 1) >> 4)
    gq, gk, gv, mix = attend_back(qkv, grad_mix, x.shape[1], mask)
    for m, part in enumerate((gq, gk, gv, mix)):
        grads_out[m * OWN : (m + 1) * OWN] = part
    grad_normed = tn(rows_of(w_ref, 1), jnp.concatenate([gq, gk, gv], axis=0))
    deal(me[0], normalise_back(normed, inverse, grad_normed), dealt, (p0, p1, p2, p3))


def ready_kernel(x_ref, w_ref, qkv_out, lines_out, probs_out, wide, held):
    normed, _ = normalise(x_ref[...].astype(F32))
    normed = normed.astype(BF)
    wide[...] = normed.astype(F32)
    lines_out[...] = regroup(wide, held)
    qkv = nn(rows_of(w_ref, 0), normed)
    qkv_out[...] = qkv
    tokens = x_ref.shape[1]
    for h in range(HEADS):
        _, _, _, q_unit, _, k_unit, _ = head_parts(qkv, h)
        for b in range(tokens // PAGE):
            at = slice(b * PAGE, (b + 1) * PAGE)
            unit_at = (h * (tokens // PAGE) + b) * PAGE
            probs_out[unit_at : unit_at + PAGE] = weights_of(k_unit[:, at], q_unit[:, at], None)


def spatial_back_kernel(
    me, g0, g1, g2, g3, qkv_ref, probs_ref, mix_ref, lines_ref, w_ref,
    keep, send, grads_out, held_g, wide, held,
):
    up = assemble(me[0], (g0, g1, g2, g3), held_g)
    wide[...] = up.astype(F32)
    grad_mix = nn(w_ref[0, 3], up)
    gq, gk, gv, _ = attend_back(qkv_ref, grad_mix, up.shape[1], None, probs_ref)
    grads = jnp.concatenate([gq, gk, gv], axis=0)
    grads_out[...] = grads
    weight_products(me[3], lines_ref[...], regroup(wide, held), grads, mix_ref[...], keep, send)


def spatial_input_kernel(me, x_ref, grads, w_ref, p0, p1, p2, p3, dealt):
    normed, inverse = normalise(x_ref[...].astype(F32))
    grad_normed = tn(rows_of(w_ref, 0), grads[...])
    deal(me[0], normalise_back(normed, inverse, grad_normed), dealt, (p0, p1, p2, p3))


def regroup(ref, held):
    for y in range(NY):
        for z in range(NZ):
            at = (y * NZ + z) * ROWS
            held[at : at + ROWS] = ref[z * NY * ROWS + y * ROWS : z * NY * ROWS + (y + 1) * ROWS]
    return held[...].astype(BF)


def weight_products(core, lines, up_lines, grads, mix, keep, send):
    zeros = lambda n: jnp.zeros((n, mix.shape[1]), BF)
    first = nt(lines, jnp.concatenate([grads[: 2 * OWN], zeros(HALF - 2 * OWN)], axis=0)).astype(BF)
    low = nt(lines, jnp.concatenate([grads[2 * OWN :], zeros(96)], axis=0))
    low = low + nt(up_lines, jnp.concatenate([zeros(OWN), mix[:96]], axis=0))
    high = nt(up_lines, jnp.concatenate([mix[96:], zeros(64)], axis=0))

    @pl.when(core == 0)
    def _():
        keep[...] = first
        send[:, :384] = low.astype(BF)
        send[:, 384:] = high.astype(BF)

    @pl.when(core == 1)
    def _():
        send[...] = first
        keep[:, :384] = low.astype(BF)
        keep[:, 384:] = high.astype(BF)


def weight_kernel(me, normed_ref, up_ref, grads_ref, keep, send, wide, held):
    wide[...] = normed_ref[...].astype(F32)
    lines = regroup(wide, held)
    wide[...] = up_ref[...].astype(F32)
    up_lines = regroup(wide, held)
    weight_products(me[3], lines, up_lines, grads_ref[: 3 * OWN], grads_ref[3 * OWN :], keep, send)


def total_of(ref):
    total = ref[0].astype(F32)
    for n in range(1, ref.shape[0]):
        total = total + ref[n].astype(F32)
    return total


def pair_kernel(me, keep, got, *outs):
    span = NZ * ROWS
    for k, out in enumerate(outs):
        rows = pl.ds(pl.multiple_of(((me[1] + k) & (NY - 1)) * span, 16), span)
        out[...] = (keep[rows].astype(F32) + got[rows].astype(F32)).astype(BF)


def sum_kernel(keep, got, out):
    out[...] = (keep[...].astype(F32) + got[...].astype(F32)).astype(BF)


def padded(lines):
    return jnp.concatenate([lines, jnp.zeros((PAD - ROWS, HALF), F32)], axis=0)


def column_kernel(parts, out):
    total = total_of(parts)
    for z in range(NZ):
        out[z] = padded(total[z * ROWS : (z + 1) * ROWS]).astype(BF)


def mark_kernel(a, b, c, d, out):
    out[...] = jnp.zeros((16, PAGE), BF)


def parity_kernel(me, a, b, c, d, keep, send):
    total = a[...].astype(F32) + b[...].astype(F32) + c[...].astype(F32) + d[...].astype(F32)
    even = (me[2] & 1) == 0
    for i in range(NZ // 2):
        at = 2 * i * ROWS
        first = padded(total[at : at + ROWS]).astype(BF)
        second = padded(total[at + ROWS : at + 2 * ROWS]).astype(BF)
        keep[i] = jnp.where(even, first, second)
        send[i] = jnp.where(even, second, first)


def quarter_kernel(me, keep, got, o0, o1, o2, o3):
    for k, out in enumerate((o0, o1, o2, o3)):
        at = ((me[2] >> 1) + k) & 3
        out[...] = (keep[at].astype(F32) + got[at].astype(F32)).astype(BF)


def last_kernel(me, spatial, mark, *refs, scale):
    temporal, (keep, send) = refs[:4], refs[4:]
    first = me[3] == 0
    other = temporal[0][...].astype(F32)
    for part in temporal[1:]:
        other = other + part[...].astype(F32)
    for at, total in ((0, total_of(spatial)), (HALF, other)):
        total = total * scale
        upper, lower = total[: ROWS // 2], total[ROWS // 2 : ROWS]
        keep[:, at : at + HALF] = jnp.where(first, upper, lower)
        send[:, at : at + HALF] = jnp.where(first, lower, upper)


def order_kernel(me, mine, other, out_ref):
    first = me[3] == 0
    for layer in range(2):
        a = mine[:, layer * HALF : (layer + 1) * HALF]
        b = other[:, layer * HALF : (layer + 1) * HALF]
        for n, part in enumerate((jnp.where(first, a, b), jnp.where(first, b, a))):
            for m in range(2):
                out_ref[:, layer, 2 * n + m] = part[:, m * OWN : (m + 1) * OWN]


def spread_kernel(me, a, b, c, d, own, keep, send):
    total = a[...].astype(F32) + b[...].astype(F32) + c[...].astype(F32) + d[...].astype(F32)
    hidden = (pages(own).astype(F32) + total).astype(BF)
    rows, tokens = CHIPS * 8, SLOTS * PAGE
    row, col = iota((rows, tokens), 0), iota((rows, tokens), 1)
    part, chip = row & 7, row >> 3
    base = (part >> 1) * PAGE + 4 * chip + (part & 1)
    for out, core in ((keep, me[3]), (send, 1 - me[3])):
        pick = jnp.logical_and(part < 6, col == base + 2 * core)
        out[...] = nt(pick.astype(BF), hidden).astype(BF)


def pick_kernel(me, arrived, index_ref, out_ref):
    rows, tokens = CHIPS * 16, 2 * PAGE
    row, col = iota((rows, tokens), 0), iota((rows, tokens), 1)
    part, chip, rel = row & 7, row >> 4, (row >> 3) & 1
    core = jnp.where(rel == 0, me[3], 1 - me[3])
    slot = (2 * chip + core) * SLOTS + (part >> 1)
    pick = jnp.logical_and(part < 6, (part & 1) == (col >> 7))
    pick = jnp.logical_and(pick, slot == index_ref[0:1])
    out_ref[...] = tn(arrived[...], pick.astype(BF)).astype(BF)


def scatter_kernel(me, a, b, c, d, own, index_ref, keep, send):
    total = a[...].astype(F32) + b[...].astype(F32) + c[...].astype(F32) + d[...].astype(F32)
    grad = (pages(own).astype(F32) + total).astype(BF)
    rows, tokens = CHIPS * 8, 2 * PAGE
    row, col = iota((rows, tokens), 0), iota((rows, tokens), 1)
    part, chip = row & 7, row >> 3
    live = jnp.logical_and(part < 6, (part & 1) == (col >> 7))
    for out, core in ((keep, me[3]), (send, 1 - me[3])):
        slot = (2 * chip + core) * SLOTS + (part >> 1)
        pick = jnp.logical_and(live, slot == index_ref[0:1])
        out[...] = nt(pick.astype(BF), grad).astype(BF)


def collect_kernel(me, arrived, out_ref):
    rows, tokens = CHIPS * 16, SLOTS * PAGE
    row, col = iota((rows, tokens), 0), iota((rows, tokens), 1)
    part, chip, rel = row & 7, row >> 4, (row >> 3) & 1
    core = jnp.where(rel == 0, me[3], 1 - me[3])
    position = 4 * chip + 2 * core + (part & 1)
    pick = jnp.logical_and(part < 6, col == (part >> 1) * PAGE + position)
    out_ref[...] = tn(arrived[...], pick.astype(BF)).astype(BF)


def finish_kernel(a, b, c, d, own, out_ref):
    total = a[...].astype(F32) + b[...].astype(F32) + c[...].astype(F32) + d[...].astype(F32)
    grad = (own[...].astype(F32) + total).astype(BF)
    for n in range(SLOTS):
        out_ref[n] = grad[:, n * PAGE : (n + 1) * PAGE]


def shift(value, axis, size, by):
    return lax.ppermute(value, axis, [(i, (i + by) % size) for i in range(size)])


def gathered(value):
    return (value,) + tuple(shift(value, "x", TP, k) for k in range(1, TP))


def exchanged(parts):
    return (parts[0],) + tuple(shift(parts[k], "x", TP, k) for k in range(1, TP))


def over_chips(keep, got):
    rows = call(join_kernel, (keep, got), [half(CHIPS, 16, OWN)], smem=0)[0]
    arrived = lax.all_to_all(rows, ("z", "y"), 0, 0)
    return arrived.reshape(CHIPS * 16, OWN)


def paired(me, keep, got):
    return call(pair_kernel, (me, keep, got), [half(NZ * ROWS, HALF)] * NY)


def over_column(cols):
    return [cols[0]] + [shift(cols[k], "y", NY, k) for k in range(1, NY)]


def over_rows(total):
    return lax.all_to_all(total, "z", 0, 0)


def finish_weights(me, spatial, temporal, mark, scale):
    out = [full(ROWS // 2, 2 * HALF)] * 2
    mine, other = call(functools.partial(last_kernel, scale=scale), (me, spatial, mark, *temporal), out)
    other = shift(other, "c", NC, 1)
    return call(order_kernel, (me, mine, other), [full(ROWS // 2, 2, 4, OWN)])[0]


def per_device(frames, frame_counts, weights, grad_out):
    me = Place()
    scale = 1.0 / math.sqrt(grad_out.shape[0] * PAGE)
    tokens, t_tokens = SLOTS * PAGE, 2 * PAGE
    own = jnp.transpose(frames, (0, 2, 1))
    up_own = jnp.transpose(grad_out, (1, 2, 0))
    turned = jnp.swapaxes(weights, 2, 3)
    held = lambda n: pltpu.VMEM((TP, OWN, n), BF)
    room = lambda n: [pltpu.VMEM((D, n), F32), pltpu.VMEM((D, n), F32)]
    lines = [half(D, HALF)] * 2
    big = 2 * tokens * D * 4 * OWN

    chunks = gathered(own)
    places = jax.ShapeDtypeStruct((8, t_tokens), jnp.int32)
    own, up_own, index = call(
        stage_kernel, (frame_counts, own, up_own, turned), [half(*own.shape), half(*up_own.shape), places]
    )
    *parts, x, mix = call(
        spatial_kernel,
        (me, own, *chunks[1:], turned),
        [half(OWN, tokens)] * TP + [half(D, tokens), half(OWN, tokens)],
        [held(tokens), held(tokens)],
        flops=big,
    )
    parts = exchanged(parts)
    keep, send = call(spread_kernel, (me, *parts, own), [half(CHIPS * 8, OWN)] * 2)
    keep, up_own = lax.optimization_barrier((keep, up_own))
    ups = gathered(up_own)
    arrived = over_chips(keep, shift(send, "c", NC, 1))
    rows = call(pick_kernel, (me, arrived, index), [half(OWN, t_tokens)])[0]
    hidden = gathered(rows)
    up, grad_mix = call(
        upstream_kernel,
        (me, *ups, turned),
        [half(D, t_tokens), full(OWN, t_tokens)],
        [held(t_tokens)],
        flops=big // 4,
    )
    *parts, normed, grads = call(
        temporal_kernel,
        (me, *hidden, grad_mix, turned),
        [half(OWN, t_tokens)] * TP + [half(D, t_tokens)] * 2,
        [held(t_tokens), held(t_tokens)],
        flops=big,
    )
    parts = exchanged(parts)
    t_keep, t_send = call(weight_kernel, (me, normed, up, grads), lines, room(t_tokens), flops=big)
    parts, t_keep, t_send = lax.optimization_barrier((parts, t_keep, t_send))
    keep, send = call(scatter_kernel, (me, *parts, up_own, index), [half(CHIPS * 8, OWN)] * 2)
    got, t_send = lax.optimization_barrier((shift(send, "c", NC, 1), t_send))
    t_cols = over_column(paired(me, t_keep, shift(t_send, "c", NC, 1)))
    arrived = over_chips(keep, got)
    grad_hidden = call(collect_kernel, (me, arrived), [half(OWN, tokens)])[0]
    ups = gathered(grad_hidden)
    qkv, rows, probs = call(
        ready_kernel,
        (x, turned),
        [full(3 * OWN, tokens), half(D, tokens), full(HEADS * tokens, PAGE)],
        room(tokens),
        smem=0,
        flops=big,
    )
    mark = call(mark_kernel, t_cols, [half(16, PAGE)], smem=0, place=pl.ANY)[0]
    ups, mark, rows = lax.optimization_barrier((ups, mark, rows))
    keep, send, grads = call(
        spatial_back_kernel,
        (me, *ups, qkv, probs, mix, rows, turned),
        lines + [half(3 * OWN, tokens)],
        [held(tokens), *room(tokens)],
        flops=big,
    )
    got = shift(send, "c", NC, 1)
    parts = call(
        spatial_input_kernel,
        (me, x, grads, turned),
        [half(OWN, tokens)] * TP,
        [held(tokens)],
        flops=big,
    )
    got, parts = lax.optimization_barrier((got, parts))
    sums = call(sum_kernel, (keep, got), [half(D, HALF)], smem=0)[0]
    t_cols, sums = lax.optimization_barrier((t_cols, sums))
    t_parts = [half(NZ // 2, PAD, HALF)] * 2
    t_keep, t_send = call(parity_kernel, (me, *t_cols), t_parts)
    t_got = lax.ppermute(t_send, "z", [(z, z ^ 1) for z in range(NZ)])
    t_parts = call(quarter_kernel, (me, t_keep, t_got), [half(PAD, HALF)] * 4)
    t_parts = [t_parts[0]] + [shift(t_parts[k], "z", NZ, 2 * k) for k in range(1, 4)]
    cols = lax.all_to_all(sums.reshape(NY, NZ * ROWS, HALF), "y", 0, 0)
    parts = exchanged(parts)
    cols, t_parts, parts = lax.optimization_barrier((cols, t_parts, parts))
    column = call(column_kernel, (cols,), [half(NZ, PAD, HALF)], smem=0)[0]
    moved = over_rows(column)
    frame_grads = call(finish_kernel, (*parts, grad_hidden), [half(SLOTS, OWN, PAGE)], smem=0)[0]
    moved, frame_grads = lax.optimization_barrier((moved, frame_grads))
    weight_grads = finish_weights(me, moved, t_parts, mark, scale)
    return jnp.transpose(frame_grads, (0, 2, 1)), weight_grads


def solution(mesh):
    fine = Mesh(mesh.devices.reshape(NZ, NY, NC, TP), ("z", "y", "c", "x"))
    seq = ("z", "y", "c")
    return jax.shard_map(
        per_device,
        mesh=fine,
        in_specs=(P(seq, None, "x"), P(), P(None, None, None, "x"), P(None, seq, "x")),
        out_specs=(P(seq, None, "x"), P(seq, None, None, "x")),
        check_vma=False,
    )
```

```python
import functools
import math

import jax
import jax.numpy as jnp
from jax import lax
from jax.experimental import pallas as pl
from jax.experimental.pallas import tpu as pltpu
from jax.sharding import Mesh
from jax.sharding import PartitionSpec as P

HD = 72
TF = 16
HEADS = 4
OWN = HEADS * HD
TP = 4
D = OWN * TP
PAGE = 128
SLOTS = 3
NZ, NY, NC = 8, 4, 2
CHIPS = NZ * NY
ROWS = 36
PAD = 40
HALF = 640
EPS = 1e-06
SCALE = HD**-0.5
F32 = jnp.float32
BF = jnp.bfloat16


def nn(a, b):
    return lax.dot_general(a, b, (((1,), (0,)), ((), ())), preferred_element_type=F32)


def nt(a, b):
    return lax.dot_general(a, b, (((1,), (1,)), ((), ())), preferred_element_type=F32)


def tn(a, b):
    return lax.dot_general(a, b, (((0,), (0,)), ((), ())), preferred_element_type=F32)


def iota(shape, dim):
    return lax.broadcasted_iota(jnp.int32, shape, dim)


class Place:
    def __getitem__(self, at):
        return lax.axis_index("xyzc"[at])


def call(body, ins, outs, scratch=(), smem=1, flops=1_000_000, limit=16, place=pltpu.VMEM):
    if isinstance(ins[0], Place):
        body, ins, smem = functools.partial(body, ins[0]), ins[1:], 0
    in_specs = [
        pl.BlockSpec(memory_space=pltpu.SMEM) if i < smem else pl.BlockSpec(memory_space=place)
        for i in range(len(ins))
    ]
    size = sum(math.prod(o.shape) * o.dtype.itemsize for o in outs)
    size += sum(math.prod(i.shape) * i.dtype.itemsize for i in ins)
    out_specs = [pl.BlockSpec(memory_space=pltpu.VMEM) for _ in outs]
    return pl.pallas_call(
        body,
        out_shape=list(outs),
        in_specs=in_specs,
        out_specs=out_specs,
        scratch_shapes=list(scratch),
        compiler_params=pltpu.CompilerParams(vmem_limit_bytes=limit * 2**20),
        cost_estimate=pl.CostEstimate(flops=flops, bytes_accessed=size, transcendentals=0),
    )(*ins)


def half(*shape):
    return jax.ShapeDtypeStruct(shape, BF)


def full(*shape):
    return jax.ShapeDtypeStruct(shape, F32)


def normalise(x):
    center = x - jnp.sum(x, axis=0, keepdims=True) * (1.0 / D)
    inverse = lax.rsqrt(jnp.sum(center * center, axis=0, keepdims=True) * (1.0 / D) + EPS)
    return center * inverse, inverse


def normalise_back(normed, inverse, up):
    mean = jnp.sum(up, axis=0, keepdims=True) * (1.0 / D)
    along = jnp.sum(up * normed, axis=0, keepdims=True) * (1.0 / D)
    return inverse * (up - mean - normed * along)


def unit(rows):
    inverse = lax.rsqrt(jnp.sum(rows * rows, axis=0, keepdims=True) * (1.0 / HD) + EPS)
    return inverse, (rows * inverse).astype(BF)


def unit_back(rows, inverse, up):
    along = jnp.sum(up * rows, axis=0, keepdims=True) * (1.0 / HD)
    return inverse * up - rows * (inverse * inverse * inverse * along)


def head_parts(qkv, h):
    q = qkv[h * HD : (h + 1) * HD]
    k = qkv[OWN + h * HD : OWN + (h + 1) * HD]
    v = qkv[2 * OWN + h * HD : 2 * OWN + (h + 1) * HD]
    q_inv, q_unit = unit(q)
    k_inv, k_unit = unit(k)
    return q, k, q_inv, q_unit, k_inv, k_unit, v.astype(BF)


def weights_of(k_unit, q_unit, mask):
    raised = jnp.exp(tn(k_unit, q_unit) * SCALE)
    if mask is not None:
        raised = jnp.where(mask, raised, 0.0)
    return raised * (1.0 / jnp.sum(raised, axis=0, keepdims=True))


def mixture_of(qkv, tokens, mask):
    heads = []
    for h in range(HEADS):
        _, _, _, q_unit, _, k_unit, v = head_parts(qkv, h)
        blocks = []
        for b in range(tokens // PAGE):
            at = slice(b * PAGE, (b + 1) * PAGE)
            probs = weights_of(k_unit[:, at], q_unit[:, at], mask)
            blocks.append(nn(v[:, at], probs.astype(BF)))
        heads.append(jnp.concatenate(blocks, axis=1))
    return jnp.concatenate(heads, axis=0).astype(BF)


def attend_back(qkv, grad_mix, tokens, mask, given=None):
    queries, keys, values, mixes = [], [], [], []
    for h in range(HEADS):
        q, k, q_inv, q_unit, k_inv, k_unit, v = head_parts(qkv, h)
        gm = grad_mix[h * HD : (h + 1) * HD].astype(BF)
        with_mixture = given is None
        q_slope, k_slope, v_grad, mix = [], [], [], []
        for b in range(tokens // PAGE):
            at = slice(b * PAGE, (b + 1) * PAGE)
            if with_mixture:
                probs = weights_of(k_unit[:, at], q_unit[:, at], mask)
            else:
                unit_at = (h * (tokens // PAGE) + b) * PAGE
                probs = given[unit_at : unit_at + PAGE]
            probs_half = probs.astype(BF)
            if with_mixture:
                mix.append(nn(v[:, at], probs_half))
            grad_probs = tn(v[:, at], gm[:, at])
            v_grad.append(nt(gm[:, at], probs_half))
            weighted = probs * grad_probs
            grad_scores = (weighted - probs * jnp.sum(weighted, axis=0, keepdims=True)).astype(BF)
            q_slope.append(nn(k_unit[:, at], grad_scores) * SCALE)
            k_slope.append(nt(q_unit[:, at], grad_scores) * SCALE)
        queries.append(unit_back(q, q_inv, jnp.concatenate(q_slope, axis=1)))
        keys.append(unit_back(k, k_inv, jnp.concatenate(k_slope, axis=1)))
        values.append(jnp.concatenate(v_grad, axis=1))
        if with_mixture:
            mixes.append(jnp.concatenate(mix, axis=1))
    join = lambda parts: jnp.concatenate(parts, axis=0).astype(BF)
    return join(queries), join(keys), join(values), join(mixes) if given is None else None


def rows_of(w_ref, layer):
    return w_ref[layer, :3].reshape(3 * OWN, D)


def assemble(own, chunks, held):
    for k, chunk in enumerate(chunks):
        at = (own + TP - k) & (TP - 1)
        if len(chunk.shape) == 3:
            for n in range(chunk.shape[0]):
                held[at, :, n * PAGE : (n + 1) * PAGE] = chunk[n]
        else:
            held[at] = chunk[...]
    return held[...].reshape(D, held.shape[2])


def deal(own, value, held, outs):
    held[...] = value.astype(BF).reshape(held.shape)
    for k, out in enumerate(outs):
        out[...] = held[(own + k) & (TP - 1)]


def pages(ref):
    return jnp.concatenate([ref[n] for n in range(ref.shape[0])], axis=1)


def stage_kernel(counts, a_ref, b_ref, w_ref, a_out, b_out, index_out):
    a_out[...] = a_ref[...]
    b_out[...] = b_ref[...]
    frame = iota(index_out.shape, 1) & (PAGE - 1)
    index = jnp.zeros(index_out.shape, jnp.int32)
    start = jnp.int32(0)
    for s in range(counts.shape[0]):
        index = jnp.where(frame >= start, frame + (s * SLOTS - start), index)
        start = start + counts[s]
    index_out[...] = index


def join_kernel(a_ref, b_ref, out_ref):
    parts = [ref[...].astype(F32).reshape(CHIPS, 8, OWN) for ref in (a_ref, b_ref)]
    out_ref[...] = jnp.concatenate(parts, axis=1).astype(BF)


def spatial_kernel(me, c0, c1, c2, c3, w_ref, p0, p1, p2, p3, x_out, mix_out, held, dealt):
    x = assemble(me[0], (c0, c1, c2, c3), held)
    x_out[...] = x
    normed, _ = normalise(x.astype(F32))
    qkv = nn(rows_of(w_ref, 0), normed.astype(BF))
    mix = mixture_of(qkv, x.shape[1], None)
    mix_out[...] = mix
    deal(me[0], tn(w_ref[0, 3], mix), dealt, (p0, p1, p2, p3))


def upstream_kernel(me, g0, g1, g2, g3, w_ref, up_out, mix_out, held):
    up = assemble(me[0], (g0, g1, g2, g3), held)
    up_out[...] = up
    mix_out[...] = nn(w_ref[1, 3], up).astype(BF).astype(F32)


def temporal_kernel(
    me, h0, h1, h2, h3, grad_mix, w_ref, p0, p1, p2, p3, normed_out, grads_out, held, dealt
):
    x = assemble(me[0], (h0, h1, h2, h3), held)
    normed, inverse = normalise(x.astype(F32))
    normed_half = normed.astype(BF)
    normed_out[...] = normed_half
    qkv = nn(rows_of(w_ref, 1), normed_half)
    mask = (iota((PAGE, PAGE), 0) >> 4) == (iota((PAGE, PAGE), 1) >> 4)
    gq, gk, gv, mix = attend_back(qkv, grad_mix, x.shape[1], mask)
    for m, part in enumerate((gq, gk, gv, mix)):
        grads_out[m * OWN : (m + 1) * OWN] = part
    grad_normed = tn(rows_of(w_ref, 1), jnp.concatenate([gq, gk, gv], axis=0))
    deal(me[0], normalise_back(normed, inverse, grad_normed), dealt, (p0, p1, p2, p3))


def ready_kernel(x_ref, w_ref, qkv_out, lines_out, probs_out, wide, held):
    normed, _ = normalise(x_ref[...].astype(F32))
    normed = normed.astype(BF)
    wide[...] = normed.astype(F32)
    lines_out[...] = regroup(wide, held)
    qkv = nn(rows_of(w_ref, 0), normed)
    qkv_out[...] = qkv
    tokens = x_ref.shape[1]
    for h in range(HEADS):
        _, _, _, q_unit, _, k_unit, _ = head_parts(qkv, h)
        for b in range(tokens // PAGE):
            at = slice(b * PAGE, (b + 1) * PAGE)
            unit_at = (h * (tokens // PAGE) + b) * PAGE
            probs_out[unit_at : unit_at + PAGE] = weights_of(k_unit[:, at], q_unit[:, at], None)


def spatial_back_kernel(
    me, g0, g1, g2, g3, qkv_ref, probs_ref, mix_ref, lines_ref, w_ref,
    keep, send, grads_out, held_g, wide, held,
):
    up = assemble(me[0], (g0, g1, g2, g3), held_g)
    wide[...] = up.astype(F32)
    grad_mix = nn(w_ref[0, 3], up)
    gq, gk, gv, _ = attend_back(qkv_ref, grad_mix, up.shape[1], None, probs_ref)
    grads = jnp.concatenate([gq, gk, gv], axis=0)
    grads_out[...] = grads
    weight_products(me[3], lines_ref[...], regroup(wide, held), grads, mix_ref[...], keep, send)


def spatial_input_kernel(me, x_ref, grads, w_ref, p0, p1, p2, p3, dealt):
    normed, inverse = normalise(x_ref[...].astype(F32))
    grad_normed = tn(rows_of(w_ref, 0), grads[...])
    deal(me[0], normalise_back(normed, inverse, grad_normed), dealt, (p0, p1, p2, p3))


def regroup(ref, held):
    for y in range(NY):
        for z in range(NZ):
            at = (y * NZ + z) * ROWS
            held[at : at + ROWS] = ref[z * NY * ROWS + y * ROWS : z * NY * ROWS + (y + 1) * ROWS]
    return held[...].astype(BF)


def weight_products(core, lines, up_lines, grads, mix, keep, send):
    zeros = lambda n: jnp.zeros((n, mix.shape[1]), BF)
    first = nt(lines, jnp.concatenate([grads[: 2 * OWN], zeros(HALF - 2 * OWN)], axis=0)).astype(BF)
    low = nt(lines, jnp.concatenate([grads[2 * OWN :], zeros(96)], axis=0))
    low = low + nt(up_lines, jnp.concatenate([zeros(OWN), mix[:96]], axis=0))
    high = nt(up_lines, jnp.concatenate([mix[96:], zeros(64)], axis=0))

    @pl.when(core == 0)
    def _():
        keep[...] = first
        send[:, :384] = low.astype(BF)
        send[:, 384:] = high.astype(BF)

    @pl.when(core == 1)
    def _():
        send[...] = first
        keep[:, :384] = low.astype(BF)
        keep[:, 384:] = high.astype(BF)


def weight_kernel(me, normed_ref, up_ref, grads_ref, keep, send, wide, held):
    wide[...] = normed_ref[...].astype(F32)
    lines = regroup(wide, held)
    wide[...] = up_ref[...].astype(F32)
    up_lines = regroup(wide, held)
    weight_products(me[3], lines, up_lines, grads_ref[: 3 * OWN], grads_ref[3 * OWN :], keep, send)


def total_of(ref):
    total = ref[0].astype(F32)
    for n in range(1, ref.shape[0]):
        total = total + ref[n].astype(F32)
    return total


def pair_kernel(me, keep, got, *outs):
    span = NZ * ROWS
    for k, out in enumerate(outs):
        rows = pl.ds(pl.multiple_of(((me[1] + k) & (NY - 1)) * span, 16), span)
        out[...] = (keep[rows].astype(F32) + got[rows].astype(F32)).astype(BF)


def sum_kernel(keep, got, out):
    out[...] = (keep[...].astype(F32) + got[...].astype(F32)).astype(BF)


def padded(lines):
    return jnp.concatenate([lines, jnp.zeros((PAD - ROWS, HALF), F32)], axis=0)


def column_kernel(parts, out):
    total = total_of(parts)
    for z in range(NZ):
        out[z] = padded(total[z * ROWS : (z + 1) * ROWS]).astype(BF)


def mark_kernel(a, b, c, d, out):
    out[...] = jnp.zeros((16, PAGE), BF)


def parity_kernel(me, a, b, c, d, keep, send):
    total = a[...].astype(F32) + b[...].astype(F32) + c[...].astype(F32) + d[...].astype(F32)
    even = (me[2] & 1) == 0
    for i in range(NZ // 2):
        at = 2 * i * ROWS
        first = padded(total[at : at + ROWS]).astype(BF)
        second = padded(total[at + ROWS : at + 2 * ROWS]).astype(BF)
        keep[i] = jnp.where(even, first, second)
        send[i] = jnp.where(even, second, first)


def quarter_kernel(me, keep, got, o0, o1, o2, o3):
    for k, out in enumerate((o0, o1, o2, o3)):
        at = ((me[2] >> 1) + k) & 3
        out[...] = (keep[at].astype(F32) + got[at].astype(F32)).astype(BF)


def last_kernel(me, spatial, mark, *refs, scale):
    temporal, (keep, send) = refs[:4], refs[4:]
    first = me[3] == 0
    other = temporal[0][...].astype(F32)
    for part in temporal[1:]:
        other = other + part[...].astype(F32)
    for at, total in ((0, total_of(spatial)), (HALF, other)):
        total = total * scale
        upper, lower = total[: ROWS // 2], total[ROWS // 2 : ROWS]
        keep[:, at : at + HALF] = jnp.where(first, upper, lower)
        send[:, at : at + HALF] = jnp.where(first, lower, upper)


def order_kernel(me, mine, other, out_ref):
    first = me[3] == 0
    for layer in range(2):
        a = mine[:, layer * HALF : (layer + 1) * HALF]
        b = other[:, layer * HALF : (layer + 1) * HALF]
        for n, part in enumerate((jnp.where(first, a, b), jnp.where(first, b, a))):
            for m in range(2):
                out_ref[:, layer, 2 * n + m] = part[:, m * OWN : (m + 1) * OWN]


def spread_kernel(me, a, b, c, d, own, keep, send):
    total = a[...].astype(F32) + b[...].astype(F32) + c[...].astype(F32) + d[...].astype(F32)
    hidden = (pages(own).astype(F32) + total).astype(BF)
    rows, tokens = CHIPS * 8, SLOTS * PAGE
    row, col = iota((rows, tokens), 0), iota((rows, tokens), 1)
    part, chip = row & 7, row >> 3
    base = (part >> 1) * PAGE + 4 * chip + (part & 1)
    for out, core in ((keep, me[3]), (send, 1 - me[3])):
        pick = jnp.logical_and(part < 6, col == base + 2 * core)
        out[...] = nt(pick.astype(BF), hidden).astype(BF)


def pick_kernel(me, arrived, index_ref, out_ref):
    rows, tokens = CHIPS * 16, 2 * PAGE
    row, col = iota((rows, tokens), 0), iota((rows, tokens), 1)
    part, chip, rel = row & 7, row >> 4, (row >> 3) & 1
    core = jnp.where(rel == 0, me[3], 1 - me[3])
    slot = (2 * chip + core) * SLOTS + (part >> 1)
    pick = jnp.logical_and(part < 6, (part & 1) == (col >> 7))
    pick = jnp.logical_and(pick, slot == index_ref[0:1])
    out_ref[...] = tn(arrived[...], pick.astype(BF)).astype(BF)


def scatter_kernel(me, a, b, c, d, own, index_ref, keep, send):
    total = a[...].astype(F32) + b[...].astype(F32) + c[...].astype(F32) + d[...].astype(F32)
    grad = (pages(own).astype(F32) + total).astype(BF)
    rows, tokens = CHIPS * 8, 2 * PAGE
    row, col = iota((rows, tokens), 0), iota((rows, tokens), 1)
    part, chip = row & 7, row >> 3
    live = jnp.logical_and(part < 6, (part & 1) == (col >> 7))
    for out, core in ((keep, me[3]), (send, 1 - me[3])):
        slot = (2 * chip + core) * SLOTS + (part >> 1)
        pick = jnp.logical_and(live, slot == index_ref[0:1])
        out[...] = nt(pick.astype(BF), grad).astype(BF)


def collect_kernel(me, arrived, out_ref):
    rows, tokens = CHIPS * 16, SLOTS * PAGE
    row, col = iota((rows, tokens), 0), iota((rows, tokens), 1)
    part, chip, rel = row & 7, row >> 4, (row >> 3) & 1
    core = jnp.where(rel == 0, me[3], 1 - me[3])
    position = 4 * chip + 2 * core + (part & 1)
    pick = jnp.logical_and(part < 6, col == (part >> 1) * PAGE + position)
    out_ref[...] = tn(arrived[...], pick.astype(BF)).astype(BF)


def finish_kernel(a, b, c, d, own, out_ref):
    total = a[...].astype(F32) + b[...].astype(F32) + c[...].astype(F32) + d[...].astype(F32)
    grad = (own[...].astype(F32) + total).astype(BF)
    for n in range(SLOTS):
        out_ref[n] = grad[:, n * PAGE : (n + 1) * PAGE]


def shift(value, axis, size, by):
    return lax.ppermute(value, axis, [(i, (i + by) % size) for i in range(size)])


def gathered(value):
    return (value,) + tuple(shift(value, "x", TP, k) for k in range(1, TP))


def exchanged(parts):
    return (parts[0],) + tuple(shift(parts[k], "x", TP, k) for k in range(1, TP))


def over_chips(keep, got):
    rows = call(join_kernel, (keep, got), [half(CHIPS, 16, OWN)], smem=0)[0]
    arrived = lax.all_to_all(rows, ("z", "y"), 0, 0)
    return arrived.reshape(CHIPS * 16, OWN)


def paired(me, keep, got):
    return call(pair_kernel, (me, keep, got), [half(NZ * ROWS, HALF)] * NY)


def over_column(cols):
    return [cols[0]] + [shift(cols[k], "y", NY, k) for k in range(1, NY)]


def over_rows(total):
    return lax.all_to_all(total, "z", 0, 0)


def finish_weights(me, spatial, temporal, mark, scale):
    out = [full(ROWS // 2, 2 * HALF)] * 2
    mine, other = call(functools.partial(last_kernel, scale=scale), (me, spatial, mark, *temporal), out)
    other = shift(other, "c", NC, 1)
    return call(order_kernel, (me, mine, other), [full(ROWS // 2, 2, 4, OWN)])[0]


def per_device(frames, frame_counts, weights, grad_out):
    me = Place()
    scale = 1.0 / math.sqrt(grad_out.shape[0] * PAGE)
    tokens, t_tokens = SLOTS * PAGE, 2 * PAGE
    own = jnp.transpose(frames, (0, 2, 1))
    up_own = jnp.transpose(grad_out, (1, 2, 0))
    turned = jnp.swapaxes(weights, 2, 3)
    held = lambda n: pltpu.VMEM((TP, OWN, n), BF)
    room = lambda n: [pltpu.VMEM((D, n), F32), pltpu.VMEM((D, n), F32)]
    lines = [half(D, HALF)] * 2
    big = 2 * tokens * D * 4 * OWN

    chunks = gathered(own)
    places = jax.ShapeDtypeStruct((8, t_tokens), jnp.int32)
    own, up_own, index = call(
        stage_kernel, (frame_counts, own, up_own, turned), [half(*own.shape), half(*up_own.shape), places]
    )
    *parts, x, mix = call(
        spatial_kernel,
        (me, own, *chunks[1:], turned),
        [half(OWN, tokens)] * TP + [half(D, tokens), half(OWN, tokens)],
        [held(tokens), held(tokens)],
        flops=big,
    )
    parts = exchanged(parts)
    keep, send = call(spread_kernel, (me, *parts, own), [half(CHIPS * 8, OWN)] * 2)
    keep, up_own = lax.optimization_barrier((keep, up_own))
    ups = gathered(up_own)
    arrived = over_chips(keep, shift(send, "c", NC, 1))
    rows = call(pick_kernel, (me, arrived, index), [half(OWN, t_tokens)])[0]
    hidden = gathered(rows)
    up, grad_mix = call(
        upstream_kernel,
        (me, *ups, turned),
        [half(D, t_tokens), full(OWN, t_tokens)],
        [held(t_tokens)],
        flops=big // 4,
    )
    *parts, normed, grads = call(
        temporal_kernel,
        (me, *hidden, grad_mix, turned),
        [half(OWN, t_tokens)] * TP + [half(D, t_tokens)] * 2,
        [held(t_tokens), held(t_tokens)],
        flops=big,
    )
    parts = exchanged(parts)
    t_keep, t_send = call(weight_kernel, (me, normed, up, grads), lines, room(t_tokens), flops=big)
    parts, t_keep, t_send = lax.optimization_barrier((parts, t_keep, t_send))
    keep, send = call(scatter_kernel, (me, *parts, up_own, index), [half(CHIPS * 8, OWN)] * 2)
    got, t_send = lax.optimization_barrier((shift(send, "c", NC, 1), t_send))
    t_cols = over_column(paired(me, t_keep, shift(t_send, "c", NC, 1)))
    arrived = over_chips(keep, got)
    grad_hidden = call(collect_kernel, (me, arrived), [half(OWN, tokens)])[0]
    ups = gathered(grad_hidden)
    qkv, rows, probs = call(
        ready_kernel,
        (x, turned),
        [full(3 * OWN, tokens), half(D, tokens), full(HEADS * tokens, PAGE)],
        room(tokens),
        smem=0,
        flops=big,
    )
    mark = call(mark_kernel, t_cols, [half(16, PAGE)], smem=0, place=pl.ANY)[0]
    ups, mark, rows = lax.optimization_barrier((ups, mark, rows))
    keep, send, grads = call(
        spatial_back_kernel,
        (me, *ups, qkv, probs, mix, rows, turned),
        lines + [half(3 * OWN, tokens)],
        [held(tokens), *room(tokens)],
        flops=big,
    )
    got = shift(send, "c", NC, 1)
    parts = call(
        spatial_input_kernel,
        (me, x, grads, turned),
        [half(OWN, tokens)] * TP,
        [held(tokens)],
        flops=big,
    )
    got, parts = lax.optimization_barrier((got, parts))
    sums = call(sum_kernel, (keep, got), [half(D, HALF)], smem=0)[0]
    t_cols, sums = lax.optimization_barrier((t_cols, sums))
    t_parts = [half(NZ // 2, PAD, HALF)] * 2
    t_keep, t_send = call(parity_kernel, (me, *t_cols), t_parts)
    t_keep, parts = lax.optimization_barrier((t_keep, parts))
    t_got = lax.ppermute(t_send, "z", [(z, z ^ 1) for z in range(NZ)])
    t_parts = call(quarter_kernel, (me, t_keep, t_got), [half(PAD, HALF)] * 4)
    t_parts = [t_parts[0]] + [shift(t_parts[k], "z", NZ, 2 * k) for k in range(1, 4)]
    cols = lax.all_to_all(sums.reshape(NY, NZ * ROWS, HALF), "y", 0, 0)
    parts = exchanged(parts)
    cols, t_parts, parts = lax.optimization_barrier((cols, t_parts, parts))
    column = call(column_kernel, (cols,), [half(NZ, PAD, HALF)], smem=0)[0]
    moved = over_rows(column)
    frame_grads = call(finish_kernel, (*parts, grad_hidden), [half(SLOTS, OWN, PAGE)], smem=0)[0]
    moved, frame_grads = lax.optimization_barrier((moved, frame_grads))
    weight_grads = finish_weights(me, moved, t_parts, mark, scale)
    return jnp.transpose(frame_grads, (0, 2, 1)), weight_grads


def solution(mesh):
    fine = Mesh(mesh.devices.reshape(NZ, NY, NC, TP), ("z", "y", "c", "x"))
    seq = ("z", "y", "c")
    return jax.shard_map(
        per_device,
        mesh=fine,
        in_specs=(P(seq, None, "x"), P(), P(None, None, None, "x"), P(None, seq, "x")),
        out_specs=(P(seq, None, "x"), P(seq, None, None, "x")),
        check_vma=False,
    )
```

```python
import functools
import math

import jax
import jax.numpy as jnp
from jax import lax
from jax.experimental import pallas as pl
from jax.experimental.pallas import tpu as pltpu
from jax.sharding import Mesh
from jax.sharding import PartitionSpec as P

HD = 72
TF = 16
HEADS = 4
OWN = HEADS * HD
TP = 4
D = OWN * TP
PAGE = 128
SLOTS = 3
NZ, NY, NC = 8, 4, 2
CHIPS = NZ * NY
ROWS = 36
PAD = 40
HALF = 640
PACK = 168
EPS = 1e-06
SCALE = HD**-0.5
F32 = jnp.float32
BF = jnp.bfloat16


def nn(a, b):
    return lax.dot_general(a, b, (((1,), (0,)), ((), ())), preferred_element_type=F32)


def nt(a, b):
    return lax.dot_general(a, b, (((1,), (1,)), ((), ())), preferred_element_type=F32)


def tn(a, b):
    return lax.dot_general(a, b, (((0,), (0,)), ((), ())), preferred_element_type=F32)


def iota(shape, dim):
    return lax.broadcasted_iota(jnp.int32, shape, dim)


class Place:
    def __getitem__(self, at):
        return lax.axis_index("xyzc"[at])


def call(body, ins, outs, scratch=(), smem=1, flops=1_000_000, limit=16, place=pltpu.VMEM):
    if isinstance(ins[0], Place):
        body, ins, smem = functools.partial(body, ins[0]), ins[1:], 0
    in_specs = [
        pl.BlockSpec(memory_space=pltpu.SMEM) if i < smem else pl.BlockSpec(memory_space=place)
        for i in range(len(ins))
    ]
    size = sum(math.prod(o.shape) * o.dtype.itemsize for o in outs)
    size += sum(math.prod(i.shape) * i.dtype.itemsize for i in ins)
    out_specs = [pl.BlockSpec(memory_space=pltpu.VMEM) for _ in outs]
    return pl.pallas_call(
        body,
        out_shape=list(outs),
        in_specs=in_specs,
        out_specs=out_specs,
        scratch_shapes=list(scratch),
        compiler_params=pltpu.CompilerParams(vmem_limit_bytes=limit * 2**20),
        cost_estimate=pl.CostEstimate(flops=flops, bytes_accessed=size, transcendentals=0),
    )(*ins)


def half(*shape):
    return jax.ShapeDtypeStruct(shape, BF)


def full(*shape):
    return jax.ShapeDtypeStruct(shape, F32)


def normalise(x):
    center = x - jnp.sum(x, axis=0, keepdims=True) * (1.0 / D)
    inverse = lax.rsqrt(jnp.sum(center * center, axis=0, keepdims=True) * (1.0 / D) + EPS)
    return center * inverse, inverse


def normalise_back(normed, inverse, up):
    mean = jnp.sum(up, axis=0, keepdims=True) * (1.0 / D)
    along = jnp.sum(up * normed, axis=0, keepdims=True) * (1.0 / D)
    return inverse * (up - mean - normed * along)


def unit(rows):
    inverse = lax.rsqrt(jnp.sum(rows * rows, axis=0, keepdims=True) * (1.0 / HD) + EPS)
    return inverse, (rows * inverse).astype(BF)


def unit_back(rows, inverse, up):
    along = jnp.sum(up * rows, axis=0, keepdims=True) * (1.0 / HD)
    return inverse * up - rows * (inverse * inverse * inverse * along)


def head_parts(qkv, h):
    q = qkv[h * HD : (h + 1) * HD]
    k = qkv[OWN + h * HD : OWN + (h + 1) * HD]
    v = qkv[2 * OWN + h * HD : 2 * OWN + (h + 1) * HD]
    q_inv, q_unit = unit(q)
    k_inv, k_unit = unit(k)
    return q, k, q_inv, q_unit, k_inv, k_unit, v.astype(BF)


def weights_of(k_unit, q_unit, mask):
    raised = jnp.exp(tn(k_unit, q_unit) * SCALE)
    if mask is not None:
        raised = jnp.where(mask, raised, 0.0)
    return raised * (1.0 / jnp.sum(raised, axis=0, keepdims=True))


def mixture_of(qkv, tokens, mask):
    heads = []
    for h in range(HEADS):
        _, _, _, q_unit, _, k_unit, v = head_parts(qkv, h)
        blocks = []
        for b in range(tokens // PAGE):
            at = slice(b * PAGE, (b + 1) * PAGE)
            probs = weights_of(k_unit[:, at], q_unit[:, at], mask)
            blocks.append(nn(v[:, at], probs.astype(BF)))
        heads.append(jnp.concatenate(blocks, axis=1))
    return jnp.concatenate(heads, axis=0).astype(BF)


def attend_back(qkv, grad_mix, tokens, mask, given=None):
    queries, keys, values, mixes = [], [], [], []
    for h in range(HEADS):
        q, k, q_inv, q_unit, k_inv, k_unit, v = head_parts(qkv, h)
        gm = grad_mix[h * HD : (h + 1) * HD].astype(BF)
        with_mixture = given is None
        q_slope, k_slope, v_grad, mix = [], [], [], []
        for b in range(tokens // PAGE):
            at = slice(b * PAGE, (b + 1) * PAGE)
            if with_mixture:
                probs = weights_of(k_unit[:, at], q_unit[:, at], mask)
            else:
                unit_at = (h * (tokens // PAGE) + b) * PAGE
                probs = given[unit_at : unit_at + PAGE]
            probs_half = probs.astype(BF)
            if with_mixture:
                mix.append(nn(v[:, at], probs_half))
            grad_probs = tn(v[:, at], gm[:, at])
            v_grad.append(nt(gm[:, at], probs_half))
            weighted = probs * grad_probs
            grad_scores = (weighted - probs * jnp.sum(weighted, axis=0, keepdims=True)).astype(BF)
            q_slope.append(nn(k_unit[:, at], grad_scores) * SCALE)
            k_slope.append(nt(q_unit[:, at], grad_scores) * SCALE)
        queries.append(unit_back(q, q_inv, jnp.concatenate(q_slope, axis=1)))
        keys.append(unit_back(k, k_inv, jnp.concatenate(k_slope, axis=1)))
        values.append(jnp.concatenate(v_grad, axis=1))
        if with_mixture:
            mixes.append(jnp.concatenate(mix, axis=1))
    join = lambda parts: jnp.concatenate(parts, axis=0).astype(BF)
    return join(queries), join(keys), join(values), join(mixes) if given is None else None


def rows_of(w_ref, layer):
    return w_ref[layer, :3].reshape(3 * OWN, D)


def assemble(own, chunks, held):
    for k, chunk in enumerate(chunks):
        at = (own + TP - k) & (TP - 1)
        if len(chunk.shape) == 3:
            for n in range(chunk.shape[0]):
                held[at, :, n * PAGE : (n + 1) * PAGE] = chunk[n]
        else:
            held[at] = chunk[...]
    return held[...].reshape(D, held.shape[2])


def deal(own, value, held, outs):
    held[...] = value.astype(BF).reshape(held.shape)
    for k, out in enumerate(outs):
        out[...] = held[(own + k) & (TP - 1)]


def pages(ref):
    return jnp.concatenate([ref[n] for n in range(ref.shape[0])], axis=1)


def stage_kernel(counts, a_ref, b_ref, w_ref, a_out, b_out, index_out):
    a_out[...] = a_ref[...]
    b_out[...] = b_ref[...]
    frame = iota(index_out.shape, 1) & (PAGE - 1)
    index = jnp.zeros(index_out.shape, jnp.int32)
    start = jnp.int32(0)
    for s in range(counts.shape[0]):
        index = jnp.where(frame >= start, frame + (s * SLOTS - start), index)
        start = start + counts[s]
    index_out[...] = index


def join_kernel(a_ref, b_ref, out_ref):
    parts = [ref[...].astype(F32).reshape(CHIPS, 8, OWN) for ref in (a_ref, b_ref)]
    out_ref[...] = jnp.concatenate(parts, axis=1).astype(BF)


def spatial_kernel(me, c0, c1, c2, c3, w_ref, p0, p1, p2, p3, x_out, mix_out, held, dealt):
    x = assemble(me[0], (c0, c1, c2, c3), held)
    x_out[...] = x
    normed, _ = normalise(x.astype(F32))
    qkv = nn(rows_of(w_ref, 0), normed.astype(BF))
    mix = mixture_of(qkv, x.shape[1], None)
    mix_out[...] = mix
    deal(me[0], tn(w_ref[0, 3], mix), dealt, (p0, p1, p2, p3))


def upstream_kernel(me, g0, g1, g2, g3, w_ref, up_out, mix_out, held):
    up = assemble(me[0], (g0, g1, g2, g3), held)
    up_out[...] = up
    mix_out[...] = nn(w_ref[1, 3], up).astype(BF).astype(F32)


def temporal_kernel(
    me, h0, h1, h2, h3, grad_mix, w_ref, p0, p1, p2, p3, normed_out, grads_out, held, dealt
):
    x = assemble(me[0], (h0, h1, h2, h3), held)
    normed, inverse = normalise(x.astype(F32))
    normed_half = normed.astype(BF)
    normed_out[...] = normed_half
    qkv = nn(rows_of(w_ref, 1), normed_half)
    mask = (iota((PAGE, PAGE), 0) >> 4) == (iota((PAGE, PAGE), 1) >> 4)
    gq, gk, gv, mix = attend_back(qkv, grad_mix, x.shape[1], mask)
    for m, part in enumerate((gq, gk, gv, mix)):
        grads_out[m * OWN : (m + 1) * OWN] = part
    grad_normed = tn(rows_of(w_ref, 1), jnp.concatenate([gq, gk, gv], axis=0))
    deal(me[0], normalise_back(normed, inverse, grad_normed), dealt, (p0, p1, p2, p3))


def ready_kernel(x_ref, w_ref, qkv_out, lines_out, probs_out, wide, held):
    normed, _ = normalise(x_ref[...].astype(F32))
    normed = normed.astype(BF)
    wide[...] = normed.astype(F32)
    lines_out[...] = regroup(wide, held)
    qkv = nn(rows_of(w_ref, 0), normed)
    qkv_out[...] = qkv
    tokens = x_ref.shape[1]
    for h in range(HEADS):
        _, _, _, q_unit, _, k_unit, _ = head_parts(qkv, h)
        for b in range(tokens // PAGE):
            at = slice(b * PAGE, (b + 1) * PAGE)
            unit_at = (h * (tokens // PAGE) + b) * PAGE
            probs_out[unit_at : unit_at + PAGE] = weights_of(k_unit[:, at], q_unit[:, at], None)


def spatial_back_kernel(
    me, g0, g1, g2, g3, qkv_ref, probs_ref, mix_ref, lines_ref, w_ref,
    keep, send, grads_out, held_g, wide, held,
):
    up = assemble(me[0], (g0, g1, g2, g3), held_g)
    wide[...] = up.astype(F32)
    grad_mix = nn(w_ref[0, 3], up)
    gq, gk, gv, _ = attend_back(qkv_ref, grad_mix, up.shape[1], None, probs_ref)
    grads = jnp.concatenate([gq, gk, gv], axis=0)
    grads_out[...] = grads
    weight_products(me[3], lines_ref[...], regroup(wide, held), grads, mix_ref[...], keep, send)


def spatial_input_kernel(me, x_ref, grads, w_ref, p0, p1, p2, p3, dealt):
    normed, inverse = normalise(x_ref[...].astype(F32))
    grad_normed = tn(rows_of(w_ref, 0), grads[...])
    deal(me[0], normalise_back(normed, inverse, grad_normed), dealt, (p0, p1, p2, p3))


def regroup(ref, held):
    for y in range(NY):
        for z in range(NZ):
            at = (y * NZ + z) * ROWS
            held[at : at + ROWS] = ref[z * NY * ROWS + y * ROWS : z * NY * ROWS + (y + 1) * ROWS]
    return held[...].astype(BF)


def weight_products(core, lines, up_lines, grads, mix, keep, send):
    zeros = lambda n: jnp.zeros((n, mix.shape[1]), BF)
    first = nt(lines, jnp.concatenate([grads[: 2 * OWN], zeros(HALF - 2 * OWN)], axis=0)).astype(BF)
    low = nt(lines, jnp.concatenate([grads[2 * OWN :], zeros(96)], axis=0))
    low = low + nt(up_lines, jnp.concatenate([zeros(OWN), mix[:96]], axis=0))
    high = nt(up_lines, jnp.concatenate([mix[96:], zeros(64)], axis=0))

    @pl.when(core == 0)
    def _():
        keep[...] = first
        send[:, :384] = low.astype(BF)
        send[:, 384:] = high.astype(BF)

    @pl.when(core == 1)
    def _():
        send[...] = first
        keep[:, :384] = low.astype(BF)
        keep[:, 384:] = high.astype(BF)


def weight_kernel(me, normed_ref, up_ref, grads_ref, keep, send, wide, held):
    wide[...] = normed_ref[...].astype(F32)
    lines = regroup(wide, held)
    wide[...] = up_ref[...].astype(F32)
    up_lines = regroup(wide, held)
    weight_products(me[3], lines, up_lines, grads_ref[: 3 * OWN], grads_ref[3 * OWN :], keep, send)


def total_of(ref):
    total = ref[0].astype(F32)
    for n in range(1, ref.shape[0]):
        total = total + ref[n].astype(F32)
    return total


def pair_kernel(me, keep, got, *outs):
    span = NZ * ROWS
    for k, out in enumerate(outs):
        rows = pl.ds(pl.multiple_of(((me[1] + k) & (NY - 1)) * span, 16), span)
        out[...] = (keep[rows].astype(F32) + got[rows].astype(F32)).astype(BF)


def sum_kernel(keep, got, out):
    out[...] = (keep[...].astype(F32) + got[...].astype(F32)).astype(BF)


def padded(lines):
    return jnp.concatenate([lines, jnp.zeros((PAD - ROWS, HALF), F32)], axis=0)


def column_kernel(parts, out, held):
    total = total_of(parts)
    part = ROWS // 2
    for z in range(NZ):
        lines = total[z * ROWS : (z + 1) * ROWS]
        for n in range(4):
            held[z, n * ROWS : (n + 1) * ROWS] = lines[:, n * PAGE : (n + 1) * PAGE]
        rest = lines[:, 4 * PAGE : 2 * OWN]
        held[z, 4 * ROWS : 4 * ROWS + part] = jnp.concatenate([rest[:part], rest[part:]], axis=1)
        held[z, 4 * ROWS + part :] = jnp.zeros((PACK - 4 * ROWS - part, PAGE), F32)
    out[...] = held[...].astype(BF)


def mark_kernel(a, b, c, d, out):
    out[...] = jnp.zeros((16, PAGE), BF)


def parity_kernel(me, a, b, c, d, keep, send):
    total = a[...].astype(F32) + b[...].astype(F32) + c[...].astype(F32) + d[...].astype(F32)
    even = (me[2] & 1) == 0
    for i in range(NZ // 2):
        at = 2 * i * ROWS
        first = padded(total[at : at + ROWS]).astype(BF)
        second = padded(total[at + ROWS : at + 2 * ROWS]).astype(BF)
        keep[i] = jnp.where(even, first, second)
        send[i] = jnp.where(even, second, first)


def quarter_kernel(me, keep, got, o0, o1, o2, o3):
    for k, out in enumerate((o0, o1, o2, o3)):
        at = ((me[2] >> 1) + k) & 3
        out[...] = (keep[at].astype(F32) + got[at].astype(F32)).astype(BF)


def last_kernel(me, spatial, mark, *refs, scale):
    temporal, (keep, send) = refs[:4], refs[4:]
    first = me[3] == 0
    other = temporal[0][...].astype(F32)
    for part in temporal[1:]:
        other = other + part[...].astype(F32)
    part = ROWS // 2
    packed = total_of(spatial) * scale
    last = packed[4 * ROWS : 4 * ROWS + part]
    uppers = [packed[n * ROWS : n * ROWS + part] for n in range(4)] + [last]
    turned = jnp.concatenate([last[:, 64:], last[:, :64]], axis=1)
    lowers = [packed[n * ROWS + part : (n + 1) * ROWS] for n in range(4)] + [turned]
    other = other * scale
    for at, upper, lower in (
        (0, jnp.concatenate(uppers, axis=1), jnp.concatenate(lowers, axis=1)),
        (HALF, other[:part], other[part:ROWS]),
    ):
        keep[:, at : at + HALF] = jnp.where(first, upper, lower)
        send[:, at : at + HALF] = jnp.where(first, lower, upper)


def order_kernel(me, mine, other, out_ref):
    first = me[3] == 0
    for layer in range(2):
        a = mine[:, layer * HALF : (layer + 1) * HALF]
        b = other[:, layer * HALF : (layer + 1) * HALF]
        for n, part in enumerate((jnp.where(first, a, b), jnp.where(first, b, a))):
            for m in range(2):
                out_ref[:, layer, 2 * n + m] = part[:, m * OWN : (m + 1) * OWN]


def spread_kernel(me, a, b, c, d, own, keep, send):
    total = a[...].astype(F32) + b[...].astype(F32) + c[...].astype(F32) + d[...].astype(F32)
    hidden = (pages(own).astype(F32) + total).astype(BF)
    rows, tokens = CHIPS * 8, SLOTS * PAGE
    row, col = iota((rows, tokens), 0), iota((rows, tokens), 1)
    part, chip = row & 7, row >> 3
    base = (part >> 1) * PAGE + 4 * chip + (part & 1)
    for out, core in ((keep, me[3]), (send, 1 - me[3])):
        pick = jnp.logical_and(part < 6, col == base + 2 * core)
        out[...] = nt(pick.astype(BF), hidden).astype(BF)


def pick_kernel(me, arrived, index_ref, out_ref):
    rows, tokens = CHIPS * 16, 2 * PAGE
    row, col = iota((rows, tokens), 0), iota((rows, tokens), 1)
    part, chip, rel = row & 7, row >> 4, (row >> 3) & 1
    core = jnp.where(rel == 0, me[3], 1 - me[3])
    slot = (2 * chip + core) * SLOTS + (part >> 1)
    pick = jnp.logical_and(part < 6, (part & 1) == (col >> 7))
    pick = jnp.logical_and(pick, slot == index_ref[0:1])
    out_ref[...] = tn(arrived[...], pick.astype(BF)).astype(BF)


def scatter_kernel(me, a, b, c, d, own, index_ref, keep, send):
    total = a[...].astype(F32) + b[...].astype(F32) + c[...].astype(F32) + d[...].astype(F32)
    grad = (pages(own).astype(F32) + total).astype(BF)
    rows, tokens = CHIPS * 8, 2 * PAGE
    row, col = iota((rows, tokens), 0), iota((rows, tokens), 1)
    part, chip = row & 7, row >> 3
    live = jnp.logical_and(part < 6, (part & 1) == (col >> 7))
    for out, core in ((keep, me[3]), (send, 1 - me[3])):
        slot = (2 * chip + core) * SLOTS + (part >> 1)
        pick = jnp.logical_and(live, slot == index_ref[0:1])
        out[...] = nt(pick.astype(BF), grad).astype(BF)


def collect_kernel(me, arrived, out_ref):
    rows, tokens = CHIPS * 16, SLOTS * PAGE
    row, col = iota((rows, tokens), 0), iota((rows, tokens), 1)
    part, chip, rel = row & 7, row >> 4, (row >> 3) & 1
    core = jnp.where(rel == 0, me[3], 1 - me[3])
    position = 4 * chip + 2 * core + (part & 1)
    pick = jnp.logical_and(part < 6, col == (part >> 1) * PAGE + position)
    out_ref[...] = tn(arrived[...], pick.astype(BF)).astype(BF)


def finish_kernel(a, b, c, d, own, out_ref):
    total = a[...].astype(F32) + b[...].astype(F32) + c[...].astype(F32) + d[...].astype(F32)
    grad = (own[...].astype(F32) + total).astype(BF)
    for n in range(SLOTS):
        out_ref[n] = grad[:, n * PAGE : (n + 1) * PAGE]


def shift(value, axis, size, by):
    return lax.ppermute(value, axis, [(i, (i + by) % size) for i in range(size)])


def gathered(value):
    return (value,) + tuple(shift(value, "x", TP, k) for k in range(1, TP))


def exchanged(parts):
    return (parts[0],) + tuple(shift(parts[k], "x", TP, k) for k in range(1, TP))


def over_chips(keep, got):
    rows = call(join_kernel, (keep, got), [half(CHIPS, 16, OWN)], smem=0)[0]
    arrived = lax.all_to_all(rows, ("z", "y"), 0, 0)
    return arrived.reshape(CHIPS * 16, OWN)


def paired(me, keep, got):
    return call(pair_kernel, (me, keep, got), [half(NZ * ROWS, HALF)] * NY)


def over_column(cols):
    return [cols[0]] + [shift(cols[k], "y", NY, k) for k in range(1, NY)]


def over_rows(total):
    return lax.all_to_all(total, "z", 0, 0)


def finish_weights(me, spatial, temporal, mark, scale):
    out = [full(ROWS // 2, 2 * HALF)] * 2
    mine, other = call(functools.partial(last_kernel, scale=scale), (me, spatial, mark, *temporal), out)
    other = shift(other, "c", NC, 1)
    return call(order_kernel, (me, mine, other), [full(ROWS // 2, 2, 4, OWN)])[0]


def per_device(frames, frame_counts, weights, grad_out):
    me = Place()
    scale = 1.0 / math.sqrt(grad_out.shape[0] * PAGE)
    tokens, t_tokens = SLOTS * PAGE, 2 * PAGE
    own = jnp.transpose(frames, (0, 2, 1))
    up_own = jnp.transpose(grad_out, (1, 2, 0))
    turned = jnp.swapaxes(weights, 2, 3)
    held = lambda n: pltpu.VMEM((TP, OWN, n), BF)
    room = lambda n: [pltpu.VMEM((D, n), F32), pltpu.VMEM((D, n), F32)]
    lines = [half(D, HALF)] * 2
    big = 2 * tokens * D * 4 * OWN

    chunks = gathered(own)
    places = jax.ShapeDtypeStruct((8, t_tokens), jnp.int32)
    own, up_own, index = call(
        stage_kernel, (frame_counts, own, up_own, turned), [half(*own.shape), half(*up_own.shape), places]
    )
    *parts, x, mix = call(
        spatial_kernel,
        (me, own, *chunks[1:], turned),
        [half(OWN, tokens)] * TP + [half(D, tokens), half(OWN, tokens)],
        [held(tokens), held(tokens)],
        flops=big,
    )
    parts = exchanged(parts)
    keep, send = call(spread_kernel, (me, *parts, own), [half(CHIPS * 8, OWN)] * 2)
    keep, up_own = lax.optimization_barrier((keep, up_own))
    ups = gathered(up_own)
    arrived = over_chips(keep, shift(send, "c", NC, 1))
    rows = call(pick_kernel, (me, arrived, index), [half(OWN, t_tokens)])[0]
    hidden = gathered(rows)
    up, grad_mix = call(
        upstream_kernel,
        (me, *ups, turned),
        [half(D, t_tokens), full(OWN, t_tokens)],
        [held(t_tokens)],
        flops=big // 4,
    )
    *parts, normed, grads = call(
        temporal_kernel,
        (me, *hidden, grad_mix, turned),
        [half(OWN, t_tokens)] * TP + [half(D, t_tokens)] * 2,
        [held(t_tokens), held(t_tokens)],
        flops=big,
    )
    parts = exchanged(parts)
    t_keep, t_send = call(weight_kernel, (me, normed, up, grads), lines, room(t_tokens), flops=big)
    parts, t_keep, t_send = lax.optimization_barrier((parts, t_keep, t_send))
    keep, send = call(scatter_kernel, (me, *parts, up_own, index), [half(CHIPS * 8, OWN)] * 2)
    got, t_send = lax.optimization_barrier((shift(send, "c", NC, 1), t_send))
    t_cols = over_column(paired(me, t_keep, shift(t_send, "c", NC, 1)))
    arrived = over_chips(keep, got)
    grad_hidden = call(collect_kernel, (me, arrived), [half(OWN, tokens)])[0]
    ups = gathered(grad_hidden)
    qkv, rows, probs = call(
        ready_kernel,
        (x, turned),
        [full(3 * OWN, tokens), half(D, tokens), full(HEADS * tokens, PAGE)],
        room(tokens),
        smem=0,
        flops=big,
    )
    mark = call(mark_kernel, t_cols, [half(16, PAGE)], smem=0, place=pl.ANY)[0]
    ups, mark, rows = lax.optimization_barrier((ups, mark, rows))
    keep, send, grads = call(
        spatial_back_kernel,
        (me, *ups, qkv, probs, mix, rows, turned),
        lines + [half(3 * OWN, tokens)],
        [held(tokens), *room(tokens)],
        flops=big,
    )
    got = shift(send, "c", NC, 1)
    parts = call(
        spatial_input_kernel,
        (me, x, grads, turned),
        [half(OWN, tokens)] * TP,
        [held(tokens)],
        flops=big,
    )
    got, parts = lax.optimization_barrier((got, parts))
    sums = call(sum_kernel, (keep, got), [half(D, HALF)], smem=0)[0]
    t_cols, sums = lax.optimization_barrier((t_cols, sums))
    t_parts = [half(NZ // 2, PAD, HALF)] * 2
    t_keep, t_send = call(parity_kernel, (me, *t_cols), t_parts)
    t_keep, parts = lax.optimization_barrier((t_keep, parts))
    t_got = lax.ppermute(t_send, "z", [(z, z ^ 1) for z in range(NZ)])
    t_parts = call(quarter_kernel, (me, t_keep, t_got), [half(PAD, HALF)] * 4)
    t_parts = [t_parts[0]] + [shift(t_parts[k], "z", NZ, 2 * k) for k in range(1, 4)]
    cols = lax.all_to_all(sums.reshape(NY, NZ * ROWS, HALF), "y", 0, 0)
    parts = exchanged(parts)
    cols, t_parts, parts = lax.optimization_barrier((cols, t_parts, parts))
    column = call(column_kernel, (cols,), [half(NZ, PACK, PAGE)], [pltpu.VMEM((NZ, PACK, PAGE), F32)], smem=0)[0]
    moved = over_rows(column)
    frame_grads = call(finish_kernel, (*parts, grad_hidden), [half(SLOTS, OWN, PAGE)], smem=0)[0]
    moved, frame_grads = lax.optimization_barrier((moved, frame_grads))
    weight_grads = finish_weights(me, moved, t_parts, mark, scale)
    return jnp.transpose(frame_grads, (0, 2, 1)), weight_grads


def solution(mesh):
    fine = Mesh(mesh.devices.reshape(NZ, NY, NC, TP), ("z", "y", "c", "x"))
    seq = ("z", "y", "c")
    return jax.shard_map(
        per_device,
        mesh=fine,
        in_specs=(P(seq, None, "x"), P(), P(None, None, None, "x"), P(None, seq, "x")),
        out_specs=(P(seq, None, "x"), P(seq, None, None, "x")),
        check_vma=False,
    )
```

```python
import functools
import math

import jax
import jax.numpy as jnp
from jax import lax
from jax.experimental import pallas as pl
from jax.experimental.pallas import tpu as pltpu
from jax.sharding import Mesh
from jax.sharding import PartitionSpec as P

HD = 72
TF = 16
HEADS = 4
OWN = HEADS * HD
TP = 4
D = OWN * TP
PAGE = 128
SLOTS = 3
NZ, NY, NC = 8, 4, 2
CHIPS = NZ * NY
ROWS = 36
PAD = 40
HALF = 640
PACK = 168
EPS = 1e-06
SCALE = HD**-0.5
F32 = jnp.float32
BF = jnp.bfloat16


def nn(a, b):
    return lax.dot_general(a, b, (((1,), (0,)), ((), ())), preferred_element_type=F32)


def nt(a, b):
    return lax.dot_general(a, b, (((1,), (1,)), ((), ())), preferred_element_type=F32)


def tn(a, b):
    return lax.dot_general(a, b, (((0,), (0,)), ((), ())), preferred_element_type=F32)


def iota(shape, dim):
    return lax.broadcasted_iota(jnp.int32, shape, dim)


class Place:
    def __getitem__(self, at):
        return lax.axis_index("xyzc"[at])


def call(body, ins, outs, scratch=(), smem=1, flops=1_000_000, limit=16, place=pltpu.VMEM):
    if isinstance(ins[0], Place):
        body, ins, smem = functools.partial(body, ins[0]), ins[1:], 0
    in_specs = [
        pl.BlockSpec(memory_space=pltpu.SMEM) if i < smem else pl.BlockSpec(memory_space=place)
        for i in range(len(ins))
    ]
    size = sum(math.prod(o.shape) * o.dtype.itemsize for o in outs)
    size += sum(math.prod(i.shape) * i.dtype.itemsize for i in ins)
    out_specs = [pl.BlockSpec(memory_space=pltpu.VMEM) for _ in outs]
    return pl.pallas_call(
        body,
        out_shape=list(outs),
        in_specs=in_specs,
        out_specs=out_specs,
        scratch_shapes=list(scratch),
        compiler_params=pltpu.CompilerParams(vmem_limit_bytes=limit * 2**20),
        cost_estimate=pl.CostEstimate(flops=flops, bytes_accessed=size, transcendentals=0),
    )(*ins)


def half(*shape):
    return jax.ShapeDtypeStruct(shape, BF)


def full(*shape):
    return jax.ShapeDtypeStruct(shape, F32)


def normalise(x):
    center = x - jnp.sum(x, axis=0, keepdims=True) * (1.0 / D)
    inverse = lax.rsqrt(jnp.sum(center * center, axis=0, keepdims=True) * (1.0 / D) + EPS)
    return center * inverse, inverse


def normalise_back(normed, inverse, up):
    mean = jnp.sum(up, axis=0, keepdims=True) * (1.0 / D)
    along = jnp.sum(up * normed, axis=0, keepdims=True) * (1.0 / D)
    return inverse * (up - mean - normed * along)


def unit(rows):
    inverse = lax.rsqrt(jnp.sum(rows * rows, axis=0, keepdims=True) * (1.0 / HD) + EPS)
    return inverse, (rows * inverse).astype(BF)


def unit_back(rows, inverse, up):
    along = jnp.sum(up * rows, axis=0, keepdims=True) * (1.0 / HD)
    return inverse * up - rows * (inverse * inverse * inverse * along)


def head_parts(qkv, h):
    q = qkv[h * HD : (h + 1) * HD]
    k = qkv[OWN + h * HD : OWN + (h + 1) * HD]
    v = qkv[2 * OWN + h * HD : 2 * OWN + (h + 1) * HD]
    q_inv, q_unit = unit(q)
    k_inv, k_unit = unit(k)
    return q, k, q_inv, q_unit, k_inv, k_unit, v.astype(BF)


def weights_of(k_unit, q_unit, mask):
    raised = jnp.exp(tn(k_unit, q_unit) * SCALE)
    if mask is not None:
        raised = jnp.where(mask, raised, 0.0)
    return raised * (1.0 / jnp.sum(raised, axis=0, keepdims=True))


def mixture_of(qkv, tokens, mask):
    heads = []
    for h in range(HEADS):
        _, _, _, q_unit, _, k_unit, v = head_parts(qkv, h)
        blocks = []
        for b in range(tokens // PAGE):
            at = slice(b * PAGE, (b + 1) * PAGE)
            probs = weights_of(k_unit[:, at], q_unit[:, at], mask)
            blocks.append(nn(v[:, at], probs.astype(BF)))
        heads.append(jnp.concatenate(blocks, axis=1))
    return jnp.concatenate(heads, axis=0).astype(BF)


def attend_back(qkv, grad_mix, tokens, mask, given=None):
    queries, keys, values, mixes = [], [], [], []
    for h in range(HEADS):
        q, k, q_inv, q_unit, k_inv, k_unit, v = head_parts(qkv, h)
        gm = grad_mix[h * HD : (h + 1) * HD].astype(BF)
        with_mixture = given is None
        q_slope, k_slope, v_grad, mix = [], [], [], []
        for b in range(tokens // PAGE):
            at = slice(b * PAGE, (b + 1) * PAGE)
            if with_mixture:
                probs = weights_of(k_unit[:, at], q_unit[:, at], mask)
            else:
                unit_at = (h * (tokens // PAGE) + b) * PAGE
                probs = given[unit_at : unit_at + PAGE]
            probs_half = probs.astype(BF)
            if with_mixture:
                mix.append(nn(v[:, at], probs_half))
            grad_probs = tn(v[:, at], gm[:, at])
            v_grad.append(nt(gm[:, at], probs_half))
            weighted = probs * grad_probs
            grad_scores = (weighted - probs * jnp.sum(weighted, axis=0, keepdims=True)).astype(BF)
            q_slope.append(nn(k_unit[:, at], grad_scores) * SCALE)
            k_slope.append(nt(q_unit[:, at], grad_scores) * SCALE)
        queries.append(unit_back(q, q_inv, jnp.concatenate(q_slope, axis=1)))
        keys.append(unit_back(k, k_inv, jnp.concatenate(k_slope, axis=1)))
        values.append(jnp.concatenate(v_grad, axis=1))
        if with_mixture:
            mixes.append(jnp.concatenate(mix, axis=1))
    join = lambda parts: jnp.concatenate(parts, axis=0).astype(BF)
    return join(queries), join(keys), join(values), join(mixes) if given is None else None


def rows_of(w_ref, layer):
    return w_ref[layer, :3].reshape(3 * OWN, D)


def assemble(own, chunks, held):
    for k, chunk in enumerate(chunks):
        at = (own + TP - k) & (TP - 1)
        if len(chunk.shape) == 3:
            for n in range(chunk.shape[0]):
                held[at, :, n * PAGE : (n + 1) * PAGE] = chunk[n]
        else:
            held[at] = chunk[...]
    return held[...].reshape(D, held.shape[2])


def deal(own, value, held, outs):
    held[...] = value.astype(BF).reshape(held.shape)
    for k, out in enumerate(outs):
        out[...] = held[(own + k) & (TP - 1)]


def pages(ref):
    return jnp.concatenate([ref[n] for n in range(ref.shape[0])], axis=1)


def stage_kernel(counts, a_ref, b_ref, w_ref, a_out, b_out, index_out):
    a_out[...] = a_ref[...]
    b_out[...] = b_ref[...]
    frame = iota(index_out.shape, 1) & (PAGE - 1)
    index = jnp.zeros(index_out.shape, jnp.int32)
    start = jnp.int32(0)
    for s in range(counts.shape[0]):
        index = jnp.where(frame >= start, frame + (s * SLOTS - start), index)
        start = start + counts[s]
    index_out[...] = index


def join_kernel(a_ref, b_ref, out_ref):
    parts = [ref[...].astype(F32).reshape(CHIPS, 8, OWN) for ref in (a_ref, b_ref)]
    out_ref[...] = jnp.concatenate(parts, axis=1).astype(BF)


def spatial_kernel(me, c0, c1, c2, c3, w_ref, p0, p1, p2, p3, x_out, mix_out, held, dealt):
    x = assemble(me[0], (c0, c1, c2, c3), held)
    x_out[...] = x
    normed, _ = normalise(x.astype(F32))
    qkv = nn(rows_of(w_ref, 0), normed.astype(BF))
    mix = mixture_of(qkv, x.shape[1], None)
    mix_out[...] = mix
    deal(me[0], tn(w_ref[0, 3], mix), dealt, (p0, p1, p2, p3))


def upstream_kernel(me, g0, g1, g2, g3, w_ref, up_out, mix_out, held):
    up = assemble(me[0], (g0, g1, g2, g3), held)
    up_out[...] = up
    mix_out[...] = nn(w_ref[1, 3], up).astype(BF).astype(F32)


def temporal_kernel(
    me, h0, h1, h2, h3, grad_mix, w_ref, p0, p1, p2, p3, normed_out, grads_out, held, dealt
):
    x = assemble(me[0], (h0, h1, h2, h3), held)
    normed, inverse = normalise(x.astype(F32))
    normed_half = normed.astype(BF)
    normed_out[...] = normed_half
    qkv = nn(rows_of(w_ref, 1), normed_half)
    mask = (iota((PAGE, PAGE), 0) >> 4) == (iota((PAGE, PAGE), 1) >> 4)
    gq, gk, gv, mix = attend_back(qkv, grad_mix, x.shape[1], mask)
    for m, part in enumerate((gq, gk, gv, mix)):
        grads_out[m * OWN : (m + 1) * OWN] = part
    grad_normed = tn(rows_of(w_ref, 1), jnp.concatenate([gq, gk, gv], axis=0))
    deal(me[0], normalise_back(normed, inverse, grad_normed), dealt, (p0, p1, p2, p3))


def ready_kernel(x_ref, w_ref, qkv_out, lines_out, probs_out, wide, held):
    normed, _ = normalise(x_ref[...].astype(F32))
    normed = normed.astype(BF)
    wide[...] = normed.astype(F32)
    lines_out[...] = regroup(wide, held)
    qkv = nn(rows_of(w_ref, 0), normed)
    qkv_out[...] = qkv
    tokens = x_ref.shape[1]
    for h in range(HEADS):
        _, _, _, q_unit, _, k_unit, _ = head_parts(qkv, h)
        for b in range(tokens // PAGE):
            at = slice(b * PAGE, (b + 1) * PAGE)
            unit_at = (h * (tokens // PAGE) + b) * PAGE
            probs_out[unit_at : unit_at + PAGE] = weights_of(k_unit[:, at], q_unit[:, at], None)


def spatial_back_kernel(
    me, g0, g1, g2, g3, qkv_ref, probs_ref, mix_ref, lines_ref, w_ref,
    keep, send, grads_out, held_g, wide, held,
):
    up = assemble(me[0], (g0, g1, g2, g3), held_g)
    wide[...] = up.astype(F32)
    grad_mix = nn(w_ref[0, 3], up)
    gq, gk, gv, _ = attend_back(qkv_ref, grad_mix, up.shape[1], None, probs_ref)
    grads = jnp.concatenate([gq, gk, gv], axis=0)
    grads_out[...] = grads
    weight_products(me[3], lines_ref[...], regroup(wide, held), grads, mix_ref[...], keep, send)


def spatial_input_kernel(me, x_ref, grads, w_ref, p0, p1, p2, p3, dealt):
    normed, inverse = normalise(x_ref[...].astype(F32))
    grad_normed = tn(rows_of(w_ref, 0), grads[...])
    deal(me[0], normalise_back(normed, inverse, grad_normed), dealt, (p0, p1, p2, p3))


def regroup(ref, held):
    for y in range(NY):
        for z in range(NZ):
            at = (y * NZ + z) * ROWS
            held[at : at + ROWS] = ref[z * NY * ROWS + y * ROWS : z * NY * ROWS + (y + 1) * ROWS]
    return held[...].astype(BF)


def weight_products(core, lines, up_lines, grads, mix, keep, send):
    zeros = lambda n: jnp.zeros((n, mix.shape[1]), BF)
    first = nt(lines, jnp.concatenate([grads[: 2 * OWN], zeros(HALF - 2 * OWN)], axis=0)).astype(BF)
    low = nt(lines, jnp.concatenate([grads[2 * OWN :], zeros(96)], axis=0))
    low = low + nt(up_lines, jnp.concatenate([zeros(OWN), mix[:96]], axis=0))
    high = nt(up_lines, jnp.concatenate([mix[96:], zeros(64)], axis=0))

    @pl.when(core == 0)
    def _():
        keep[...] = first
        send[:, :384] = low.astype(BF)
        send[:, 384:] = high.astype(BF)

    @pl.when(core == 1)
    def _():
        send[...] = first
        keep[:, :384] = low.astype(BF)
        keep[:, 384:] = high.astype(BF)


def weight_kernel(me, normed_ref, up_ref, grads_ref, keep, send, wide, held):
    wide[...] = normed_ref[...].astype(F32)
    lines = regroup(wide, held)
    wide[...] = up_ref[...].astype(F32)
    up_lines = regroup(wide, held)
    weight_products(me[3], lines, up_lines, grads_ref[: 3 * OWN], grads_ref[3 * OWN :], keep, send)


def total_of(ref):
    total = ref[0].astype(F32)
    for n in range(1, ref.shape[0]):
        total = total + ref[n].astype(F32)
    return total


def pair_kernel(me, keep, got, *outs):
    span = NZ * ROWS
    for k, out in enumerate(outs):
        rows = pl.ds(pl.multiple_of(((me[1] + k) & (NY - 1)) * span, 16), span)
        out[...] = (keep[rows].astype(F32) + got[rows].astype(F32)).astype(BF)


def sum_kernel(keep, got, out):
    out[...] = (keep[...].astype(F32) + got[...].astype(F32)).astype(BF)


def padded(lines):
    return jnp.concatenate([lines, jnp.zeros((PAD - ROWS, HALF), F32)], axis=0)


def pack(total, held):
    part = ROWS // 2
    for z in range(NZ):
        lines = total[z * ROWS : (z + 1) * ROWS]
        for n in range(4):
            held[z, n * ROWS : (n + 1) * ROWS] = lines[:, n * PAGE : (n + 1) * PAGE]
        rest = lines[:, 4 * PAGE : 2 * OWN]
        held[z, 4 * ROWS : 4 * ROWS + part] = jnp.concatenate([rest[:part], rest[part:]], axis=1)
        held[z, 4 * ROWS + part :] = jnp.zeros((PACK - 4 * ROWS - part, PAGE), F32)


def unpack(packed):
    part = ROWS // 2
    last = packed[4 * ROWS : 4 * ROWS + part]
    uppers = [packed[n * ROWS : n * ROWS + part] for n in range(4)] + [last]
    turned = jnp.concatenate([last[:, 64:], last[:, :64]], axis=1)
    lowers = [packed[n * ROWS + part : (n + 1) * ROWS] for n in range(4)] + [turned]
    return jnp.concatenate(uppers, axis=1), jnp.concatenate(lowers, axis=1)


def column_kernel(parts, out, held):
    pack(total_of(parts), held)
    out[...] = held[...].astype(BF)


def mark_kernel(a, b, c, d, out):
    out[...] = jnp.zeros((16, PAGE), BF)


def parity_kernel(me, a, b, c, d, keep, send, held):
    pack(a[...].astype(F32) + b[...].astype(F32) + c[...].astype(F32) + d[...].astype(F32), held)
    even = (me[2] & 1) == 0
    for i in range(NZ // 2):
        first, second = held[2 * i].astype(BF), held[2 * i + 1].astype(BF)
        keep[i] = jnp.where(even, first, second)
        send[i] = jnp.where(even, second, first)


def quarter_kernel(me, keep, got, o0, o1, o2, o3):
    for k, out in enumerate((o0, o1, o2, o3)):
        at = ((me[2] >> 1) + k) & 3
        out[...] = (keep[at].astype(F32) + got[at].astype(F32)).astype(BF)


def last_kernel(me, spatial, mark, *refs, scale):
    temporal, (keep, send) = refs[:4], refs[4:]
    first = me[3] == 0
    other = temporal[0][...].astype(F32)
    for part in temporal[1:]:
        other = other + part[...].astype(F32)
    for at, total in ((0, total_of(spatial)), (HALF, other)):
        upper, lower = unpack(total * scale)
        keep[:, at : at + HALF] = jnp.where(first, upper, lower)
        send[:, at : at + HALF] = jnp.where(first, lower, upper)


def order_kernel(me, mine, other, out_ref):
    first = me[3] == 0
    for layer in range(2):
        a = mine[:, layer * HALF : (layer + 1) * HALF]
        b = other[:, layer * HALF : (layer + 1) * HALF]
        for n, part in enumerate((jnp.where(first, a, b), jnp.where(first, b, a))):
            for m in range(2):
                out_ref[:, layer, 2 * n + m] = part[:, m * OWN : (m + 1) * OWN]


def spread_kernel(me, a, b, c, d, own, keep, send):
    total = a[...].astype(F32) + b[...].astype(F32) + c[...].astype(F32) + d[...].astype(F32)
    hidden = (pages(own).astype(F32) + total).astype(BF)
    rows, tokens = CHIPS * 8, SLOTS * PAGE
    row, col = iota((rows, tokens), 0), iota((rows, tokens), 1)
    part, chip = row & 7, row >> 3
    base = (part >> 1) * PAGE + 4 * chip + (part & 1)
    for out, core in ((keep, me[3]), (send, 1 - me[3])):
        pick = jnp.logical_and(part < 6, col == base + 2 * core)
        out[...] = nt(pick.astype(BF), hidden).astype(BF)


def pick_kernel(me, arrived, index_ref, out_ref):
    rows, tokens = CHIPS * 16, 2 * PAGE
    row, col = iota((rows, tokens), 0), iota((rows, tokens), 1)
    part, chip, rel = row & 7, row >> 4, (row >> 3) & 1
    core = jnp.where(rel == 0, me[3], 1 - me[3])
    slot = (2 * chip + core) * SLOTS + (part >> 1)
    pick = jnp.logical_and(part < 6, (part & 1) == (col >> 7))
    pick = jnp.logical_and(pick, slot == index_ref[0:1])
    out_ref[...] = tn(arrived[...], pick.astype(BF)).astype(BF)


def scatter_kernel(me, a, b, c, d, own, index_ref, keep, send):
    total = a[...].astype(F32) + b[...].astype(F32) + c[...].astype(F32) + d[...].astype(F32)
    grad = (pages(own).astype(F32) + total).astype(BF)
    rows, tokens = CHIPS * 8, 2 * PAGE
    row, col = iota((rows, tokens), 0), iota((rows, tokens), 1)
    part, chip = row & 7, row >> 3
    live = jnp.logical_and(part < 6, (part & 1) == (col >> 7))
    for out, core in ((keep, me[3]), (send, 1 - me[3])):
        slot = (2 * chip + core) * SLOTS + (part >> 1)
        pick = jnp.logical_and(live, slot == index_ref[0:1])
        out[...] = nt(pick.astype(BF), grad).astype(BF)


def collect_kernel(me, arrived, out_ref):
    rows, tokens = CHIPS * 16, SLOTS * PAGE
    row, col = iota((rows, tokens), 0), iota((rows, tokens), 1)
    part, chip, rel = row & 7, row >> 4, (row >> 3) & 1
    core = jnp.where(rel == 0, me[3], 1 - me[3])
    position = 4 * chip + 2 * core + (part & 1)
    pick = jnp.logical_and(part < 6, col == (part >> 1) * PAGE + position)
    out_ref[...] = tn(arrived[...], pick.astype(BF)).astype(BF)


def finish_kernel(a, b, c, d, own, out_ref):
    total = a[...].astype(F32) + b[...].astype(F32) + c[...].astype(F32) + d[...].astype(F32)
    grad = (own[...].astype(F32) + total).astype(BF)
    for n in range(SLOTS):
        out_ref[n] = grad[:, n * PAGE : (n + 1) * PAGE]


def shift(value, axis, size, by):
    return lax.ppermute(value, axis, [(i, (i + by) % size) for i in range(size)])


def gathered(value):
    return (value,) + tuple(shift(value, "x", TP, k) for k in range(1, TP))


def exchanged(parts):
    return (parts[0],) + tuple(shift(parts[k], "x", TP, k) for k in range(1, TP))


def over_chips(keep, got):
    rows = call(join_kernel, (keep, got), [half(CHIPS, 16, OWN)], smem=0)[0]
    arrived = lax.all_to_all(rows, ("z", "y"), 0, 0)
    return arrived.reshape(CHIPS * 16, OWN)


def paired(me, keep, got):
    return call(pair_kernel, (me, keep, got), [half(NZ * ROWS, HALF)] * NY)


def over_column(cols):
    return [cols[0]] + [shift(cols[k], "y", NY, k) for k in range(1, NY)]


def over_rows(total):
    return lax.all_to_all(total, "z", 0, 0)


def finish_weights(me, spatial, temporal, mark, scale):
    out = [full(ROWS // 2, 2 * HALF)] * 2
    mine, other = call(functools.partial(last_kernel, scale=scale), (me, spatial, mark, *temporal), out)
    other = shift(other, "c", NC, 1)
    return call(order_kernel, (me, mine, other), [full(ROWS // 2, 2, 4, OWN)])[0]


def per_device(frames, frame_counts, weights, grad_out):
    me = Place()
    scale = 1.0 / math.sqrt(grad_out.shape[0] * PAGE)
    tokens, t_tokens = SLOTS * PAGE, 2 * PAGE
    own = jnp.transpose(frames, (0, 2, 1))
    up_own = jnp.transpose(grad_out, (1, 2, 0))
    turned = jnp.swapaxes(weights, 2, 3)
    held = lambda n: pltpu.VMEM((TP, OWN, n), BF)
    room = lambda n: [pltpu.VMEM((D, n), F32), pltpu.VMEM((D, n), F32)]
    lines = [half(D, HALF)] * 2
    big = 2 * tokens * D * 4 * OWN

    chunks = gathered(own)
    places = jax.ShapeDtypeStruct((8, t_tokens), jnp.int32)
    own, up_own, index = call(
        stage_kernel, (frame_counts, own, up_own, turned), [half(*own.shape), half(*up_own.shape), places]
    )
    *parts, x, mix = call(
        spatial_kernel,
        (me, own, *chunks[1:], turned),
        [half(OWN, tokens)] * TP + [half(D, tokens), half(OWN, tokens)],
        [held(tokens), held(tokens)],
        flops=big,
    )
    parts = exchanged(parts)
    keep, send = call(spread_kernel, (me, *parts, own), [half(CHIPS * 8, OWN)] * 2)
    keep, up_own = lax.optimization_barrier((keep, up_own))
    ups = gathered(up_own)
    arrived = over_chips(keep, shift(send, "c", NC, 1))
    rows = call(pick_kernel, (me, arrived, index), [half(OWN, t_tokens)])[0]
    hidden = gathered(rows)
    up, grad_mix = call(
        upstream_kernel,
        (me, *ups, turned),
        [half(D, t_tokens), full(OWN, t_tokens)],
        [held(t_tokens)],
        flops=big // 4,
    )
    *parts, normed, grads = call(
        temporal_kernel,
        (me, *hidden, grad_mix, turned),
        [half(OWN, t_tokens)] * TP + [half(D, t_tokens)] * 2,
        [held(t_tokens), held(t_tokens)],
        flops=big,
    )
    parts = exchanged(parts)
    t_keep, t_send = call(weight_kernel, (me, normed, up, grads), lines, room(t_tokens), flops=big)
    parts, t_keep, t_send = lax.optimization_barrier((parts, t_keep, t_send))
    keep, send = call(scatter_kernel, (me, *parts, up_own, index), [half(CHIPS * 8, OWN)] * 2)
    got, t_send = lax.optimization_barrier((shift(send, "c", NC, 1), t_send))
    t_cols = over_column(paired(me, t_keep, shift(t_send, "c", NC, 1)))
    arrived = over_chips(keep, got)
    grad_hidden = call(collect_kernel, (me, arrived), [half(OWN, tokens)])[0]
    ups = gathered(grad_hidden)
    qkv, rows, probs = call(
        ready_kernel,
        (x, turned),
        [full(3 * OWN, tokens), half(D, tokens), full(HEADS * tokens, PAGE)],
        room(tokens),
        smem=0,
        flops=big,
    )
    mark = call(mark_kernel, t_cols, [half(16, PAGE)], smem=0, place=pl.ANY)[0]
    ups, mark, rows = lax.optimization_barrier((ups, mark, rows))
    keep, send, grads = call(
        spatial_back_kernel,
        (me, *ups, qkv, probs, mix, rows, turned),
        lines + [half(3 * OWN, tokens)],
        [held(tokens), *room(tokens)],
        flops=big,
    )
    got = shift(send, "c", NC, 1)
    parts = call(
        spatial_input_kernel,
        (me, x, grads, turned),
        [half(OWN, tokens)] * TP,
        [held(tokens)],
        flops=big,
    )
    got, parts = lax.optimization_barrier((got, parts))
    sums = call(sum_kernel, (keep, got), [half(D, HALF)], smem=0)[0]
    t_cols, sums = lax.optimization_barrier((t_cols, sums))
    t_parts = [half(NZ // 2, PACK, PAGE)] * 2
    room_z = [pltpu.VMEM((NZ, PACK, PAGE), F32)]
    t_keep, t_send = call(parity_kernel, (me, *t_cols), t_parts, room_z)
    t_keep, parts = lax.optimization_barrier((t_keep, parts))
    t_got = lax.ppermute(t_send, "z", [(z, z ^ 1) for z in range(NZ)])
    t_parts = call(quarter_kernel, (me, t_keep, t_got), [half(PACK, PAGE)] * 4)
    t_parts = [t_parts[0]] + [shift(t_parts[k], "z", NZ, 2 * k) for k in range(1, 4)]
    cols = lax.all_to_all(sums.reshape(NY, NZ * ROWS, HALF), "y", 0, 0)
    parts = exchanged(parts)
    cols, t_parts, parts = lax.optimization_barrier((cols, t_parts, parts))
    column = call(column_kernel, (cols,), [half(NZ, PACK, PAGE)], [pltpu.VMEM((NZ, PACK, PAGE), F32)], smem=0)[0]
    moved = over_rows(column)
    frame_grads = call(finish_kernel, (*parts, grad_hidden), [half(SLOTS, OWN, PAGE)], smem=0)[0]
    moved, frame_grads = lax.optimization_barrier((moved, frame_grads))
    weight_grads = finish_weights(me, moved, t_parts, mark, scale)
    return jnp.transpose(frame_grads, (0, 2, 1)), weight_grads


def solution(mesh):
    fine = Mesh(mesh.devices.reshape(NZ, NY, NC, TP), ("z", "y", "c", "x"))
    seq = ("z", "y", "c")
    return jax.shard_map(
        per_device,
        mesh=fine,
        in_specs=(P(seq, None, "x"), P(), P(None, None, None, "x"), P(None, seq, "x")),
        out_specs=(P(seq, None, "x"), P(seq, None, None, "x")),
        check_vma=False,
    )
```
